128 devices in a mesh: group: 16 (over z, x), tp: 8 (over y, core).
Axes of the slice: x: 4, y: 4, z: 4, core: 2. Of those that a mesh axis runs over, the one named last changes fastest.
Arguments:
- attention_slot_outputs: bfloat16 [12288, 8192], P('group', 'tp'), may hold values from -6 to 6
- output_gradient_rows: bfloat16 [6144, 8192], P('group', 'tp'), may hold values from -6 to 6
- output_weight: bfloat16 [8192, 8192], P('tp'), may hold values from -0.0625 to 0.0625
- down_weight: bfloat16 [8192, 64], P('tp'), may hold values from -0.0625 to 0.0625
- up_weight: bfloat16 [64, 8192], P(None, 'tp'), may hold values from -0.0625 to 0.0625
- assign: int32 [48], replicated, may hold values from 0 to 15, as said below
- counts: int32 [16], replicated, may hold values from 0 to 6, as said below
Outputs:
- attention_input_gradient: bfloat16 [12288, 8192], P('group', 'tp')
- down_weight_gradient: float32 [8192, 64], P('tp')
- up_weight_gradient: float32 [64, 8192], P(None, 'tp')
The draws below stay inside these ranges and needn't reach their ends.
Inputs may be any that keep to these rules, and one draw needn't show every extreme that they name: `assign`: the 3 rows g * 3 to g * 3 + 2 go to 3 different groups. Some group receives 6 rows. counts[g] is at least the number of rows assigned to group g.
All inputs are finite; a program needn't handle non-finite values.
Results may differ from the reference program's by a relative error of at most 0.0034.
Values may be sent and summed in bfloat16 or wider, within the bound.
No kernel may reach another device: no remote copies, remote signals or barrier semaphores. Data moves between devices by JAX's collectives and lax.ppermute only.
A program may use at most 128 MiB of HBM per device.

```python
import math
import jax
import jax.numpy as jnp
from jax import lax

MODEL_WIDTH = 8192
ADAPTER_RANK = 64
ROW_TOKENS = 128
ROWS_DEV = 3
CAP = 6
TOKENS = 6144
SLOT_TOKENS = 12288
N_GROUP = 16


def plan_tables(key):
    first, second, third = jax.random.split(key, 3)
    sigma = jax.random.permutation(first, N_GROUP).astype(jnp.int32)
    order = jax.random.permutation(second, N_GROUP).astype(jnp.int32)
    place = jnp.zeros((N_GROUP,), jnp.int32).at[order].set(jnp.arange(N_GROUP, dtype=jnp.int32))
    lane = place[:, None]
    step = jnp.arange(ROWS_DEV, dtype=jnp.int32)[None, :]
    spread = ROWS_DEV + ((lane - CAP) * ROWS_DEV + step) % max(N_GROUP - ROWS_DEV, 1)
    ranked = jnp.where(lane < CAP, step + 0 * lane, spread)
    assign = sigma[ranked].reshape(-1).astype(jnp.int32)
    loads = jnp.sum((assign[:, None] == jnp.arange(N_GROUP, dtype=jnp.int32)[None, :]).astype(jnp.int32), axis=0)
    extra = jax.random.randint(third, (N_GROUP,), 0, 1 << 20, dtype=jnp.int32)
    counts = loads + extra % (CAP - loads + 1)
    return (assign, counts.astype(jnp.int32))


def draw_assign(key, part):
    tables = plan_tables(key)
    return tables[0]


def draw_counts(key, part):
    tables = plan_tables(key)
    return tables[1]


def block_scale(own_key, extent, cuts, low, largest):
    level = 1.0
    for dim, blocks in cuts:
        steps = jax.random.uniform(jax.random.fold_in(jax.random.fold_in(own_key, 6), dim), (blocks,), jnp.float32, low / len(cuts), largest / len(cuts))
        level = level * jnp.repeat(jnp.exp(steps), extent[dim] // blocks).reshape((-1,) + (1,) * (len(extent) - 1 - dim))
    return level


def bell_draw(key, dims, scale, bound, pieces=(), held_as=jnp.bfloat16):
    array = jax.random.normal(key, dims, jnp.float32) * scale
    if len(pieces) > 0:
        array = block_scale(key, dims, pieces, -0.22, 0.18) * array
    return jnp.clip(array, min=-bound, max=bound).astype(held_as)


def setup_inputs(seed: int = 0) -> dict:
    arg_keys = jax.random.split(jax.random.key(seed), 8)
    return {
        "attention_slot_outputs": bell_draw(arg_keys[0], (SLOT_TOKENS, MODEL_WIDTH), 1.0, 6.0, ((0, 16), (1, 8))),
        "output_gradient_rows": bell_draw(arg_keys[1], (TOKENS, MODEL_WIDTH), 1.0, 6.0, ((0, 16), (1, 8))),
        "output_weight": bell_draw(arg_keys[2], (MODEL_WIDTH, MODEL_WIDTH), MODEL_WIDTH ** -0.5, 0.0625, ((0, 8),)),
        "down_weight": bell_draw(arg_keys[3], (MODEL_WIDTH, ADAPTER_RANK), MODEL_WIDTH ** -0.5, 0.0625, ((0, 8),)),
        "up_weight": bell_draw(arg_keys[4], (ADAPTER_RANK, MODEL_WIDTH), MODEL_WIDTH ** -0.5, 0.0625, ((1, 8),)),
        "assign": draw_assign(jax.random.fold_in(arg_keys[7], 71), 0),
        "counts": draw_counts(jax.random.fold_in(arg_keys[7], 71), 0),
    }


adapter_scale = 2.0

def reference(attention_slot_outputs, output_gradient_rows, output_weight, down_weight, up_weight, assign, counts):
    groups = counts.shape[0]
    group_ids = jnp.arange(groups, dtype=jnp.int32)
    onehot = (assign[:, None] == group_ids[None, :]).astype(jnp.int32)
    before = jnp.cumsum(onehot, axis=0) - onehot
    order_in = lax.optimization_barrier(jnp.sum(before * onehot, axis=1))
    free_slots = lax.optimization_barrier(jnp.sum(onehot * counts[None, :], axis=1))
    position = assign * CAP + CAP - free_slots + order_in
    token_position = (position[:, None] * ROW_TOKENS + jnp.arange(ROW_TOKENS, dtype=jnp.int32)[None, :]).reshape(-1).astype(jnp.int32)
    lowrank_gradient = jnp.dot(output_gradient_rows, up_weight.T, preferred_element_type=jnp.float32).astype(jnp.bfloat16)
    row_ordered_input = jnp.dot(output_gradient_rows, output_weight.T, preferred_element_type=jnp.float32)
    row_ordered_input = row_ordered_input + adapter_scale * jnp.dot(lowrank_gradient, down_weight.T, preferred_element_type=jnp.float32)
    row_ordered_input = row_ordered_input.astype(jnp.bfloat16)
    attention_input_gradient = jnp.zeros((attention_slot_outputs.shape[0], attention_slot_outputs.shape[1]), jnp.bfloat16).at[token_position].set(row_ordered_input)
    projected_gradient = jnp.dot(attention_slot_outputs, down_weight, preferred_element_type=jnp.float32).astype(jnp.bfloat16)
    selected_rows = attention_slot_outputs[token_position]
    projected_row_values = projected_gradient[token_position]
    scale_factor = adapter_scale / math.sqrt(token_position.shape[0])
    down_weight_gradient = scale_factor * jnp.dot(selected_rows.T, lowrank_gradient, preferred_element_type=jnp.float32)
    up_weight_gradient = scale_factor * jnp.dot(projected_row_values.T, output_gradient_rows, preferred_element_type=jnp.float32)
    return (attention_input_gradient, down_weight_gradient, up_weight_gradient)
```

```python
import math

import jax
import jax.numpy as jnp
from jax import lax
from jax.sharding import PartitionSpec as P

ROW_TOKENS = 128


adapter_scale = 2.0


def body(
    attention_slot_outputs,
    output_gradient_rows,
    output_weight,
    down_weight,
    up_weight,
    assign,
    counts,
):
    groups = counts.shape[0]
    rows = assign.shape[0]
    rows_here = output_gradient_rows.shape[0] // ROW_TOKENS
    slot_cap = attention_slot_outputs.shape[0] // ROW_TOKENS
    width_here = output_gradient_rows.shape[1]
    rank = up_weight.shape[0]
    tp = lax.axis_size("tp")
    piece = ROW_TOKENS // groups
    own_group = lax.axis_index("group")
    group_ids = jnp.arange(groups, dtype=jnp.int32)
    onehot = (assign[:, None] == group_ids[None, :]).astype(jnp.int32)
    before = jnp.cumsum(onehot, axis=0) - onehot
    order_in = jnp.sum(before * onehot, axis=1)
    free_slots = jnp.sum(onehot * counts[None, :], axis=1)
    position = slot_cap - free_slots + order_in
    own_dest = lax.dynamic_slice_in_dim(assign, own_group * rows_here, rows_here)
    own_position = lax.dynamic_slice_in_dim(position, own_group * rows_here, rows_here)
    scale_factor = adapter_scale / math.sqrt(rows * ROW_TOKENS)

    spread = lax.all_to_all(
        output_gradient_rows.reshape(rows_here, groups, piece, width_here).transpose(1, 0, 2, 3),
        "group",
        split_axis=0,
        concat_axis=0,
        tiled=True,
    ).reshape(rows * piece, width_here)

    low_part = lax.dot_general(
        up_weight, output_gradient_rows, (((1,), (1,)), ((), ())),
        preferred_element_type=jnp.float32,
    )
    projected_part = lax.dot_general(
        down_weight, attention_slot_outputs, (((0,), (1,)), ((), ())),
        preferred_element_type=jnp.float32,
    )
    parts = jnp.concatenate([low_part, projected_part], axis=1)
    tokens_both = parts.shape[1]
    parts = lax.all_to_all(
        parts.reshape(tp, rank // tp, tokens_both), "tp", split_axis=0, concat_axis=0, tiled=True
    )
    sums = jnp.sum(parts, axis=0).astype(jnp.bfloat16)
    sums = lax.all_to_all(
        jnp.broadcast_to(sums[None], (tp, rank // tp, tokens_both)),
        "tp", split_axis=0, concat_axis=0, tiled=True,
    ).reshape(rank, tokens_both)
    low = sums[:, : rows_here * ROW_TOKENS].reshape(rank, rows_here, ROW_TOKENS)
    projected = sums[:, rows_here * ROW_TOKENS :].reshape(rank, slot_cap, ROW_TOKENS)

    low_send = jnp.zeros((groups, rank, ROW_TOKENS), jnp.bfloat16)
    for r in range(rows_here):
        hit = own_dest[r] == group_ids
        low_send = jnp.where(hit[:, None, None], low[:, r][None], low_send)
    row_position = position.reshape(groups, rows_here)
    hit_row = assign.reshape(groups, rows_here) == own_group
    wanted = jnp.sum(jnp.where(hit_row, row_position, 0), axis=1)
    projected_send = jnp.zeros((groups, rank, ROW_TOKENS), jnp.bfloat16)
    for s in range(slot_cap):
        hit = wanted == s
        projected_send = jnp.where(hit[:, None, None], projected[:, s][None], projected_send)
    crossed = lax.all_to_all(
        jnp.concatenate([low_send, projected_send], axis=1),
        "group", split_axis=0, concat_axis=0, tiled=True,
    )
    slot_ids = jnp.arange(slot_cap, dtype=jnp.int32)
    slot_match = (hit_row[:, :, None] & (row_position[:, :, None] == slot_ids)).any(axis=1)
    slot_has = slot_match.any(axis=0)
    slot_source = jnp.sum(slot_match * group_ids[:, None], axis=0)
    low_slot = jnp.concatenate(
        [
            jnp.where(
                slot_has[s],
                lax.dynamic_index_in_dim(crossed, slot_source[s], 0, keepdims=False)[:rank],
                jnp.zeros((rank, ROW_TOKENS), jnp.bfloat16),
            )
            for s in range(slot_cap)
        ],
        axis=1,
    )
    projected_row = jnp.concatenate(
        [
            lax.dynamic_index_in_dim(crossed, own_dest[r], 0, keepdims=False)[rank:]
            for r in range(rows_here)
        ],
        axis=1,
    )
    down_part = jnp.dot(low_slot, attention_slot_outputs, preferred_element_type=jnp.float32)
    up_part = jnp.dot(projected_row, output_gradient_rows, preferred_element_type=jnp.float32)
    grads = (scale_factor * jnp.concatenate([down_part, up_part], axis=0)).astype(jnp.bfloat16)
    share = 2 * rank // groups
    grads = lax.all_to_all(
        grads.reshape(groups, share, width_here), "group", split_axis=0, concat_axis=0, tiled=True
    )
    grads = jnp.sum(grads.astype(jnp.float32), axis=0)
    grads = lax.all_to_all(
        jnp.broadcast_to(grads[None], (groups, share, width_here)),
        "group", split_axis=0, concat_axis=0, tiled=True,
    ).reshape(2 * rank, width_here)
    down_weight_gradient = grads[:rank].T
    up_weight_gradient = grads[rank:]

    index = lax.axis_index("tp")
    chips = tp // 2
    y, core = index // 2, index % 2
    forward = [(2 * a + b, 2 * ((a + 1) % chips) + b) for a in range(chips) for b in range(2)]
    backward = [(2 * a + b, 2 * ((a - 1) % chips) + b) for a in range(chips) for b in range(2)]
    swap = [(i, i ^ 1) for i in range(tp)]
    half = spread.shape[0] // 2

    from_left = lax.ppermute(spread, "tp", forward)
    from_right = lax.ppermute(spread, "tp", backward)
    far = jnp.concatenate(
        [
            lax.ppermute(from_left[:half], "tp", forward),
            lax.ppermute(from_right[half:], "tp", backward),
        ],
        axis=0,
    )

    def term(block, owner_y, owner_core):
        columns = lax.dynamic_slice_in_dim(
            output_weight, (owner_y * 2 + owner_core) * width_here, width_here, axis=1
        )
        columns_up = lax.dynamic_slice_in_dim(
            up_all, owner_y * 2 + owner_core, 1, axis=0
        )[0]
        return (
            lax.dot_general(
                block, columns, (((1,), (1,)), ((), ())), preferred_element_type=jnp.float32
            ),
            lax.dot_general(
                block, columns_up, (((1,), (1,)), ((), ())), preferred_element_type=jnp.float32
            ),
        )

    up_all = lax.all_gather(up_weight, "tp", axis=0)
    base, low_own = 0.0, 0.0
    for block, step in ((spread, 0), (from_left, chips - 1), (from_right, 1), (far, 2)):
        owner = lax.rem(y + step, chips)
        for part, owner_core in ((block, core), (lax.ppermute(block, "tp", swap), 1 - core)):
            a, b = term(part, owner, owner_core)
            base, low_own = base + a, low_own + b
    row_input = (
        base
        + adapter_scale
        * lax.dot_general(
            low_own.astype(jnp.bfloat16), down_weight, (((1,), (1,)), ((), ())),
            preferred_element_type=jnp.float32,
        )
    ).astype(jnp.bfloat16)

    all_match = (assign[None, :] == group_ids[:, None])[:, None, :] & (
        position[None, None, :] == slot_ids[None, :, None]
    )
    all_match = all_match.reshape(groups * slot_cap, rows)
    all_has = all_match.any(axis=1)
    all_source = jnp.sum(all_match * jnp.arange(rows, dtype=jnp.int32)[None, :], axis=1)
    placed = jnp.take(row_input.reshape(rows, piece, width_here), all_source, axis=0)
    placed = jnp.where(all_has[:, None, None], placed, jnp.zeros_like(placed))
    arrived = lax.all_to_all(
        placed.reshape(groups, slot_cap, piece, width_here),
        "group", split_axis=0, concat_axis=0, tiled=True,
    )
    attention_input_gradient = arrived.transpose(1, 0, 2, 3).reshape(
        slot_cap * ROW_TOKENS, width_here
    )
    return (attention_input_gradient, down_weight_gradient, up_weight_gradient)


def solution(mesh):
    in_specs = (
        P("group", "tp"),
        P("group", "tp"),
        P("tp", None),
        P("tp", None),
        P(None, "tp"),
        P(),
        P(),
    )
    out_specs = (P("group", "tp"), P("tp", None), P(None, "tp"))
    return jax.shard_map(body, mesh=mesh, in_specs=in_specs, out_specs=out_specs, check_vma=False)
```

```python
import functools
import math

import jax
import jax.numpy as jnp
from jax import lax
from jax.experimental import pallas as pl
from jax.experimental.pallas import tpu as pltpu
from jax.sharding import PartitionSpec as P

ROW_TOKENS = 128
LANES = 128


adapter_scale = 2.0

CONTRACT_MINOR = (((1,), (1,)), ((), ()))


def dot_minor(left, right):
    return lax.dot_general(left, right, CONTRACT_MINOR, preferred_element_type=jnp.float32)


def early_kernel(count, owner, *refs):
    blocks, (weight, up, base, low) = refs[:count], refs[count:]
    block_id, tile = pl.program_id(0), pl.program_id(1)
    width = weight.shape[0]
    columns = pl.ds(pl.multiple_of(tile * width, width), width)
    for i in range(count):

        @pl.when(block_id == i)
        def _():
            value = dot_minor(blocks[i][...], weight[...])
            if i == 0:
                base[:, columns] = value
            else:
                base[:, columns] += value

            @pl.when(tile == 0)
            def _():
                value_low = dot_minor(blocks[i][...], up[0])
                if i == 0:
                    low[...] = value_low
                else:
                    low[...] += value_low


def early_products(owner, blocks, output_weight, up_all):
    count = len(blocks)
    tokens, width = blocks[0].shape
    out_width = output_weight.shape[0]
    rank = up_all.shape[1]
    tiles = 2
    whole = pl.BlockSpec((tokens, width), lambda k, n, owner: (0, 0))
    return pl.pallas_call(
        functools.partial(early_kernel, count),
        grid_spec=pltpu.PrefetchScalarGridSpec(
            num_scalar_prefetch=1,
            grid=(count, tiles),
            in_specs=[whole] * count
            + [
                pl.BlockSpec((out_width // tiles, width), lambda k, n, owner: (n, owner[k])),
                pl.BlockSpec((1, rank, width), lambda k, n, owner: (owner[k], 0, 0)),
            ],
            out_specs=[
                pl.BlockSpec((tokens, out_width), lambda k, n, owner: (0, 0)),
                pl.BlockSpec((tokens, rank), lambda k, n, owner: (0, 0)),
            ],
        ),
        out_shape=[
            jax.ShapeDtypeStruct((tokens, out_width), jnp.float32),
            jax.ShapeDtypeStruct((tokens, rank), jnp.float32),
        ],
        compiler_params=pltpu.CompilerParams(vmem_limit_bytes=40 * 2**20),
        cost_estimate=pl.CostEstimate(
            flops=2 * count * tokens * width * out_width,
            bytes_accessed=2 * count * width * (tokens + out_width) + 8 * tokens * out_width,
            transcendentals=0,
        ),
        name="early_products",
    )(owner, *blocks, output_weight, up_all)


def last_kernel(
    owner, dest, place, far_a, far_b, other_a, other_b, weight_far, weight_other,
    up_far, up_other, base, low, down, out, low_rounded,
):
    half = far_a.shape[0]
    rows = dest.shape[0]
    piece = 2 * half // rows

    @pl.when(pl.program_id(0) == 0)
    def _():
        for start, far, other in ((0, far_a, other_a), (half, far_b, other_b)):
            part = pl.ds(start, half)
            total = low[part, :] + dot_minor(far[...], up_far[0]) + dot_minor(other[...], up_other[0])
            low_rounded[part, :] = total.astype(jnp.bfloat16)

    out[...] = jnp.zeros_like(out)
    for start, far, other in ((0, far_a, other_a), (half, far_b, other_b)):
        part = pl.ds(start, half)
        total = base[part, :] + dot_minor(far[...], weight_far[...])
        total += dot_minor(other[...], weight_other[...])
        total += adapter_scale * dot_minor(low_rounded[part, :], down[...])
        for i in range(half // piece):
            row = start // piece + i
            mine = total[i * piece : (i + 1) * piece]
            folded = jnp.concatenate([mine[:, :LANES], mine[:, LANES:]], axis=0)
            out[dest[row], place[row]] = folded.astype(jnp.bfloat16)


def last_products(
    owner, dest, place, far, other, output_weight, up_all, base, low, down_weight, groups, slots
):
    half, width = far[0].shape
    tokens = 2 * half
    out_width = output_weight.shape[0]
    rank = up_all.shape[1]
    piece = tokens // dest.shape[0]
    tile = 2 * LANES
    whole = pl.BlockSpec((half, width), lambda n, *s: (0, 0))
    return pl.pallas_call(
        last_kernel,
        grid_spec=pltpu.PrefetchScalarGridSpec(
            num_scalar_prefetch=3,
            grid=(out_width // tile,),
            in_specs=[whole] * 4
            + [
                pl.BlockSpec((tile, width), lambda n, owner, *s: (n, owner[0])),
                pl.BlockSpec((tile, width), lambda n, owner, *s: (n, owner[1])),
                pl.BlockSpec((1, rank, width), lambda n, owner, *s: (owner[0], 0, 0)),
                pl.BlockSpec((1, rank, width), lambda n, owner, *s: (owner[1], 0, 0)),
                pl.BlockSpec((tokens, tile), lambda n, *s: (0, n)),
                pl.BlockSpec((tokens, rank), lambda n, *s: (0, 0)),
                pl.BlockSpec((tile, rank), lambda n, *s: (n, 0)),
            ],
            out_specs=pl.BlockSpec(
                (groups, slots + 1, 2 * piece, LANES), lambda n, *s: (0, 0, 0, n)
            ),
            scratch_shapes=[pltpu.VMEM((tokens, rank), jnp.bfloat16)],
        ),
        out_shape=jax.ShapeDtypeStruct(
            (groups, slots + 1, 2 * piece, out_width // 2), jnp.bfloat16
        ),
        compiler_params=pltpu.CompilerParams(vmem_limit_bytes=40 * 2**20),
        cost_estimate=pl.CostEstimate(
            flops=4 * tokens * width * out_width,
            bytes_accessed=4 * width * (tokens + out_width) + 8 * tokens * out_width,
            transcendentals=0,
        ),
        name="last_products",
    )(
        owner, dest, place, *far, *other, output_weight, output_weight, up_all, up_all, base, low,
        down_weight,
    )


def unfold_kernel(arrived, out):
    groups, _, folded, _ = arrived.shape
    piece = folded // 2
    for pair in range(groups // 2):
        halves = []
        for j in (2 * pair, 2 * pair + 1):
            value = arrived[j, 0].astype(jnp.float32)
            pieces = []
            for n in range(value.shape[1] // LANES):
                lanes = slice(n * LANES, (n + 1) * LANES)
                pieces += [value[:piece, lanes], value[piece:, lanes]]
            halves.append(jnp.concatenate(pieces, axis=1))
        out[pl.ds(pair * folded, folded), :] = jnp.concatenate(halves, axis=0).astype(out.dtype)


def unfold(arrived, slots):
    groups, _, folded, half_width = arrived.shape
    return pl.pallas_call(
        unfold_kernel,
        grid=(slots,),
        in_specs=[pl.BlockSpec((groups, 1, folded, half_width), lambda s: (0, s, 0, 0))],
        out_specs=pl.BlockSpec((groups * folded // 2, 2 * half_width), lambda s: (s, 0)),
        out_shape=jax.ShapeDtypeStruct(
            (slots * groups * folded // 2, 2 * half_width), jnp.bfloat16
        ),
        compiler_params=pltpu.CompilerParams(vmem_limit_bytes=16 * 2**20),
        name="unfold",
    )(arrived)


def body(
    attention_slot_outputs,
    output_gradient_rows,
    output_weight,
    down_weight,
    up_weight,
    assign,
    counts,
):
    groups = counts.shape[0]
    rows = assign.shape[0]
    rows_here = output_gradient_rows.shape[0] // ROW_TOKENS
    slot_cap = attention_slot_outputs.shape[0] // ROW_TOKENS
    width_here = output_gradient_rows.shape[1]
    rank = up_weight.shape[0]
    tp = lax.axis_size("tp")
    piece = ROW_TOKENS // groups
    own_group = lax.axis_index("group")
    group_ids = jnp.arange(groups, dtype=jnp.int32)
    onehot = (assign[:, None] == group_ids[None, :]).astype(jnp.int32)
    before = jnp.cumsum(onehot, axis=0) - onehot
    order_in = jnp.sum(before * onehot, axis=1)
    free_slots = jnp.sum(onehot * counts[None, :], axis=1)
    position = slot_cap - free_slots + order_in
    own_dest = lax.dynamic_slice_in_dim(assign, own_group * rows_here, rows_here)
    scale_factor = adapter_scale / math.sqrt(rows * ROW_TOKENS)

    spread = lax.all_to_all(
        output_gradient_rows.reshape(rows_here, groups, piece, width_here).transpose(1, 0, 2, 3),
        "group",
        split_axis=0,
        concat_axis=0,
        tiled=True,
    ).reshape(rows * piece, width_here)

    up_all = lax.all_gather(up_weight, "tp", axis=0)
    low_part = dot_minor(up_weight, output_gradient_rows)
    projected_part = lax.dot_general(
        down_weight, attention_slot_outputs, (((0,), (1,)), ((), ())),
        preferred_element_type=jnp.float32,
    )
    parts = lax.all_gather(jnp.concatenate([low_part, projected_part], axis=1), "tp", axis=0)
    sums = jnp.sum(parts, axis=0).astype(jnp.bfloat16)
    low = sums[:, : rows_here * ROW_TOKENS].reshape(rank, rows_here, ROW_TOKENS)
    projected = sums[:, rows_here * ROW_TOKENS :].reshape(rank, slot_cap, ROW_TOKENS)

    low_send = jnp.zeros((groups, rank, ROW_TOKENS), jnp.bfloat16)
    for r in range(rows_here):
        hit = own_dest[r] == group_ids
        low_send = jnp.where(hit[:, None, None], low[:, r][None], low_send)
    row_position = position.reshape(groups, rows_here)
    hit_row = assign.reshape(groups, rows_here) == own_group
    wanted = jnp.sum(jnp.where(hit_row, row_position, 0), axis=1)
    projected_send = jnp.zeros((groups, rank, ROW_TOKENS), jnp.bfloat16)
    for s in range(slot_cap):
        hit = wanted == s
        projected_send = jnp.where(hit[:, None, None], projected[:, s][None], projected_send)
    crossed = lax.all_to_all(
        jnp.concatenate([low_send, projected_send], axis=1),
        "group", split_axis=0, concat_axis=0, tiled=True,
    )
    slot_ids = jnp.arange(slot_cap, dtype=jnp.int32)
    slot_match = (hit_row[:, :, None] & (row_position[:, :, None] == slot_ids)).any(axis=1)
    slot_has = slot_match.any(axis=0)
    slot_source = jnp.sum(slot_match * group_ids[:, None], axis=0)
    low_slot = jnp.concatenate(
        [
            jnp.where(
                slot_has[s],
                lax.dynamic_index_in_dim(crossed, slot_source[s], 0, keepdims=False)[:rank],
                jnp.zeros((rank, ROW_TOKENS), jnp.bfloat16),
            )
            for s in range(slot_cap)
        ],
        axis=1,
    )
    projected_row = jnp.concatenate(
        [
            lax.dynamic_index_in_dim(crossed, own_dest[r], 0, keepdims=False)[rank:]
            for r in range(rows_here)
        ],
        axis=1,
    )
    down_part = jnp.dot(low_slot, attention_slot_outputs, preferred_element_type=jnp.float32)
    up_part = jnp.dot(projected_row, output_gradient_rows, preferred_element_type=jnp.float32)
    share = 2 * rank // groups
    grads = lax.all_to_all(
        jnp.concatenate([down_part, up_part], axis=0).reshape(groups, share, width_here),
        "group", split_axis=0, concat_axis=0, tiled=True,
    )
    grads = (scale_factor * jnp.sum(grads, axis=0)).astype(jnp.bfloat16)

    index = lax.axis_index("tp")
    chips = tp // 2
    y, core = index // 2, index % 2
    forward = [(2 * a + b, 2 * ((a + 1) % chips) + b) for a in range(chips) for b in range(2)]
    backward = [(2 * a + b, 2 * ((a - 1) % chips) + b) for a in range(chips) for b in range(2)]
    swap = [(i, i ^ 1) for i in range(tp)]
    half = spread.shape[0] // 2

    from_left = lax.ppermute(spread, "tp", forward)
    from_right = lax.ppermute(spread, "tp", backward)
    far = [
        lax.ppermute(from_left[:half], "tp", forward),
        lax.ppermute(from_right[half:], "tp", backward),
    ]
    blocks, owner = [], []
    for block, step in ((spread, 0), (from_left, chips - 1), (from_right, 1)):
        blocks += [block, lax.ppermute(block, "tp", swap)]
        pair = 2 * lax.rem(y + step, chips)
        owner += [pair + core, pair + 1 - core]
    base, low_own = early_products(jnp.stack(owner), blocks, output_weight, up_all)
    pair = 2 * lax.rem(y + 2, chips)
    placed = last_products(
        jnp.stack([pair + core, pair + 1 - core]),
        assign,
        position,
        far,
        [lax.ppermute(part, "tp", swap) for part in far],
        output_weight,
        up_all,
        base,
        low_own,
        down_weight,
        groups,
        slot_cap,
    )

    folded = (2 * piece, width_here // 2)
    placed = placed.at[:, slot_cap].set(jnp.broadcast_to(grads.reshape(folded), (groups,) + folded))
    arrived = lax.all_to_all(placed, "group", split_axis=0, concat_axis=0, tiled=True)
    attention_input_gradient = unfold(arrived, slot_cap)
    grads = arrived[:, slot_cap].reshape(2 * rank, width_here).astype(jnp.float32)
    return (attention_input_gradient, grads[:rank].T, grads[rank:])


def solution(mesh):
    in_specs = (
        P("group", "tp"),
        P("group", "tp"),
        P("tp", None),
        P("tp", None),
        P(None, "tp"),
        P(),
        P(),
    )
    out_specs = (P("group", "tp"), P("tp", None), P(None, "tp"))
    return jax.shard_map(body, mesh=mesh, in_specs=in_specs, out_specs=out_specs, check_vma=False)
```

```python
import functools
import math

import jax
import jax.numpy as jnp
from jax import lax
from jax.experimental import pallas as pl
from jax.experimental.pallas import tpu as pltpu
from jax.sharding import PartitionSpec as P

ROW_TOKENS = 128
LANES = 128


adapter_scale = 2.0

HBM = pl.BlockSpec(memory_space=pl.ANY)
VMEM = pl.BlockSpec(memory_space=pltpu.VMEM)
SMEM = pl.BlockSpec(memory_space=pltpu.SMEM)


def dot_minor(left, right):
    return lax.dot_general(
        left, right, (((1,), (1,)), ((), ())), preferred_element_type=jnp.float32
    )


def block_kernel(sizes, ahead, first, owner, *refs):
    refs = list(refs)
    count, loads = len(sizes), owner.shape[0] - len(sizes)
    parts = [[refs.pop(0) for _ in range(size)] for size in sizes]
    weight, up = refs.pop(0), refs.pop(0)
    if not first:
        base_in, low_in = refs.pop(0), refs.pop(0)
    base, low = refs.pop(0), refs.pop(0)
    if loads:
        later_w, later_u = refs.pop(0), refs.pop(0)
    x, w, u, x_sem, w_sem, u_sem = refs
    width = x.shape[2]
    copies = []
    for k in range(count):
        each, start = [], 0
        for i, part in enumerate(parts[k]):
            rows = pl.ds(start, part.shape[0])
            each.append(pltpu.make_async_copy(part, x.at[k, rows], x_sem.at[k, i]))
            start += part.shape[0]
        columns = pl.ds(pl.multiple_of(owner[k] * width, width), width)
        each.append(pltpu.make_async_copy(weight.at[:, columns], w.at[k], w_sem.at[k]))
        each.append(pltpu.make_async_copy(up.at[owner[k]], u.at[k], u_sem.at[k]))
        copies.append(each)
    for k in range(loads):
        columns = pl.ds(pl.multiple_of(owner[count + k] * width, width), width)
        lanes = pl.ds(k * width, width)
        copies.append([
            pltpu.make_async_copy(weight.at[:, columns], later_w.at[:, lanes], w_sem.at[count + k]),
            pltpu.make_async_copy(up.at[owner[count + k]], later_u.at[:, lanes], u_sem.at[count + k]),
        ])
    for k in range(ahead):
        for copy in copies[k]:
            copy.start()
    for k in range(count):
        for copy in copies[k]:
            copy.wait()
        if k + ahead < len(copies):
            for copy in copies[k + ahead]:
                copy.start()
        value, value_low = dot_minor(x[k], w[k]), dot_minor(x[k], u[k])
        if k > 0:
            base[...] += value
            low[...] += value_low
        elif first:
            base[...] = value
            low[...] = value_low
        else:
            base[...] = base_in[...] + value
            low[...] = low_in[...] + value_low
    for k in range(count, count + loads):
        if k + ahead < len(copies) and k >= count:
            for copy in copies[k + ahead]:
                copy.start()
        for copy in copies[k]:
            copy.wait()


def block_products(owner, blocks, output_weight, up_all, base=None, low=None, name="block_products"):
    count = len(blocks)
    loads = owner.shape[0] - count
    tokens = sum(part.shape[0] for part in blocks[0])
    width = blocks[0][0].shape[1]
    out_width = output_weight.shape[0]
    rank = up_all.shape[1]
    first = base is None
    out_shape = [
        jax.ShapeDtypeStruct((tokens, out_width), jnp.float32),
        jax.ShapeDtypeStruct((tokens, rank), jnp.float32),
    ]
    if loads:
        out_shape += [
            jax.ShapeDtypeStruct((out_width, loads * width), jnp.bfloat16),
            jax.ShapeDtypeStruct((rank, loads * width), jnp.bfloat16),
        ]
    parts = [part for block in blocks for part in block]
    return pl.pallas_call(
        functools.partial(block_kernel, [len(block) for block in blocks], 2, first),
        in_specs=[SMEM] + [HBM] * (len(parts) + 2) + ([] if first else [VMEM] * 2),
        out_specs=[VMEM] * len(out_shape),
        out_shape=out_shape,
        scratch_shapes=[
            pltpu.VMEM((count, tokens, width), jnp.bfloat16),
            pltpu.VMEM((count, out_width, width), jnp.bfloat16),
            pltpu.VMEM((count, rank, width), jnp.bfloat16),
            pltpu.SemaphoreType.DMA((count, 2)),
            pltpu.SemaphoreType.DMA((count + loads,)),
            pltpu.SemaphoreType.DMA((count + loads,)),
        ],
        compiler_params=pltpu.CompilerParams(vmem_limit_bytes=30 * 2**20),
        cost_estimate=pl.CostEstimate(
            flops=2 * count * tokens * width * out_width,
            bytes_accessed=2 * width * (count * tokens + (count + loads) * out_width),
            transcendentals=0,
        ),
        name=name,
    )(owner, *parts, output_weight, up_all, *([] if first else [base, low]))


def last_kernel(
    dest, place, far_a, far_b, other_a, other_b, w, u, base, low, down, out, x, low_rounded, x_sem
):
    half, width = far_a.shape
    rows = dest.shape[0]
    piece = 2 * half // rows
    tile = 2 * LANES
    copies = []
    for i, part in enumerate((far_a, far_b, other_a, other_b)):
        lanes = pl.ds((i // 2) * width, width)
        rows_of = pl.ds((i % 2) * half, half)
        copies.append(pltpu.make_async_copy(part, x.at[rows_of, lanes], x_sem.at[i]))
    for copy in copies:
        copy.start()
    out[...] = jnp.zeros_like(out)
    for copy in copies:
        copy.wait()
    low_rounded[...] = (low[...] + dot_minor(x[...], u[...])).astype(jnp.bfloat16)
    for n in range(w.shape[0] // tile):
        span = slice(n * tile, (n + 1) * tile)
        total = base[:, span] + dot_minor(x[...], w[span])
        total += adapter_scale * dot_minor(low_rounded[...], down[span])
        for row in range(rows):
            mine = total[row * piece : (row + 1) * piece]
            folded = jnp.concatenate([mine[:, :LANES], mine[:, LANES:]], axis=0)
            out[dest[row], place[row], :, n * LANES : (n + 1) * LANES] = folded.astype(jnp.bfloat16)


def last_products(dest, place, far, other, w, u, base, low, down_weight, groups, slots):
    half, width = far[0].shape
    tokens = 2 * half
    out_width, rank = down_weight.shape
    piece = tokens // dest.shape[0]
    return pl.pallas_call(
        last_kernel,
        in_specs=[SMEM] * 2 + [HBM] * 4 + [VMEM] * 5,
        out_specs=VMEM,
        scratch_shapes=[
            pltpu.VMEM((tokens, 2 * width), jnp.bfloat16),
            pltpu.VMEM((tokens, rank), jnp.bfloat16),
            pltpu.SemaphoreType.DMA((4,)),
        ],
        out_shape=jax.ShapeDtypeStruct(
            (groups, slots + 1, 2 * piece, out_width // 2), jnp.bfloat16
        ),
        compiler_params=pltpu.CompilerParams(vmem_limit_bytes=20 * 2**20),
        cost_estimate=pl.CostEstimate(
            flops=4 * tokens * width * out_width,
            bytes_accessed=4 * width * (tokens + out_width) + 8 * tokens * out_width,
            transcendentals=0,
        ),
        name="last_products",
    )(dest, place, *far, *other, w, u, base, low, down_weight)


def gradient_kernel(source, has, dest, crossed, attention, gradient, out, low, projected):
    rank = crossed.shape[2]
    for s in range(source.shape[0]):
        value = crossed[source[s], 0].astype(jnp.float32) * has[s].astype(jnp.float32)
        low[:, s * ROW_TOKENS : (s + 1) * ROW_TOKENS] = value.astype(jnp.bfloat16)
    for r in range(dest.shape[0]):
        projected[:, r * ROW_TOKENS : (r + 1) * ROW_TOKENS] = crossed[dest[r], 1]
    out[:rank] = jnp.dot(low[...], attention[...], preferred_element_type=jnp.float32)
    out[rank:] = jnp.dot(projected[...], gradient[...], preferred_element_type=jnp.float32)


def gradient_products(source, has, dest, crossed, attention, gradient):
    rank = crossed.shape[2]
    slot_tokens, width = attention.shape
    row_tokens = gradient.shape[0]
    return pl.pallas_call(
        gradient_kernel,
        in_specs=[SMEM] * 3 + [VMEM] * 3,
        out_specs=VMEM,
        out_shape=jax.ShapeDtypeStruct((2 * rank, width), jnp.float32),
        scratch_shapes=[
            pltpu.VMEM((rank, slot_tokens), jnp.bfloat16),
            pltpu.VMEM((rank, row_tokens), jnp.bfloat16),
        ],
        compiler_params=pltpu.CompilerParams(vmem_limit_bytes=16 * 2**20),
        cost_estimate=pl.CostEstimate(
            flops=2 * rank * width * (slot_tokens + row_tokens),
            bytes_accessed=2 * width * (slot_tokens + row_tokens),
            transcendentals=0,
        ),
        name="gradient_products",
    )(source, has, dest, crossed, attention, gradient)


def unfold_kernel(slots, arrived, out, down_gradient, up_gradient):
    groups, _, folded, half_width = arrived.shape
    piece = folded // 2
    step = pl.program_id(0)

    @pl.when(step < slots)
    def _():
        for pair in range(groups // 2):
            halves = []
            for j in (2 * pair, 2 * pair + 1):
                value = arrived[j, 0].astype(jnp.float32)
                pieces = []
                for n in range(half_width // LANES):
                    lanes = slice(n * LANES, (n + 1) * LANES)
                    pieces += [value[:piece, lanes], value[piece:, lanes]]
                halves.append(jnp.concatenate(pieces, axis=1))
            out[pl.ds(pair * folded, folded), :] = jnp.concatenate(halves, axis=0).astype(out.dtype)

    @pl.when(step == slots)
    def _():
        values = []
        for j in range(groups):
            value = arrived[j, 0].astype(jnp.float32)
            values.append(jnp.concatenate([value[:piece], value[piece:]], axis=1))
        down_gradient[...] = jnp.concatenate(values[: groups // 2], axis=0).T
        up_gradient[...] = jnp.concatenate(values[groups // 2 :], axis=0)


def unfold(arrived, slots):
    groups, _, folded, half_width = arrived.shape
    piece, width = folded // 2, 2 * half_width
    rank = groups * piece // 2
    return pl.pallas_call(
        functools.partial(unfold_kernel, slots),
        grid=(slots + 1,),
        in_specs=[pl.BlockSpec((groups, 1, folded, half_width), lambda s: (0, s, 0, 0))],
        out_specs=[
            pl.BlockSpec((groups * piece, width), lambda s: (jnp.minimum(s, slots - 1), 0)),
            pl.BlockSpec((width, rank), lambda s: (0, 0)),
            pl.BlockSpec((rank, width), lambda s: (0, 0)),
        ],
        out_shape=[
            jax.ShapeDtypeStruct((slots * groups * piece, width), jnp.bfloat16),
            jax.ShapeDtypeStruct((width, rank), jnp.float32),
            jax.ShapeDtypeStruct((rank, width), jnp.float32),
        ],
        compiler_params=pltpu.CompilerParams(vmem_limit_bytes=16 * 2**20),
        name="unfold",
    )(arrived)


def body(
    attention_slot_outputs,
    output_gradient_rows,
    output_weight,
    down_weight,
    up_weight,
    assign,
    counts,
):
    groups = counts.shape[0]
    rows = assign.shape[0]
    rows_here = output_gradient_rows.shape[0] // ROW_TOKENS
    slot_cap = attention_slot_outputs.shape[0] // ROW_TOKENS
    width_here = output_gradient_rows.shape[1]
    rank = up_weight.shape[0]
    tp = lax.axis_size("tp")
    piece = ROW_TOKENS // groups
    own_group = lax.axis_index("group")
    group_ids = jnp.arange(groups, dtype=jnp.int32)
    onehot = (assign[:, None] == group_ids[None, :]).astype(jnp.int32)
    before = jnp.cumsum(onehot, axis=0) - onehot
    order_in = jnp.sum(before * onehot, axis=1)
    free_slots = jnp.sum(onehot * counts[None, :], axis=1)
    position = slot_cap - free_slots + order_in
    own_dest = lax.dynamic_slice_in_dim(assign, own_group * rows_here, rows_here)
    scale_factor = adapter_scale / math.sqrt(rows * ROW_TOKENS)

    index = lax.axis_index("tp")
    chips = tp // 2
    y, core = index // 2, index % 2

    def move(value, n):
        pairs = [(2 * a + b, 2 * ((a + n) % chips) + b) for a in range(chips) for b in range(2)]
        return lax.ppermute(value, "tp", pairs)

    def swap(value):
        return lax.ppermute(value, "tp", [(i, i ^ 1) for i in range(tp)])

    spread = lax.all_to_all(
        output_gradient_rows.reshape(rows_here, groups, piece, width_here).transpose(1, 0, 2, 3),
        "group",
        split_axis=0,
        concat_axis=0,
        tiled=True,
    ).reshape(rows * piece, width_here)

    up_all = lax.all_gather(up_weight, "tp", axis=0)
    low_part = dot_minor(up_weight, output_gradient_rows)
    projected_part = lax.dot_general(
        down_weight, attention_slot_outputs, (((0,), (1,)), ((), ())),
        preferred_element_type=jnp.float32,
    )
    parts = jnp.concatenate([low_part, projected_part], axis=1)
    parts = parts + swap(parts)
    share = lax.dynamic_slice_in_dim(parts, core * (rank // 2), rank // 2, axis=0)
    share = share + move(share, 1) + move(share, -1) + move(share, 2)
    share = share.astype(jnp.bfloat16)
    other = swap(share)
    sums = jnp.where(
        core == 0, jnp.concatenate([share, other]), jnp.concatenate([other, share])
    ).reshape(rank, rows_here + slot_cap, ROW_TOKENS)

    row_position = position.reshape(groups, rows_here)
    hit_row = assign.reshape(groups, rows_here) == own_group
    low_pick = jnp.sum(
        jnp.where(own_dest[None, :] == group_ids[:, None], jnp.arange(1, rows_here + 1), 0), axis=1
    )
    projected_pick = jnp.sum(jnp.where(hit_row, rows_here + 1 + row_position, 0), axis=1)
    pick = jnp.stack([low_pick, projected_pick], axis=1)[:, :, None, None]
    send = jnp.zeros((groups, 2, rank, ROW_TOKENS), jnp.bfloat16)
    for i in range(rows_here + slot_cap):
        send = jnp.where(pick == i + 1, sums[:, i][None, None], send)
    crossed = lax.all_to_all(send, "group", split_axis=0, concat_axis=0, tiled=True)
    slot_ids = jnp.arange(slot_cap, dtype=jnp.int32)
    slot_match = (hit_row[:, :, None] & (row_position[:, :, None] == slot_ids)).any(axis=1)
    slot_has = slot_match.any(axis=0).astype(jnp.int32)
    slot_source = jnp.sum(slot_match * group_ids[:, None], axis=0)

    half = spread.shape[0] // 2
    top, bottom = lax.optimization_barrier((spread[:half], spread[half:]))
    left_top, right_bottom = move(top, 1), move(bottom, -1)
    left_bottom, right_top = move(bottom, 1), move(top, -1)
    far = [move(left_top, 1), move(right_bottom, -1)]

    def owners(*steps):
        pairs = [2 * lax.rem(y + step, chips) for step in steps]
        return jnp.stack([owner for pair in pairs for owner in (pair + core, pair + 1 - core)])

    base, low_own = block_products(
        owners(0), [(spread,), (swap(spread),)], output_weight, up_all, name="own_products"
    )
    left, right = (left_top, left_bottom), (right_top, right_bottom)
    base, low_own, far_weight, far_up = block_products(
        owners(chips - 1, 1, 2),
        [left, tuple(swap(part) for part in left), right, tuple(swap(part) for part in right)],
        output_weight,
        up_all,
        base,
        low_own,
        name="side_products",
    )
    crossed, _ = lax.optimization_barrier((crossed, base))
    grads = gradient_products(
        slot_source, slot_has, own_dest, crossed, attention_slot_outputs, output_gradient_rows
    )
    share_rows = 2 * rank // groups
    grads = lax.all_to_all(
        grads.reshape(groups, share_rows, width_here), "group", split_axis=0, concat_axis=0,
        tiled=True,
    )
    grads = (scale_factor * jnp.sum(grads, axis=0)).astype(jnp.bfloat16)
    placed = last_products(
        assign, position, far, [swap(part) for part in far], far_weight, far_up, base, low_own,
        down_weight, groups, slot_cap,
    )

    folded = (2 * piece, width_here // 2)
    grads = jnp.concatenate([grads[:, : folded[1]], grads[:, folded[1] :]], axis=0)
    placed = placed.at[:, slot_cap].set(jnp.broadcast_to(grads, (groups,) + folded))
    arrived = lax.all_to_all(placed, "group", split_axis=0, concat_axis=0, tiled=True)
    return tuple(unfold(arrived, slot_cap))


def solution(mesh):
    in_specs = (
        P("group", "tp"),
        P("group", "tp"),
        P("tp", None),
        P("tp", None),
        P(None, "tp"),
        P(),
        P(),
    )
    out_specs = (P("group", "tp"), P("tp", None), P(None, "tp"))
    return jax.shard_map(body, mesh=mesh, in_specs=in_specs, out_specs=out_specs, check_vma=False)
```

```python
import functools
import math

import jax
import jax.numpy as jnp
from jax import lax
from jax.experimental import pallas as pl
from jax.experimental.pallas import tpu as pltpu
from jax.sharding import PartitionSpec as P

ROW_TOKENS = 128
LANES = 128


adapter_scale = 2.0

HBM = pl.BlockSpec(memory_space=pltpu.HBM)
VMEM = pl.BlockSpec(memory_space=pltpu.VMEM)
SMEM = pl.BlockSpec(memory_space=pltpu.SMEM)


def dot_minor(left, right):
    return lax.dot_general(
        left, right, (((1,), (1,)), ((), ())), preferred_element_type=jnp.float32
    )


def block_kernel(table, first, index, *refs):
    refs = list(refs)
    count = len(table)
    blocks = [refs.pop(0) for _ in range(count)]
    weight, up = refs.pop(0), refs.pop(0)
    if not first:
        base_in, low_in = refs.pop(0), refs.pop(0)
    base, low, x, x_sem = refs
    width = x.shape[2]
    copies = [pltpu.make_async_copy(blocks[k], x.at[k], x_sem.at[k]) for k in range(count)]
    for copy in copies[:2]:
        copy.start()
    for k in range(count):
        copies[k].wait()
        if k + 2 < count:
            copies[k + 2].start()
        owner = index[table[k]]
        columns = pl.ds(pl.multiple_of(owner * width, width), width)
        value, value_low = dot_minor(x[k], weight[:, columns]), dot_minor(x[k], up[owner])
        if k > 0:
            base[...] += value
            low[...] += value_low
        elif first:
            base[...] = value
            low[...] = value_low
        else:
            base[...] = base_in[...] + value
            low[...] = low_in[...] + value_low


def block_products(index, table, blocks, output_weight, up_all, base=None, low=None, name=""):
    count = len(blocks)
    tokens, width = blocks[0].shape
    out_width = output_weight.shape[0]
    rank = up_all.shape[1]
    first = base is None
    return pl.pallas_call(
        functools.partial(block_kernel, table, first),
        in_specs=[SMEM] + [HBM] * count + [VMEM] * (2 if first else 4),
        out_specs=[VMEM] * 2,
        out_shape=[
            jax.ShapeDtypeStruct((tokens, out_width), jnp.float32),
            jax.ShapeDtypeStruct((tokens, rank), jnp.float32),
        ],
        scratch_shapes=[
            pltpu.VMEM((count, tokens, width), jnp.bfloat16),
            pltpu.SemaphoreType.DMA((count,)),
        ],
        compiler_params=pltpu.CompilerParams(vmem_limit_bytes=32 * 2**20),
        cost_estimate=pl.CostEstimate(
            flops=2 * count * tokens * width * out_width,
            bytes_accessed=2 * width * count * tokens,
            transcendentals=0,
        ),
        name=name,
    )(index, *blocks, output_weight, up_all, *([] if first else [base, low]))


def last_kernel(
    rows, table, index, far_a, far_b, other_a, other_b, weight, up, base, low, down, out, x,
    low_rounded, x_sem,
):
    half, width = far_a.shape
    piece = 2 * half // rows
    tile = 2 * LANES
    copies = []
    for i, part in enumerate((far_a, far_b, other_a, other_b)):
        rows_of = pl.ds((i % 2) * half, half)
        copies.append(pltpu.make_async_copy(part, x.at[i // 2, rows_of], x_sem.at[i]))
    for copy in copies:
        copy.start()
    out[...] = jnp.zeros_like(out)
    for copy in copies:
        copy.wait()
    owners = [index[i] for i in table]
    total = low[...]
    for k, owner in enumerate(owners):
        total += dot_minor(x[k], up[owner])
    low_rounded[...] = total.astype(jnp.bfloat16)
    for n in range(weight.shape[0] // tile):
        span = slice(n * tile, (n + 1) * tile)
        total = base[:, span]
        for k, owner in enumerate(owners):
            columns = pl.ds(pl.multiple_of(owner * width, width), width)
            total += dot_minor(x[k], weight[span, columns])
        total += adapter_scale * jnp.dot(
            low_rounded[...], down[:, span], preferred_element_type=jnp.float32
        )
        for row in range(rows):
            mine = total[row * piece : (row + 1) * piece]
            folded = jnp.concatenate([mine[:, :LANES], mine[:, LANES:]], axis=0)
            out[index[row], index[rows + row], :, n * LANES : (n + 1) * LANES] = folded.astype(
                jnp.bfloat16
            )


def last_products(rows, index, table, far, other, weight, up, base, low, down, groups, slots):
    half, width = far[0].shape
    tokens = 2 * half
    rank, out_width = down.shape
    piece = tokens // rows
    return pl.pallas_call(
        functools.partial(last_kernel, rows, table),
        in_specs=[SMEM] + [HBM] * 4 + [VMEM] * 5,
        out_specs=VMEM,
        scratch_shapes=[
            pltpu.VMEM((2, tokens, width), jnp.bfloat16),
            pltpu.VMEM((tokens, rank), jnp.bfloat16),
            pltpu.SemaphoreType.DMA((4,)),
        ],
        out_shape=jax.ShapeDtypeStruct(
            (groups, slots + 1, 2 * piece, out_width // 2), jnp.bfloat16
        ),
        compiler_params=pltpu.CompilerParams(vmem_limit_bytes=32 * 2**20),
        cost_estimate=pl.CostEstimate(
            flops=4 * tokens * width * out_width,
            bytes_accessed=4 * width * tokens + 8 * tokens * out_width,
            transcendentals=0,
        ),
        name="last_products",
    )(index, *far, *other, weight, up, base, low, down)


def send_kernel(groups, core_at, pick_at, index, share, other, out):
    half = share.shape[0]
    core = index[core_at]
    for group in range(groups):
        for kind in range(2):
            pick = index[pick_at + 2 * group + kind]
            lanes = pl.ds(pl.multiple_of(jnp.maximum(pick, 0) * ROW_TOKENS, ROW_TOKENS), ROW_TOKENS)
            keep = (pick >= 0).astype(jnp.float32)
            for owner, part in ((core, share), (1 - core, other)):
                value = part[:, lanes].astype(jnp.float32) * keep
                rows = pl.ds(pl.multiple_of(owner * half, half), half)
                out[group, kind, rows] = value.astype(jnp.bfloat16)


def rank_sums_to_send(index, core_at, pick_at, groups, share, other):
    rank = 2 * share.shape[0]
    return pl.pallas_call(
        functools.partial(send_kernel, groups, core_at, pick_at),
        in_specs=[SMEM, VMEM, VMEM],
        out_specs=VMEM,
        out_shape=jax.ShapeDtypeStruct((groups, 2, rank, ROW_TOKENS), jnp.bfloat16),
        compiler_params=pltpu.CompilerParams(vmem_limit_bytes=16 * 2**20),
        cost_estimate=pl.CostEstimate(
            flops=groups * rank * ROW_TOKENS, bytes_accessed=4 * groups * rank * ROW_TOKENS,
            transcendentals=0,
        ),
        name="rank_sums_to_send",
    )(index, share, other)


def gradient_kernel(
    source_at, dest_at, index, crossed, attention, gradient, out, low, projected, tokens, more, sem
):
    rank = crossed.shape[2]
    copies = [
        pltpu.make_async_copy(attention, tokens, sem.at[0]),
        pltpu.make_async_copy(gradient, more, sem.at[1]),
    ]
    for copy in copies:
        copy.start()
    for s in range(tokens.shape[0] // ROW_TOKENS):
        source = index[source_at + s]
        keep = (source >= 0).astype(jnp.float32)
        value = crossed[jnp.maximum(source, 0), 0].astype(jnp.float32) * keep
        low[:, s * ROW_TOKENS : (s + 1) * ROW_TOKENS] = value.astype(jnp.bfloat16)
    for r in range(more.shape[0] // ROW_TOKENS):
        projected[:, r * ROW_TOKENS : (r + 1) * ROW_TOKENS] = crossed[index[dest_at + r], 1]
    copies[0].wait()
    out[:rank] = jnp.dot(low[...], tokens[...], preferred_element_type=jnp.float32)
    copies[1].wait()
    out[rank:] = jnp.dot(projected[...], more[...], preferred_element_type=jnp.float32)


def gradient_products(index, source_at, dest_at, crossed, attention, gradient):
    rank = crossed.shape[2]
    slot_tokens, width = attention.shape
    row_tokens = gradient.shape[0]
    return pl.pallas_call(
        functools.partial(gradient_kernel, source_at, dest_at),
        in_specs=[SMEM, VMEM, HBM, HBM],
        out_specs=VMEM,
        out_shape=jax.ShapeDtypeStruct((2 * rank, width), jnp.float32),
        scratch_shapes=[
            pltpu.VMEM((rank, slot_tokens), jnp.bfloat16),
            pltpu.VMEM((rank, row_tokens), jnp.bfloat16),
            pltpu.VMEM(attention.shape, jnp.bfloat16),
            pltpu.VMEM(gradient.shape, jnp.bfloat16),
            pltpu.SemaphoreType.DMA((2,)),
        ],
        compiler_params=pltpu.CompilerParams(vmem_limit_bytes=16 * 2**20),
        cost_estimate=pl.CostEstimate(
            flops=2 * rank * width * (slot_tokens + row_tokens),
            bytes_accessed=2 * width * (slot_tokens + row_tokens),
            transcendentals=0,
        ),
        name="gradient_products",
    )(index, crossed, attention, gradient)


def unfold_kernel(slots, arrived, out, down_gradient, up_gradient):
    groups, _, folded, half_width = arrived.shape
    piece = folded // 2
    step = pl.program_id(0)

    @pl.when(step < slots)
    def _():
        for pair in range(groups // 2):
            halves = []
            for j in (2 * pair, 2 * pair + 1):
                value = arrived[j, 0].astype(jnp.float32)
                pieces = []
                for n in range(half_width // LANES):
                    lanes = slice(n * LANES, (n + 1) * LANES)
                    pieces += [value[:piece, lanes], value[piece:, lanes]]
                halves.append(jnp.concatenate(pieces, axis=1))
            out[pl.ds(pair * folded, folded), :] = jnp.concatenate(halves, axis=0).astype(out.dtype)

    @pl.when(step == slots)
    def _():
        values = []
        for j in range(groups):
            value = arrived[j, 0].astype(jnp.float32)
            values.append(jnp.concatenate([value[:piece], value[piece:]], axis=1))
        down_gradient[...] = jnp.concatenate(values[: groups // 2], axis=0)
        up_gradient[...] = jnp.concatenate(values[groups // 2 :], axis=0)


def unfold(arrived, slots):
    groups, _, folded, half_width = arrived.shape
    piece, width = folded // 2, 2 * half_width
    rank = groups * piece // 2
    return pl.pallas_call(
        functools.partial(unfold_kernel, slots),
        grid=(slots + 1,),
        in_specs=[pl.BlockSpec((groups, 1, folded, half_width), lambda s: (0, s, 0, 0))],
        out_specs=[
            pl.BlockSpec((groups * piece, width), lambda s: (jnp.minimum(s, slots - 1), 0)),
            pl.BlockSpec((rank, width), lambda s: (0, 0)),
            pl.BlockSpec((rank, width), lambda s: (0, 0)),
        ],
        out_shape=[
            jax.ShapeDtypeStruct((slots * groups * piece, width), jnp.bfloat16),
            jax.ShapeDtypeStruct((rank, width), jnp.float32),
            jax.ShapeDtypeStruct((rank, width), jnp.float32),
        ],
        compiler_params=pltpu.CompilerParams(vmem_limit_bytes=16 * 2**20),
        name="unfold",
    )(arrived)


def body(
    attention_slot_outputs,
    output_gradient_rows,
    output_weight,
    down_weight,
    up_weight,
    assign,
    counts,
):
    groups = counts.shape[0]
    rows = assign.shape[0]
    rows_here = output_gradient_rows.shape[0] // ROW_TOKENS
    slot_cap = attention_slot_outputs.shape[0] // ROW_TOKENS
    width_here = output_gradient_rows.shape[1]
    rank = up_weight.shape[0]
    tp = lax.axis_size("tp")
    piece = ROW_TOKENS // groups
    own_group = lax.axis_index("group")
    group_ids = jnp.arange(groups, dtype=jnp.int32)
    onehot = (assign[:, None] == group_ids[None, :]).astype(jnp.int32)
    before = jnp.cumsum(onehot, axis=0) - onehot
    order_in = jnp.sum(before * onehot, axis=1)
    free_slots = jnp.sum(onehot * counts[None, :], axis=1)
    position = slot_cap - free_slots + order_in
    own_dest = lax.dynamic_slice_in_dim(assign, own_group * rows_here, rows_here)
    scale_factor = adapter_scale / math.sqrt(rows * ROW_TOKENS)

    index = lax.axis_index("tp")
    chips = tp // 2
    y, core = index // 2, index % 2

    def move(value, n):
        pairs = [(2 * a + b, 2 * ((a + n) % chips) + b) for a in range(chips) for b in range(2)]
        return lax.ppermute(value, "tp", pairs)

    def swap(value):
        return lax.ppermute(value, "tp", [(i, i ^ 1) for i in range(tp)])

    spread = lax.all_to_all(
        output_gradient_rows.reshape(rows_here, groups, piece, width_here).transpose(1, 0, 2, 3),
        "group",
        split_axis=0,
        concat_axis=0,
        tiled=True,
    ).reshape(rows * piece, width_here)

    slot_ids = jnp.arange(slot_cap, dtype=jnp.int32)
    row_ids = jnp.arange(rows_here, dtype=jnp.int32)
    row_position = position.reshape(groups, rows_here)
    hit_row = assign.reshape(groups, rows_here) == own_group
    low_pick = jnp.max(jnp.where(own_dest[None, :] == group_ids[:, None], row_ids, -1), axis=1)
    projected_pick = jnp.max(jnp.where(hit_row, rows_here + row_position, -1), axis=1)
    slot_match = hit_row[:, :, None] & (row_position[:, :, None] == slot_ids)
    slot_source = jnp.max(jnp.where(slot_match, group_ids[:, None, None], -1), axis=(0, 1))
    owners = []
    for step in (0, chips - 1, 1, 2):
        pair = 2 * lax.rem(y + step, chips)
        owners += [pair + core, pair + 1 - core]
    pieces = [
        assign, position, jnp.stack([low_pick, projected_pick], axis=1).reshape(-1), slot_source,
        own_dest, jnp.stack(owners + [core]).astype(jnp.int32),
    ]
    at = [0]
    for part in pieces:
        at.append(at[-1] + part.shape[0])
    _, _, pick_at, source_at, dest_at, owner_at, end = at
    table = jnp.concatenate(pieces)

    up_all = lax.all_gather(up_weight, "tp", axis=0)
    low_part = dot_minor(up_weight, output_gradient_rows)
    projected_part = lax.dot_general(
        down_weight, attention_slot_outputs, (((0,), (1,)), ((), ())),
        preferred_element_type=jnp.float32,
    )
    parts = jnp.concatenate([low_part, projected_part], axis=1)
    parts = parts + swap(parts)
    share = lax.dynamic_slice_in_dim(parts, core * (rank // 2), rank // 2, axis=0)
    share = share + move(share, 1) + move(share, -1) + move(share, 2)
    share = share.astype(jnp.bfloat16)

    crossed = lax.all_to_all(
        rank_sums_to_send(table, end - 1, pick_at, groups, share, swap(share)),
        "group", split_axis=0, concat_axis=0, tiled=True,
    )

    half = spread.shape[0] // 2
    left, right = move(spread, 1), move(spread, -1)
    far = [move(left[:half], 1), move(right[half:], -1)]
    base, low_own = block_products(
        table, [owner_at, owner_at + 1], [spread, swap(spread)], output_weight, up_all,
        name="own_products",
    )
    swapped = [swap(left), swap(right)]
    crossed, _ = lax.optimization_barrier((crossed, (base, swapped)))
    base, low_own = block_products(
        table, [owner_at + i for i in range(2, 6)], [left, swapped[0], right, swapped[1]],
        output_weight, up_all, base, low_own, name="side_products",
    )
    grads = gradient_products(
        table, source_at, dest_at, crossed, attention_slot_outputs, output_gradient_rows
    )
    share_rows = 2 * rank // groups
    grads = lax.all_to_all(
        grads.reshape(groups, share_rows, width_here), "group", split_axis=0, concat_axis=0,
        tiled=True,
    )
    grads = (scale_factor * jnp.sum(grads, axis=0)).astype(jnp.bfloat16)
    placed = last_products(
        rows, table, [owner_at + 6, owner_at + 7], far, [swap(part) for part in far],
        output_weight, up_all, base, low_own, down_weight.T, groups, slot_cap,
    )

    folded = (2 * piece, width_here // 2)
    grads = jnp.concatenate([grads[:, : folded[1]], grads[:, folded[1] :]], axis=0)
    placed = placed.at[:, slot_cap].set(jnp.broadcast_to(grads, (groups,) + folded))
    arrived = lax.all_to_all(placed, "group", split_axis=0, concat_axis=0, tiled=True)
    attention_gradient, down_gradient, up_gradient = unfold(arrived, slot_cap)
    return attention_gradient, down_gradient.T, up_gradient


def solution(mesh):
    in_specs = (
        P("group", "tp"),
        P("group", "tp"),
        P("tp", None),
        P("tp", None),
        P(None, "tp"),
        P(),
        P(),
    )
    out_specs = (P("group", "tp"), P("tp", None), P(None, "tp"))
    return jax.shard_map(body, mesh=mesh, in_specs=in_specs, out_specs=out_specs, check_vma=False)
```

```python
import functools
import math

import jax
import jax.numpy as jnp
from jax import lax
from jax.experimental import pallas as pl
from jax.experimental.pallas import tpu as pltpu
from jax.sharding import PartitionSpec as P

ROW_TOKENS = 128
LANES = 128


adapter_scale = 2.0

HBM = pl.BlockSpec(memory_space=pltpu.HBM)
VMEM = pl.BlockSpec(memory_space=pltpu.VMEM)
SMEM = pl.BlockSpec(memory_space=pltpu.SMEM)


def dot_minor(left, right):
    return lax.dot_general(
        left, right, (((1,), (1,)), ((), ())), preferred_element_type=jnp.float32
    )


def load_kernel(weight, out, sem):
    count, _, width = out.shape
    copies = [
        pltpu.make_async_copy(weight.at[:, pl.ds(k * width, width)], out.at[k], sem.at[k])
        for k in range(count)
    ]
    for copy in copies:
        copy.start()
    for copy in copies:
        copy.wait()


def load_columns(weight, count):
    rows, width = weight.shape[0], weight.shape[1] // count
    return pl.pallas_call(
        load_kernel,
        in_specs=[HBM],
        out_specs=VMEM,
        out_shape=jax.ShapeDtypeStruct((count, rows, width), weight.dtype),
        scratch_shapes=[pltpu.SemaphoreType.DMA((count,))],
        compiler_params=pltpu.CompilerParams(vmem_limit_bytes=20 * 2**20),
        cost_estimate=pl.CostEstimate(
            flops=0, bytes_accessed=4 * count * rows * width, transcendentals=0
        ),
        name="load_columns",
    )(weight)


def halves_kernel(left, right, top, bottom, sem):
    half = top.shape[0]
    copies = [
        pltpu.make_async_copy(left.at[pl.ds(0, half)], top, sem.at[0]),
        pltpu.make_async_copy(right.at[pl.ds(half, half)], bottom, sem.at[1]),
    ]
    for copy in copies:
        copy.start()
    for copy in copies:
        copy.wait()


def take_halves(left, right):
    half = jax.ShapeDtypeStruct((left.shape[0] // 2, left.shape[1]), left.dtype)
    return pl.pallas_call(
        halves_kernel,
        in_specs=[HBM] * 2,
        out_specs=[HBM] * 2,
        out_shape=[half] * 2,
        scratch_shapes=[pltpu.SemaphoreType.DMA((2,))],
        name="take_halves",
    )(left, right)


def block_kernel(table, first, index, *refs):
    refs = list(refs)
    count = len(table)
    blocks = [refs.pop(0) for _ in range(count)]
    weight, up = refs.pop(0), refs.pop(0)
    if not first:
        base_in, low_in = refs.pop(0), refs.pop(0)
    base, low, x, x_sem = refs
    copies = [pltpu.make_async_copy(blocks[k], x.at[k], x_sem.at[k]) for k in range(count)]
    for copy in copies[:2]:
        copy.start()
    for k in range(count):
        copies[k].wait()
        if k + 2 < count:
            copies[k + 2].start()
        owner = index[table[k]]
        value, value_low = dot_minor(x[k], weight[owner]), dot_minor(x[k], up[owner])
        if k > 0:
            base[...] += value
            low[...] += value_low
        elif first:
            base[...] = value
            low[...] = value_low
        else:
            base[...] = base_in[...] + value
            low[...] = low_in[...] + value_low


def block_products(index, table, blocks, output_weight, up_all, base=None, low=None, name=""):
    count = len(blocks)
    tokens, width = blocks[0].shape
    out_width = output_weight.shape[1]
    rank = up_all.shape[1]
    first = base is None
    return pl.pallas_call(
        functools.partial(block_kernel, table, first),
        in_specs=[SMEM] + [HBM] * count + [VMEM] * (2 if first else 4),
        out_specs=[VMEM] * 2,
        out_shape=[
            jax.ShapeDtypeStruct((tokens, out_width), jnp.float32),
            jax.ShapeDtypeStruct((tokens, rank), jnp.float32),
        ],
        scratch_shapes=[
            pltpu.VMEM((count, tokens, width), jnp.bfloat16),
            pltpu.SemaphoreType.DMA((count,)),
        ],
        compiler_params=pltpu.CompilerParams(vmem_limit_bytes=32 * 2**20),
        cost_estimate=pl.CostEstimate(
            flops=2 * count * tokens * width * out_width,
            bytes_accessed=2 * width * count * tokens,
            transcendentals=0,
        ),
        name=name,
    )(index, *blocks, output_weight, up_all, *([] if first else [base, low]))


def last_kernel(
    rows, table, index, far_a, far_b, other_a, other_b, weight, up, base, low, down, out, x,
    low_rounded, x_sem,
):
    half = far_a.shape[0]
    piece = 2 * half // rows
    tile = 2 * LANES
    copies = []
    for i, part in enumerate((far_a, far_b, other_a, other_b)):
        rows_of = pl.ds((i % 2) * half, half)
        copies.append(pltpu.make_async_copy(part, x.at[i // 2, rows_of], x_sem.at[i]))
    for copy in copies:
        copy.start()
    out[...] = jnp.zeros_like(out)
    for copy in copies:
        copy.wait()
    owners = [index[i] for i in table]
    total = low[...]
    for k, owner in enumerate(owners):
        total += dot_minor(x[k], up[owner])
    low_rounded[...] = total.astype(jnp.bfloat16)
    for n in range(weight.shape[1] // tile):
        span = slice(n * tile, (n + 1) * tile)
        total = base[:, span]
        for k, owner in enumerate(owners):
            total += dot_minor(x[k], weight[owner, span])
        total += adapter_scale * jnp.dot(
            low_rounded[...], down[:, span], preferred_element_type=jnp.float32
        )
        for row in range(rows):
            mine = total[row * piece : (row + 1) * piece]
            folded = jnp.concatenate([mine[:, :LANES], mine[:, LANES:]], axis=0)
            out[index[row], index[rows + row], :, n * LANES : (n + 1) * LANES] = folded.astype(
                jnp.bfloat16
            )


def last_products(rows, index, table, far, other, weight, up, base, low, down, groups, slots):
    half, width = far[0].shape
    tokens = 2 * half
    rank, out_width = down.shape
    piece = tokens // rows
    return pl.pallas_call(
        functools.partial(last_kernel, rows, table),
        in_specs=[SMEM] + [HBM] * 4 + [VMEM] * 5,
        out_specs=VMEM,
        scratch_shapes=[
            pltpu.VMEM((2, tokens, width), jnp.bfloat16),
            pltpu.VMEM((tokens, rank), jnp.bfloat16),
            pltpu.SemaphoreType.DMA((4,)),
        ],
        out_shape=jax.ShapeDtypeStruct(
            (groups, slots + 1, 2 * piece, out_width // 2), jnp.bfloat16
        ),
        compiler_params=pltpu.CompilerParams(vmem_limit_bytes=32 * 2**20),
        cost_estimate=pl.CostEstimate(
            flops=4 * tokens * width * out_width,
            bytes_accessed=4 * width * tokens + 8 * tokens * out_width,
            transcendentals=0,
        ),
        name="last_products",
    )(index, *far, *other, weight, up, base, low, down)


def send_kernel(groups, core_at, pick_at, index, share, other, out):
    half = share.shape[0]
    core = index[core_at]
    for group in range(groups):
        for kind in range(2):
            pick = index[pick_at + 2 * group + kind]
            lanes = pl.ds(pl.multiple_of(jnp.maximum(pick, 0) * ROW_TOKENS, ROW_TOKENS), ROW_TOKENS)
            keep = (pick >= 0).astype(jnp.float32)
            for owner, part in ((core, share), (1 - core, other)):
                value = part[:, lanes].astype(jnp.float32) * keep
                rows = pl.ds(pl.multiple_of(owner * half, half), half)
                out[group, kind, rows] = value.astype(jnp.bfloat16)


def rank_sums_to_send(index, core_at, pick_at, groups, share, other):
    rank = 2 * share.shape[0]
    return pl.pallas_call(
        functools.partial(send_kernel, groups, core_at, pick_at),
        in_specs=[SMEM, VMEM, VMEM],
        out_specs=VMEM,
        out_shape=jax.ShapeDtypeStruct((groups, 2, rank, ROW_TOKENS), jnp.bfloat16),
        compiler_params=pltpu.CompilerParams(vmem_limit_bytes=16 * 2**20),
        cost_estimate=pl.CostEstimate(
            flops=groups * rank * ROW_TOKENS, bytes_accessed=4 * groups * rank * ROW_TOKENS,
            transcendentals=0,
        ),
        name="rank_sums_to_send",
    )(index, share, other)


def gradient_kernel(
    source_at, dest_at, index, crossed, attention, gradient, out, low, projected, tokens, more, sem
):
    rank = crossed.shape[2]
    copies = [
        pltpu.make_async_copy(attention, tokens, sem.at[0]),
        pltpu.make_async_copy(gradient, more, sem.at[1]),
    ]
    for copy in copies:
        copy.start()
    for s in range(tokens.shape[0] // ROW_TOKENS):
        source = index[source_at + s]
        keep = (source >= 0).astype(jnp.float32)
        value = crossed[jnp.maximum(source, 0), 0].astype(jnp.float32) * keep
        low[:, s * ROW_TOKENS : (s + 1) * ROW_TOKENS] = value.astype(jnp.bfloat16)
    for r in range(more.shape[0] // ROW_TOKENS):
        projected[:, r * ROW_TOKENS : (r + 1) * ROW_TOKENS] = crossed[index[dest_at + r], 1]
    copies[0].wait()
    out[:rank] = jnp.dot(low[...], tokens[...], preferred_element_type=jnp.float32)
    copies[1].wait()
    out[rank:] = jnp.dot(projected[...], more[...], preferred_element_type=jnp.float32)


def gradient_products(index, source_at, dest_at, crossed, attention, gradient):
    rank = crossed.shape[2]
    slot_tokens, width = attention.shape
    row_tokens = gradient.shape[0]
    return pl.pallas_call(
        functools.partial(gradient_kernel, source_at, dest_at),
        in_specs=[SMEM, VMEM, HBM, HBM],
        out_specs=VMEM,
        out_shape=jax.ShapeDtypeStruct((2 * rank, width), jnp.float32),
        scratch_shapes=[
            pltpu.VMEM((rank, slot_tokens), jnp.bfloat16),
            pltpu.VMEM((rank, row_tokens), jnp.bfloat16),
            pltpu.VMEM(attention.shape, jnp.bfloat16),
            pltpu.VMEM(gradient.shape, jnp.bfloat16),
            pltpu.SemaphoreType.DMA((2,)),
        ],
        compiler_params=pltpu.CompilerParams(vmem_limit_bytes=16 * 2**20),
        cost_estimate=pl.CostEstimate(
            flops=2 * rank * width * (slot_tokens + row_tokens),
            bytes_accessed=2 * width * (slot_tokens + row_tokens),
            transcendentals=0,
        ),
        name="gradient_products",
    )(index, crossed, attention, gradient)


def unfold_kernel(slots, arrived, out, down_gradient, up_gradient):
    groups, _, folded, half_width = arrived.shape
    piece = folded // 2
    step = pl.program_id(0)

    @pl.when(step < slots)
    def _():
        for pair in range(groups // 2):
            halves = []
            for j in (2 * pair, 2 * pair + 1):
                value = arrived[j, 0].astype(jnp.float32)
                pieces = []
                for n in range(half_width // LANES):
                    lanes = slice(n * LANES, (n + 1) * LANES)
                    pieces += [value[:piece, lanes], value[piece:, lanes]]
                halves.append(jnp.concatenate(pieces, axis=1))
            out[pl.ds(pair * folded, folded), :] = jnp.concatenate(halves, axis=0).astype(out.dtype)

    @pl.when(step == slots)
    def _():
        values = []
        for j in range(groups):
            value = arrived[j, 0].astype(jnp.float32)
            values.append(jnp.concatenate([value[:piece], value[piece:]], axis=1))
        down_gradient[...] = jnp.concatenate(values[: groups // 2], axis=0)
        up_gradient[...] = jnp.concatenate(values[groups // 2 :], axis=0)


def unfold(arrived, slots):
    groups, _, folded, half_width = arrived.shape
    piece, width = folded // 2, 2 * half_width
    rank = groups * piece // 2
    return pl.pallas_call(
        functools.partial(unfold_kernel, slots),
        grid=(slots + 1,),
        in_specs=[pl.BlockSpec((groups, 1, folded, half_width), lambda s: (0, s, 0, 0))],
        out_specs=[
            pl.BlockSpec((groups * piece, width), lambda s: (jnp.minimum(s, slots - 1), 0)),
            pl.BlockSpec((rank, width), lambda s: (0, 0)),
            pl.BlockSpec((rank, width), lambda s: (0, 0)),
        ],
        out_shape=[
            jax.ShapeDtypeStruct((slots * groups * piece, width), jnp.bfloat16),
            jax.ShapeDtypeStruct((rank, width), jnp.float32),
            jax.ShapeDtypeStruct((rank, width), jnp.float32),
        ],
        compiler_params=pltpu.CompilerParams(vmem_limit_bytes=16 * 2**20),
        name="unfold",
    )(arrived)


def body(
    attention_slot_outputs,
    output_gradient_rows,
    output_weight,
    down_weight,
    up_weight,
    assign,
    counts,
):
    groups = counts.shape[0]
    rows = assign.shape[0]
    rows_here = output_gradient_rows.shape[0] // ROW_TOKENS
    slot_cap = attention_slot_outputs.shape[0] // ROW_TOKENS
    width_here = output_gradient_rows.shape[1]
    rank = up_weight.shape[0]
    tp = lax.axis_size("tp")
    piece = ROW_TOKENS // groups
    own_group = lax.axis_index("group")
    group_ids = jnp.arange(groups, dtype=jnp.int32)
    onehot = (assign[:, None] == group_ids[None, :]).astype(jnp.int32)
    before = jnp.cumsum(onehot, axis=0) - onehot
    order_in = jnp.sum(before * onehot, axis=1)
    free_slots = jnp.sum(onehot * counts[None, :], axis=1)
    position = slot_cap - free_slots + order_in
    own_dest = lax.dynamic_slice_in_dim(assign, own_group * rows_here, rows_here)
    scale_factor = adapter_scale / math.sqrt(rows * ROW_TOKENS)

    index = lax.axis_index("tp")
    chips = tp // 2
    y, core = index // 2, index % 2

    def move(value, n):
        pairs = [(2 * a + b, 2 * ((a + n) % chips) + b) for a in range(chips) for b in range(2)]
        return lax.ppermute(value, "tp", pairs)

    def swap(value):
        return lax.ppermute(value, "tp", [(i, i ^ 1) for i in range(tp)])

    spread = lax.all_to_all(
        output_gradient_rows.reshape(rows_here, groups, piece, width_here).transpose(1, 0, 2, 3),
        "group",
        split_axis=0,
        concat_axis=0,
        tiled=True,
    ).reshape(rows * piece, width_here)

    slot_ids = jnp.arange(slot_cap, dtype=jnp.int32)
    row_ids = jnp.arange(rows_here, dtype=jnp.int32)
    row_position = position.reshape(groups, rows_here)
    hit_row = assign.reshape(groups, rows_here) == own_group
    low_pick = jnp.max(jnp.where(own_dest[None, :] == group_ids[:, None], row_ids, -1), axis=1)
    projected_pick = jnp.max(jnp.where(hit_row, rows_here + row_position, -1), axis=1)
    slot_match = hit_row[:, :, None] & (row_position[:, :, None] == slot_ids)
    slot_source = jnp.max(jnp.where(slot_match, group_ids[:, None, None], -1), axis=(0, 1))
    owners = []
    for step in (0, chips - 1, 1, 2):
        pair = 2 * lax.rem(y + step, chips)
        owners += [pair + core, pair + 1 - core]
    pieces = [
        assign, position, jnp.stack([low_pick, projected_pick], axis=1).reshape(-1), slot_source,
        own_dest, jnp.stack(owners + [core]).astype(jnp.int32),
    ]
    at = [0]
    for part in pieces:
        at.append(at[-1] + part.shape[0])
    _, _, pick_at, source_at, dest_at, owner_at, end = at
    table = jnp.concatenate(pieces)

    up_all = lax.all_gather(up_weight, "tp", axis=0)
    low_part = dot_minor(up_weight, output_gradient_rows)
    projected_part = lax.dot_general(
        down_weight, attention_slot_outputs, (((0,), (1,)), ((), ())),
        preferred_element_type=jnp.float32,
    )
    parts = jnp.concatenate([low_part, projected_part], axis=1)
    parts = parts + swap(parts)
    share = lax.dynamic_slice_in_dim(parts, core * (rank // 2), rank // 2, axis=0)
    share = share + move(share, 1) + move(share, -1) + move(share, 2)
    share = share.astype(jnp.bfloat16)

    crossed = lax.all_to_all(
        rank_sums_to_send(table, end - 1, pick_at, groups, share, swap(share)),
        "group", split_axis=0, concat_axis=0, tiled=True,
    )

    weight = load_columns(output_weight, tp)
    spread, _ = lax.optimization_barrier((spread, share))
    left, right = move(spread, 1), move(spread, -1)
    left_top, right_bottom = take_halves(left, right)
    far = [move(left_top, 1), move(right_bottom, -1)]
    base, low_own = block_products(
        table, [owner_at, owner_at + 1], [spread, swap(spread)], weight, up_all,
        name="own_products",
    )
    swapped = [swap(left), swap(right)]
    crossed, _ = lax.optimization_barrier((crossed, (base, swapped)))
    base, low_own = block_products(
        table, [owner_at + i for i in range(2, 6)], [left, swapped[0], right, swapped[1]],
        weight, up_all, base, low_own, name="side_products",
    )
    grads = gradient_products(
        table, source_at, dest_at, crossed, attention_slot_outputs, output_gradient_rows
    )
    share_rows = 2 * rank // groups
    grads = lax.all_to_all(
        grads.reshape(groups, share_rows, width_here), "group", split_axis=0, concat_axis=0,
        tiled=True,
    )
    grads = (scale_factor * jnp.sum(grads, axis=0)).astype(jnp.bfloat16)
    placed = last_products(
        rows, table, [owner_at + 6, owner_at + 7], far, [swap(part) for part in far],
        weight, up_all, base, low_own, down_weight.T, groups, slot_cap,
    )

    folded = (2 * piece, width_here // 2)
    grads = jnp.concatenate([grads[:, : folded[1]], grads[:, folded[1] :]], axis=0)
    placed = placed.at[:, slot_cap].set(jnp.broadcast_to(grads, (groups,) + folded))
    arrived = lax.all_to_all(placed, "group", split_axis=0, concat_axis=0, tiled=True)
    attention_gradient, down_gradient, up_gradient = unfold(arrived, slot_cap)
    return attention_gradient, down_gradient.T, up_gradient


def solution(mesh):
    in_specs = (
        P("group", "tp"),
        P("group", "tp"),
        P("tp", None),
        P("tp", None),
        P(None, "tp"),
        P(),
        P(),
    )
    out_specs = (P("group", "tp"), P("tp", None), P(None, "tp"))
    return jax.shard_map(body, mesh=mesh, in_specs=in_specs, out_specs=out_specs, check_vma=False)
```

```python
import functools
import math

import jax
import jax.numpy as jnp
from jax import lax
from jax.experimental import pallas as pl
from jax.experimental.pallas import tpu as pltpu
from jax.sharding import PartitionSpec as P

ROW_TOKENS = 128
LANES = 128
VMEM_LIMIT = 56 * 2**20


adapter_scale = 2.0

HBM = pl.BlockSpec(memory_space=pltpu.HBM)
VMEM = pl.BlockSpec(memory_space=pltpu.VMEM)
SMEM = pl.BlockSpec(memory_space=pltpu.SMEM)


def dot_minor(left, right):
    return lax.dot_general(
        left, right, (((1,), (1,)), ((), ())), preferred_element_type=jnp.float32
    )


def halves_kernel(left, right, top, bottom):
    top[...] = left[...]
    bottom[...] = right[...]


def take_halves(left, right):
    tokens, width = left.shape
    half, lanes = tokens // 2, width // 2
    shape = jax.ShapeDtypeStruct((half, width), left.dtype)
    return pl.pallas_call(
        halves_kernel,
        grid=(width // lanes,),
        in_specs=[
            pl.BlockSpec((half, lanes), lambda i: (0, i)),
            pl.BlockSpec((half, lanes), lambda i: (1, i)),
        ],
        out_specs=[pl.BlockSpec((half, lanes), lambda i: (0, i))] * 2,
        out_shape=[shape] * 2,
        compiler_params=pltpu.CompilerParams(vmem_limit_bytes=VMEM_LIMIT),
        name="take_halves",
    )(left, right)


def block_kernel(table, first, index, *refs):
    refs = list(refs)
    count = len(table)
    blocks = [refs.pop(0) for _ in range(count)]
    weight, up = refs.pop(0), refs.pop(0)
    if not first:
        base_in, low_in = refs.pop(0), refs.pop(0)
    base, low, x, w, u, x_sem, w_sem, u_sem = refs[:8]
    width = x.shape[2]
    copies = []
    for k in range(count):
        owner = index[table[k]]
        columns = pl.ds(pl.multiple_of(owner * width, width), width)
        copies.append([
            pltpu.make_async_copy(blocks[k], x.at[k], x_sem.at[k]),
            pltpu.make_async_copy(weight.at[:, columns], w.at[k], w_sem.at[k]),
            pltpu.make_async_copy(up.at[owner], u.at[k], u_sem.at[k]),
        ])
    if not first:
        base_was, low_was, was_sem = refs[8:]
        copies.append([
            pltpu.make_async_copy(base_in, base_was, was_sem.at[0]),
            pltpu.make_async_copy(low_in, low_was, was_sem.at[1]),
        ])
    for each in copies[:2]:
        for copy in each:
            copy.start()
    for k in range(count):
        for copy in copies[k]:
            copy.wait()
        if k + 2 < len(copies):
            for copy in copies[k + 2]:
                copy.start()
        value, value_low = dot_minor(x[k], w[k]), dot_minor(x[k], u[k])
        if k == 0:
            base[...] = value
            low[...] = value_low
        else:
            base[...] += value
            low[...] += value_low
    if not first:
        for copy in copies[count]:
            copy.wait()
        base[...] += base_was[...]
        low[...] += low_was[...]


def block_products(index, table, blocks, weight, up_all, base=None, low=None, name=""):
    count = len(blocks)
    tokens, width = blocks[0].shape
    out_width = weight.shape[0]
    rank = up_all.shape[1]
    first = base is None
    out_shape = [
        jax.ShapeDtypeStruct((tokens, out_width), jnp.float32),
        jax.ShapeDtypeStruct((tokens, rank), jnp.float32),
    ]
    scratch = [
        pltpu.VMEM((count, tokens, width), jnp.bfloat16),
        pltpu.VMEM((count, out_width, width), jnp.bfloat16),
        pltpu.VMEM((count, rank, width), jnp.bfloat16),
        pltpu.SemaphoreType.DMA((count,)),
        pltpu.SemaphoreType.DMA((count,)),
        pltpu.SemaphoreType.DMA((count,)),
    ]
    if not first:
        scratch += [pltpu.VMEM(part.shape, part.dtype) for part in out_shape]
        scratch += [pltpu.SemaphoreType.DMA((2,))]
    return pl.pallas_call(
        functools.partial(block_kernel, table, first),
        in_specs=[SMEM] + [HBM] * (count + (2 if first else 4)),
        out_specs=[VMEM] * 2,
        out_shape=out_shape,
        scratch_shapes=scratch,
        compiler_params=pltpu.CompilerParams(vmem_limit_bytes=VMEM_LIMIT),
        cost_estimate=pl.CostEstimate(
            flops=2 * count * tokens * width * out_width,
            bytes_accessed=2 * width * count * (tokens + out_width),
            transcendentals=0,
        ),
        name=name,
    )(index, *blocks, weight, up_all, *([] if first else [base, low]))


def last_kernel(
    rows, table, index, far_a, far_b, other_a, other_b, weight, up, base_in, low_in, down, out, x,
    w, u, base, low, low_rounded, x_sem, w_sem, u_sem, was_sem,
):
    half, width = far_a.shape
    piece = 2 * half // rows
    tile = 2 * LANES
    tiles = w.shape[0] // tile
    copies = []
    for i, part in enumerate((far_a, far_b, other_a, other_b)):
        rows_of, lanes = pl.ds((i % 2) * half, half), pl.ds((i // 2) * width, width)
        copies.append(pltpu.make_async_copy(part, x.at[rows_of, lanes], x_sem.at[i]))
    for k in range(2):
        lanes = pl.ds(k * width, width)
        copies.append(pltpu.make_async_copy(up.at[index[table[k]]], u.at[:, lanes], u_sem.at[k]))
    copies.append(pltpu.make_async_copy(low_in, low, was_sem.at[tiles]))
    for copy in copies:
        copy.start()
    tile_copies = []
    for n in range(tiles):
        span = pl.ds(n * tile, tile)
        each = [pltpu.make_async_copy(base_in.at[:, span], base.at[:, span], was_sem.at[n])]
        for k in range(2):
            columns = pl.ds(pl.multiple_of(index[table[k]] * width, width), width)
            lanes = pl.ds(k * width, width)
            each.append(
                pltpu.make_async_copy(weight.at[span, columns], w.at[span, lanes], w_sem.at[n, k])
            )
        tile_copies.append(each)
    for each in tile_copies[:2]:
        for copy in each:
            copy.start()
    out[...] = jnp.zeros_like(out)
    for copy in copies:
        copy.wait()
    low_rounded[...] = (low[...] + dot_minor(x[...], u[...])).astype(jnp.bfloat16)
    for n in range(tiles):
        span = slice(n * tile, (n + 1) * tile)
        for copy in tile_copies[n]:
            copy.wait()
        if n + 2 < tiles:
            for copy in tile_copies[n + 2]:
                copy.start()
        total = base[:, span] + dot_minor(x[...], w[span])
        total += adapter_scale * jnp.dot(
            low_rounded[...], down[:, span], preferred_element_type=jnp.float32
        )
        for row in range(rows):
            mine = total[row * piece : (row + 1) * piece]
            folded = jnp.concatenate([mine[:, :LANES], mine[:, LANES:]], axis=0)
            out[index[row], index[rows + row], :, n * LANES : (n + 1) * LANES] = folded.astype(
                jnp.bfloat16
            )


def last_products(rows, index, table, far, other, weight, up, base, low, down, groups, slots):
    half, width = far[0].shape
    tokens = 2 * half
    rank, out_width = down.shape
    piece = tokens // rows
    tiles = out_width // (2 * LANES)
    return pl.pallas_call(
        functools.partial(last_kernel, rows, table),
        in_specs=[SMEM] + [HBM] * 8 + [VMEM],
        out_specs=VMEM,
        scratch_shapes=[
            pltpu.VMEM((tokens, 2 * width), jnp.bfloat16),
            pltpu.VMEM((out_width, 2 * width), jnp.bfloat16),
            pltpu.VMEM((rank, 2 * width), jnp.bfloat16),
            pltpu.VMEM((tokens, out_width), jnp.float32),
            pltpu.VMEM((tokens, rank), jnp.float32),
            pltpu.VMEM((tokens, rank), jnp.bfloat16),
            pltpu.SemaphoreType.DMA((4,)),
            pltpu.SemaphoreType.DMA((tiles, 2)),
            pltpu.SemaphoreType.DMA((2,)),
            pltpu.SemaphoreType.DMA((tiles + 1,)),
        ],
        out_shape=jax.ShapeDtypeStruct(
            (groups, slots + 1, 2 * piece, out_width // 2), jnp.bfloat16
        ),
        compiler_params=pltpu.CompilerParams(vmem_limit_bytes=VMEM_LIMIT),
        cost_estimate=pl.CostEstimate(
            flops=4 * tokens * width * out_width,
            bytes_accessed=4 * width * tokens + 8 * tokens * out_width,
            transcendentals=0,
        ),
        name="last_products",
    )(index, *far, *other, weight, up, base, low, down)


def send_kernel(groups, core_at, pick_at, index, share, other, out):
    half = share.shape[0]
    core = index[core_at]
    for group in range(groups):
        for kind in range(2):
            pick = index[pick_at + 2 * group + kind]
            lanes = pl.ds(pl.multiple_of(jnp.maximum(pick, 0) * ROW_TOKENS, ROW_TOKENS), ROW_TOKENS)
            keep = (pick >= 0).astype(jnp.float32)
            for owner, part in ((core, share), (1 - core, other)):
                value = part[:, lanes].astype(jnp.float32) * keep
                rows = pl.ds(pl.multiple_of(owner * half, half), half)
                out[group, kind, rows] = value.astype(jnp.bfloat16)


def rank_sums_to_send(index, core_at, pick_at, groups, share, other):
    rank = 2 * share.shape[0]
    return pl.pallas_call(
        functools.partial(send_kernel, groups, core_at, pick_at),
        in_specs=[SMEM, VMEM, VMEM],
        out_specs=VMEM,
        out_shape=jax.ShapeDtypeStruct((groups, 2, rank, ROW_TOKENS), jnp.bfloat16),
        compiler_params=pltpu.CompilerParams(vmem_limit_bytes=VMEM_LIMIT),
        cost_estimate=pl.CostEstimate(
            flops=groups * rank * ROW_TOKENS, bytes_accessed=4 * groups * rank * ROW_TOKENS,
            transcendentals=0,
        ),
        name="rank_sums_to_send",
    )(index, share, other)


def gradient_kernel(
    source_at, dest_at, index, crossed, attention, gradient, out, low, projected, tokens, more, sem
):
    rank = crossed.shape[2]
    copies = [
        pltpu.make_async_copy(attention, tokens, sem.at[0]),
        pltpu.make_async_copy(gradient, more, sem.at[1]),
    ]
    for copy in copies:
        copy.start()
    for s in range(tokens.shape[0] // ROW_TOKENS):
        source = index[source_at + s]
        keep = (source >= 0).astype(jnp.float32)
        value = crossed[jnp.maximum(source, 0), 0].astype(jnp.float32) * keep
        low[:, s * ROW_TOKENS : (s + 1) * ROW_TOKENS] = value.astype(jnp.bfloat16)
    for r in range(more.shape[0] // ROW_TOKENS):
        projected[:, r * ROW_TOKENS : (r + 1) * ROW_TOKENS] = crossed[index[dest_at + r], 1]
    copies[0].wait()
    out[:rank] = jnp.dot(low[...], tokens[...], preferred_element_type=jnp.float32)
    copies[1].wait()
    out[rank:] = jnp.dot(projected[...], more[...], preferred_element_type=jnp.float32)


def gradient_products(index, source_at, dest_at, crossed, attention, gradient):
    rank = crossed.shape[2]
    slot_tokens, width = attention.shape
    row_tokens = gradient.shape[0]
    return pl.pallas_call(
        functools.partial(gradient_kernel, source_at, dest_at),
        in_specs=[SMEM, VMEM, HBM, HBM],
        out_specs=VMEM,
        out_shape=jax.ShapeDtypeStruct((2 * rank, width), jnp.float32),
        scratch_shapes=[
            pltpu.VMEM((rank, slot_tokens), jnp.bfloat16),
            pltpu.VMEM((rank, row_tokens), jnp.bfloat16),
            pltpu.VMEM(attention.shape, jnp.bfloat16),
            pltpu.VMEM(gradient.shape, jnp.bfloat16),
            pltpu.SemaphoreType.DMA((2,)),
        ],
        compiler_params=pltpu.CompilerParams(vmem_limit_bytes=VMEM_LIMIT),
        cost_estimate=pl.CostEstimate(
            flops=2 * rank * width * (slot_tokens + row_tokens),
            bytes_accessed=2 * width * (slot_tokens + row_tokens),
            transcendentals=0,
        ),
        name="gradient_products",
    )(index, crossed, attention, gradient)


def unfold_kernel(slots, arrived, out, down_gradient, up_gradient):
    groups, _, folded, half_width = arrived.shape
    piece = folded // 2
    step = pl.program_id(0)

    @pl.when(step < slots)
    def _():
        for pair in range(groups // 2):
            halves = []
            for j in (2 * pair, 2 * pair + 1):
                value = arrived[j, 0].astype(jnp.float32)
                pieces = []
                for n in range(half_width // LANES):
                    lanes = slice(n * LANES, (n + 1) * LANES)
                    pieces += [value[:piece, lanes], value[piece:, lanes]]
                halves.append(jnp.concatenate(pieces, axis=1))
            out[pl.ds(pair * folded, folded), :] = jnp.concatenate(halves, axis=0).astype(out.dtype)

    @pl.when(step == slots)
    def _():
        values = []
        for j in range(groups):
            value = arrived[j, 0].astype(jnp.float32)
            values.append(jnp.concatenate([value[:piece], value[piece:]], axis=1))
        down_gradient[...] = jnp.concatenate(values[: groups // 2], axis=0)
        up_gradient[...] = jnp.concatenate(values[groups // 2 :], axis=0)


def unfold(arrived, slots):
    groups, _, folded, half_width = arrived.shape
    piece, width = folded // 2, 2 * half_width
    rank = groups * piece // 2
    return pl.pallas_call(
        functools.partial(unfold_kernel, slots),
        grid=(slots + 1,),
        in_specs=[pl.BlockSpec((groups, 1, folded, half_width), lambda s: (0, s, 0, 0))],
        out_specs=[
            pl.BlockSpec((groups * piece, width), lambda s: (jnp.minimum(s, slots - 1), 0)),
            pl.BlockSpec((rank, width), lambda s: (0, 0)),
            pl.BlockSpec((rank, width), lambda s: (0, 0)),
        ],
        out_shape=[
            jax.ShapeDtypeStruct((slots * groups * piece, width), jnp.bfloat16),
            jax.ShapeDtypeStruct((rank, width), jnp.float32),
            jax.ShapeDtypeStruct((rank, width), jnp.float32),
        ],
        compiler_params=pltpu.CompilerParams(vmem_limit_bytes=VMEM_LIMIT),
        name="unfold",
    )(arrived)


def body(
    attention_slot_outputs,
    output_gradient_rows,
    output_weight,
    down_weight,
    up_weight,
    assign,
    counts,
):
    groups = counts.shape[0]
    rows = assign.shape[0]
    rows_here = output_gradient_rows.shape[0] // ROW_TOKENS
    slot_cap = attention_slot_outputs.shape[0] // ROW_TOKENS
    width_here = output_gradient_rows.shape[1]
    rank = up_weight.shape[0]
    tp = lax.axis_size("tp")
    piece = ROW_TOKENS // groups
    own_group = lax.axis_index("group")
    group_ids = jnp.arange(groups, dtype=jnp.int32)
    onehot = (assign[:, None] == group_ids[None, :]).astype(jnp.int32)
    before = jnp.cumsum(onehot, axis=0) - onehot
    order_in = jnp.sum(before * onehot, axis=1)
    free_slots = jnp.sum(onehot * counts[None, :], axis=1)
    position = slot_cap - free_slots + order_in
    own_dest = lax.dynamic_slice_in_dim(assign, own_group * rows_here, rows_here)
    scale_factor = adapter_scale / math.sqrt(rows * ROW_TOKENS)

    index = lax.axis_index("tp")
    chips = tp // 2
    y, core = index // 2, index % 2

    def move(value, n):
        pairs = [(2 * a + b, 2 * ((a + n) % chips) + b) for a in range(chips) for b in range(2)]
        return lax.ppermute(value, "tp", pairs)

    def swap(value):
        return lax.ppermute(value, "tp", [(i, i ^ 1) for i in range(tp)])

    spread = lax.all_to_all(
        output_gradient_rows.reshape(rows_here, groups, piece, width_here).transpose(1, 0, 2, 3),
        "group",
        split_axis=0,
        concat_axis=0,
        tiled=True,
    ).reshape(rows * piece, width_here)

    slot_ids = jnp.arange(slot_cap, dtype=jnp.int32)
    row_ids = jnp.arange(rows_here, dtype=jnp.int32)
    row_position = position.reshape(groups, rows_here)
    hit_row = assign.reshape(groups, rows_here) == own_group
    low_pick = jnp.max(jnp.where(own_dest[None, :] == group_ids[:, None], row_ids, -1), axis=1)
    projected_pick = jnp.max(jnp.where(hit_row, rows_here + row_position, -1), axis=1)
    slot_match = hit_row[:, :, None] & (row_position[:, :, None] == slot_ids)
    slot_source = jnp.max(jnp.where(slot_match, group_ids[:, None, None], -1), axis=(0, 1))
    owners = []
    for step in (0, chips - 1, 1, 2):
        pair = 2 * lax.rem(y + step, chips)
        owners += [pair + core, pair + 1 - core]
    pieces = [
        assign, position, jnp.stack([low_pick, projected_pick], axis=1).reshape(-1), slot_source,
        own_dest, jnp.stack(owners + [core]).astype(jnp.int32),
    ]
    at = [0]
    for part in pieces:
        at.append(at[-1] + part.shape[0])
    _, _, pick_at, source_at, dest_at, owner_at, end = at
    table = jnp.concatenate(pieces)

    up_all = lax.all_gather(up_weight, "tp", axis=0)
    low_part = dot_minor(up_weight, output_gradient_rows)
    projected_part = lax.dot_general(
        down_weight, attention_slot_outputs, (((0,), (1,)), ((), ())),
        preferred_element_type=jnp.float32,
    )
    parts = jnp.concatenate([low_part, projected_part], axis=1)
    parts = parts + swap(parts)
    share = lax.dynamic_slice_in_dim(parts, core * (rank // 2), rank // 2, axis=0)
    share = share + move(share, 1) + move(share, -1) + move(share, 2)
    share = share.astype(jnp.bfloat16)

    crossed = lax.all_to_all(
        rank_sums_to_send(table, end - 1, pick_at, groups, share, swap(share)),
        "group", split_axis=0, concat_axis=0, tiled=True,
    )

    spread, _ = lax.optimization_barrier((spread, share))
    left, right = move(spread, 1), move(spread, -1)
    base, low_own = block_products(
        table, [owner_at, owner_at + 1], [spread, swap(spread)], output_weight, up_all,
        name="own_products",
    )
    left, right, _ = lax.optimization_barrier((left, right, (crossed, base)))
    left_top, right_bottom = take_halves(left, right)
    far = [move(left_top, 1), move(right_bottom, -1)]
    base, low_own = block_products(
        table, [owner_at + i for i in range(2, 6)], [left, swap(left), right, swap(right)],
        output_weight, up_all, base, low_own, name="side_products",
    )
    grads = gradient_products(
        table, source_at, dest_at, crossed, attention_slot_outputs, output_gradient_rows
    )
    share_rows = 2 * rank // groups
    grads = lax.all_to_all(
        grads.reshape(groups, share_rows, width_here), "group", split_axis=0, concat_axis=0,
        tiled=True,
    )
    grads = (scale_factor * jnp.sum(grads, axis=0)).astype(jnp.bfloat16)
    placed = last_products(
        rows, table, [owner_at + 6, owner_at + 7], far, [swap(part) for part in far],
        output_weight, up_all, base, low_own, down_weight.T, groups, slot_cap,
    )

    folded = (2 * piece, width_here // 2)
    grads = jnp.concatenate([grads[:, : folded[1]], grads[:, folded[1] :]], axis=0)
    placed = placed.at[:, slot_cap].set(jnp.broadcast_to(grads, (groups,) + folded))
    arrived = lax.all_to_all(placed, "group", split_axis=0, concat_axis=0, tiled=True)
    attention_gradient, down_gradient, up_gradient = unfold(arrived, slot_cap)
    return attention_gradient, down_gradient.T, up_gradient


def solution(mesh):
    in_specs = (
        P("group", "tp"),
        P("group", "tp"),
        P("tp", None),
        P("tp", None),
        P(None, "tp"),
        P(),
        P(),
    )
    out_specs = (P("group", "tp"), P("tp", None), P(None, "tp"))
    return jax.shard_map(body, mesh=mesh, in_specs=in_specs, out_specs=out_specs, check_vma=False)
```

```python
import functools
import math

import jax
import jax.numpy as jnp
from jax import lax
from jax.experimental import pallas as pl
from jax.experimental.pallas import tpu as pltpu
from jax.sharding import PartitionSpec as P

ROW_TOKENS = 128
LANES = 128
VMEM_LIMIT = 44 * 2**20
BASE_ROOM = 16
SMALL_LIMIT = 18 * 2**20


adapter_scale = 2.0

ANY = pl.BlockSpec(memory_space=pl.ANY)
HBM = pl.BlockSpec(memory_space=pltpu.HBM)
VMEM = pl.BlockSpec(memory_space=pltpu.VMEM)
SMEM = pl.BlockSpec(memory_space=pltpu.SMEM)


def dot_minor(left, right):
    return lax.dot_general(
        left, right, (((1,), (1,)), ((), ())), preferred_element_type=jnp.float32
    )


def halves_kernel(left, right, token, token_too, top, bottom, left_out, right_out, buffer, sem):
    half = top.shape[0]
    parts = ((left.at[pl.ds(0, half)], top), (right.at[pl.ds(half, half)], bottom))
    loads = [
        pltpu.make_async_copy(part, buffer.at[i], sem.at[i]) for i, (part, _) in enumerate(parts)
    ]
    stores = [
        pltpu.make_async_copy(buffer.at[i], out, sem.at[2 + i]) for i, (_, out) in enumerate(parts)
    ]
    for load in loads:
        load.start()
    for load, store in zip(loads, stores):
        load.wait()
        store.start()
    for store in stores:
        store.wait()


def take_halves(left, right, *tokens):
    half = jax.ShapeDtypeStruct((left.shape[0] // 2, left.shape[1]), left.dtype)
    return pl.pallas_call(
        halves_kernel,
        in_specs=[ANY] * 4,
        out_specs=[HBM] * 2 + [ANY] * 2,
        out_shape=[half] * 2 + [jax.ShapeDtypeStruct(left.shape, left.dtype)] * 2,
        input_output_aliases={0: 2, 1: 3},
        scratch_shapes=[
            pltpu.VMEM((2,) + half.shape, half.dtype),
            pltpu.SemaphoreType.DMA((4,)),
        ],
        compiler_params=pltpu.CompilerParams(vmem_limit_bytes=SMALL_LIMIT),
        cost_estimate=pl.CostEstimate(
            flops=0, bytes_accessed=8 * left.shape[0] * left.shape[1], transcendentals=0
        ),
        name="take_halves",
    )(left, right, *tokens)


def block_kernel(table, first, index, *refs):
    refs = list(refs)
    count = len(table)
    blocks = [refs.pop(0) for _ in range(count)]
    weight, up, _ = refs.pop(0), refs.pop(0), refs.pop(0)
    if not first:
        sums_in = refs.pop(0)
    sums_out, done, x, w, u, sums, sums_was, x_sem, w_sem, u_sem, sem = refs
    tokens, width = x.shape[1:]
    out_width, rank = w.shape[1], u.shape[1]
    done[...] = jnp.zeros_like(done)
    copies = []
    for k, place in enumerate(table):
        owner = index[place]
        columns = pl.ds(pl.multiple_of(owner * width, width), width)
        copies.append([
            pltpu.make_async_copy(blocks[k], x.at[k], x_sem.at[k]),
            pltpu.make_async_copy(weight.at[:, columns], w.at[k % 3], w_sem.at[k]),
            pltpu.make_async_copy(up.at[owner], u.at[k], u_sem.at[k]),
        ])
    if not first:
        copies.append([pltpu.make_async_copy(sums_in.at[pl.ds(0, tokens)], sums_was, sem.at[0])])
    for each in copies[:2]:
        for copy in each:
            copy.start()
    for k in range(count):
        for copy in copies[k]:
            copy.wait()
        if k + 2 < len(copies):
            for copy in copies[k + 2]:
                copy.start()
        value, value_low = dot_minor(x[k], w[k % 3]), dot_minor(x[k], u[k])
        if k > 0:
            sums[:, :out_width] += value
            sums[:, out_width : out_width + rank] += value_low
        else:
            sums[:, :out_width] = value
            sums[:, out_width : out_width + rank] = value_low
    if not first:
        copies[count][0].wait()
        sums[...] += sums_was[...]
    store = pltpu.make_async_copy(sums, sums_out.at[pl.ds(0, tokens)], sem.at[1])
    store.start()
    store.wait()


def block_products(index, table, blocks, weight, up_all, token, sums=None, name=""):
    count = len(blocks)
    tokens, width = blocks[0].shape
    out_width = weight.shape[0]
    rank = up_all.shape[1]
    first = sums is None
    return pl.pallas_call(
        functools.partial(block_kernel, table, first),
        in_specs=[SMEM] + [ANY] * (count + (3 if first else 4)),
        out_specs=[HBM, VMEM],
        out_shape=[
            jax.ShapeDtypeStruct((BASE_ROOM * tokens, out_width + LANES), jnp.float32),
            jax.ShapeDtypeStruct((8, LANES), jnp.float32),
        ],
        scratch_shapes=[
            pltpu.VMEM((count, tokens, width), jnp.bfloat16),
            pltpu.VMEM((3, out_width, width), jnp.bfloat16),
            pltpu.VMEM((count, rank, width), jnp.bfloat16),
            pltpu.VMEM((tokens, out_width + LANES), jnp.float32),
            pltpu.VMEM((tokens, out_width + LANES), jnp.float32),
            pltpu.SemaphoreType.DMA((count,)),
            pltpu.SemaphoreType.DMA((count,)),
            pltpu.SemaphoreType.DMA((count,)),
            pltpu.SemaphoreType.DMA((2,)),
        ],
        compiler_params=pltpu.CompilerParams(vmem_limit_bytes=VMEM_LIMIT),
        cost_estimate=pl.CostEstimate(
            flops=2 * count * tokens * width * out_width,
            bytes_accessed=2 * width * count * (tokens + out_width),
            transcendentals=0,
        ),
        name=name,
    )(index, *blocks, weight, up_all, token, *([] if first else [sums]))


def last_kernel(
    rows, scale, table, index, far_a, far_b, other_a, other_b, grads_in, weight, up, sums_in, down,
    out, x, w, u, sums, grads, low_rounded, x_sem, w_sem, u_sem, sem,
):
    half, width = far_a.shape
    out_width, rank = w.shape[0], u.shape[0]
    tokens = 2 * half
    piece = tokens // rows
    tile = 2 * LANES
    tiles = out_width // tile

    def load_sums(columns, semaphore):
        return pltpu.make_async_copy(
            sums_in.at[pl.ds(0, tokens), columns], sums.at[:, columns], semaphore
        )

    copies = []
    for i, part in enumerate((far_a, far_b, other_a, other_b)):
        rows_of, lanes = pl.ds((i % 2) * half, half), pl.ds((i // 2) * width, width)
        copies.append(pltpu.make_async_copy(part, x.at[rows_of, lanes], x_sem.at[i]))
    for k in range(2):
        lanes = pl.ds(k * width, width)
        copies.append(pltpu.make_async_copy(up.at[index[table[k]]], u.at[:, lanes], u_sem.at[k]))
    copies.append(load_sums(pl.ds(out_width, LANES), sem.at[tiles]))
    tile_copies = []
    for n in range(tiles):
        span = pl.ds(n * tile, tile)
        each = []
        for k in range(2):
            columns = pl.ds(pl.multiple_of(index[table[k]] * width, width), width)
            lanes = pl.ds(k * width, width)
            each.append(
                pltpu.make_async_copy(weight.at[span, columns], w.at[span, lanes], w_sem.at[n, k])
            )
        each.append(load_sums(span, sem.at[n]))
        tile_copies.append(each)
    load_grads = pltpu.make_async_copy(grads_in, grads, sem.at[tiles + 1])
    for each in [copies] + tile_copies + [[load_grads]]:
        for copy in each:
            copy.start()
    out[...] = jnp.zeros_like(out)
    for copy in copies:
        copy.wait()
    total = sums[:, out_width : out_width + rank] + dot_minor(x[...], u[...])
    low_rounded[...] = total.astype(jnp.bfloat16)
    for n in range(tiles):
        span = slice(n * tile, (n + 1) * tile)
        for copy in tile_copies[n]:
            copy.wait()
        total = sums[:, span] + dot_minor(x[...], w[span])
        total += adapter_scale * jnp.dot(
            low_rounded[...], down[:, span], preferred_element_type=jnp.float32
        )
        for row in range(rows):
            mine = total[row * piece : (row + 1) * piece]
            folded = jnp.concatenate([mine[:, :LANES], mine[:, LANES:]], axis=0)
            out[index[row], index[rows + row], :, n * LANES : (n + 1) * LANES] = folded.astype(
                jnp.bfloat16
            )
    load_grads.wait()
    total = scale * jnp.sum(grads[...], axis=0)
    folded = jnp.concatenate([total[:, : width // 2], total[:, width // 2 :]], axis=0)
    folded = folded.astype(jnp.bfloat16)
    for group in range(out.shape[0]):
        out[group, out.shape[1] - 1] = folded


def last_products(
    rows, scale, index, table, far, other, grads, weight, up, sums, down, groups, slots
):
    half, width = far[0].shape
    tokens = 2 * half
    rank, out_width = down.shape
    piece = tokens // rows
    tiles = out_width // (2 * LANES)
    return pl.pallas_call(
        functools.partial(last_kernel, rows, scale, table),
        in_specs=[SMEM] + [ANY] * 8 + [VMEM],
        out_specs=VMEM,
        scratch_shapes=[
            pltpu.VMEM((tokens, 2 * width), jnp.bfloat16),
            pltpu.VMEM((out_width, 2 * width), jnp.bfloat16),
            pltpu.VMEM((rank, 2 * width), jnp.bfloat16),
            pltpu.VMEM((tokens, out_width + LANES), jnp.float32),
            pltpu.VMEM(grads.shape, grads.dtype),
            pltpu.VMEM((tokens, rank), jnp.bfloat16),
            pltpu.SemaphoreType.DMA((4,)),
            pltpu.SemaphoreType.DMA((tiles, 2)),
            pltpu.SemaphoreType.DMA((2,)),
            pltpu.SemaphoreType.DMA((tiles + 2,)),
        ],
        out_shape=jax.ShapeDtypeStruct(
            (groups, slots + 1, 2 * piece, out_width // 2), jnp.bfloat16
        ),
        compiler_params=pltpu.CompilerParams(vmem_limit_bytes=VMEM_LIMIT),
        cost_estimate=pl.CostEstimate(
            flops=4 * tokens * width * out_width,
            bytes_accessed=4 * width * tokens + 8 * tokens * out_width,
            transcendentals=0,
        ),
        name="last_products",
    )(index, *far, *other, grads, weight, up, sums, down)


def send_kernel(groups, pick_at, index, share, out):
    for group in range(groups):
        for kind in range(2):
            pick = index[pick_at + 2 * group + kind]
            lanes = pl.ds(pl.multiple_of(jnp.maximum(pick, 0) * ROW_TOKENS, ROW_TOKENS), ROW_TOKENS)
            keep = (pick >= 0).astype(jnp.float32)
            out[group, kind] = (share[:, lanes] * keep).astype(jnp.bfloat16)


def rank_sums_to_send(index, pick_at, groups, share):
    half = share.shape[0]
    return pl.pallas_call(
        functools.partial(send_kernel, groups, pick_at),
        in_specs=[SMEM, VMEM],
        out_specs=VMEM,
        out_shape=jax.ShapeDtypeStruct((groups, 2, half, ROW_TOKENS), jnp.bfloat16),
        compiler_params=pltpu.CompilerParams(vmem_limit_bytes=SMALL_LIMIT),
        cost_estimate=pl.CostEstimate(
            flops=2 * groups * half * ROW_TOKENS, bytes_accessed=8 * groups * half * ROW_TOKENS,
            transcendentals=0,
        ),
        name="rank_sums_to_send",
    )(index, share)


def gradient_kernel(
    core_at, source_at, dest_at, index, crossed, crossed_other, token, attention, gradient, out,
    low, projected, tokens, more, sem,
):
    half = crossed.shape[2]
    rank = 2 * half
    core = index[core_at]
    halves = [
        (pl.ds(pl.multiple_of(owner * half, half), half), part)
        for owner, part in ((core, crossed), (1 - core, crossed_other))
    ]
    copies = [
        pltpu.make_async_copy(attention, tokens, sem.at[0]),
        pltpu.make_async_copy(gradient, more, sem.at[1]),
    ]
    for copy in copies:
        copy.start()
    for s in range(tokens.shape[0] // ROW_TOKENS):
        source = index[source_at + s]
        keep = (source >= 0).astype(jnp.float32)
        for ranks, part in halves:
            value = part[jnp.maximum(source, 0), 0].astype(jnp.float32) * keep
            low[ranks, s * ROW_TOKENS : (s + 1) * ROW_TOKENS] = value.astype(jnp.bfloat16)
    for r in range(more.shape[0] // ROW_TOKENS):
        for ranks, part in halves:
            projected[ranks, r * ROW_TOKENS : (r + 1) * ROW_TOKENS] = part[index[dest_at + r], 1]
    copies[0].wait()
    out[:rank] = jnp.dot(low[...], tokens[...], preferred_element_type=jnp.float32)
    copies[1].wait()
    out[rank:] = jnp.dot(projected[...], more[...], preferred_element_type=jnp.float32)


def gradient_products(
    index, core_at, source_at, dest_at, crossed, other, token, attention, gradient
):
    rank = 2 * crossed.shape[2]
    slot_tokens, width = attention.shape
    row_tokens = gradient.shape[0]
    return pl.pallas_call(
        functools.partial(gradient_kernel, core_at, source_at, dest_at),
        in_specs=[SMEM, VMEM, VMEM, ANY, ANY, ANY],
        out_specs=VMEM,
        out_shape=jax.ShapeDtypeStruct((2 * rank, width), jnp.float32),
        scratch_shapes=[
            pltpu.VMEM((rank, slot_tokens), jnp.bfloat16),
            pltpu.VMEM((rank, row_tokens), jnp.bfloat16),
            pltpu.VMEM(attention.shape, jnp.bfloat16),
            pltpu.VMEM(gradient.shape, jnp.bfloat16),
            pltpu.SemaphoreType.DMA((2,)),
        ],
        compiler_params=pltpu.CompilerParams(vmem_limit_bytes=SMALL_LIMIT),
        cost_estimate=pl.CostEstimate(
            flops=2 * rank * width * (slot_tokens + row_tokens),
            bytes_accessed=2 * width * (slot_tokens + row_tokens),
            transcendentals=0,
        ),
        name="gradient_products",
    )(index, crossed, other, token, attention, gradient)


def unfold_kernel(slots, arrived, out, down_gradient, up_gradient):
    groups, _, folded, half_width = arrived.shape
    piece = folded // 2
    step = pl.program_id(0)

    @pl.when(step < slots)
    def _():
        for pair in range(groups // 2):
            halves = []
            for j in (2 * pair, 2 * pair + 1):
                value = arrived[j, 0].astype(jnp.float32)
                pieces = []
                for n in range(half_width // LANES):
                    lanes = slice(n * LANES, (n + 1) * LANES)
                    pieces += [value[:piece, lanes], value[piece:, lanes]]
                halves.append(jnp.concatenate(pieces, axis=1))
            out[pl.ds(pair * folded, folded), :] = jnp.concatenate(halves, axis=0).astype(out.dtype)

    @pl.when(step == slots)
    def _():
        values = []
        for j in range(groups):
            value = arrived[j, 0].astype(jnp.float32)
            values.append(jnp.concatenate([value[:piece], value[piece:]], axis=1))
        down_gradient[...] = jnp.concatenate(values[: groups // 2], axis=0)
        up_gradient[...] = jnp.concatenate(values[groups // 2 :], axis=0)


def unfold(arrived, slots):
    groups, _, folded, half_width = arrived.shape
    piece, width = folded // 2, 2 * half_width
    rank = groups * piece // 2
    return pl.pallas_call(
        functools.partial(unfold_kernel, slots),
        grid=(slots + 1,),
        in_specs=[pl.BlockSpec((groups, 1, folded, half_width), lambda s: (0, s, 0, 0))],
        out_specs=[
            pl.BlockSpec((groups * piece, width), lambda s: (jnp.minimum(s, slots - 1), 0)),
            pl.BlockSpec((rank, width), lambda s: (0, 0)),
            pl.BlockSpec((rank, width), lambda s: (0, 0)),
        ],
        out_shape=[
            jax.ShapeDtypeStruct((slots * groups * piece, width), jnp.bfloat16),
            jax.ShapeDtypeStruct((rank, width), jnp.float32),
            jax.ShapeDtypeStruct((rank, width), jnp.float32),
        ],
        compiler_params=pltpu.CompilerParams(vmem_limit_bytes=SMALL_LIMIT),
        name="unfold",
    )(arrived)


def body(
    attention_slot_outputs,
    output_gradient_rows,
    output_weight,
    down_weight,
    up_weight,
    assign,
    counts,
):
    groups = counts.shape[0]
    rows = assign.shape[0]
    rows_here = output_gradient_rows.shape[0] // ROW_TOKENS
    slot_cap = attention_slot_outputs.shape[0] // ROW_TOKENS
    width_here = output_gradient_rows.shape[1]
    rank = up_weight.shape[0]
    tp = lax.axis_size("tp")
    piece = ROW_TOKENS // groups
    own_group = lax.axis_index("group")
    group_ids = jnp.arange(groups, dtype=jnp.int32)
    onehot = (assign[:, None] == group_ids[None, :]).astype(jnp.int32)
    before = jnp.cumsum(onehot, axis=0) - onehot
    order_in = jnp.sum(before * onehot, axis=1)
    free_slots = jnp.sum(onehot * counts[None, :], axis=1)
    position = slot_cap - free_slots + order_in
    own_dest = lax.dynamic_slice_in_dim(assign, own_group * rows_here, rows_here)
    scale_factor = adapter_scale / math.sqrt(rows * ROW_TOKENS)

    index = lax.axis_index("tp")
    chips = tp // 2
    y, core = index // 2, index % 2

    def move(value, n):
        pairs = [(2 * a + b, 2 * ((a + n) % chips) + b) for a in range(chips) for b in range(2)]
        return lax.ppermute(value, "tp", pairs)

    def swap(value):
        return lax.ppermute(value, "tp", [(i, i ^ 1) for i in range(tp)])

    pieces_out = output_gradient_rows.reshape(rows_here, groups, piece, width_here)
    pieces_out = pieces_out.transpose(1, 0, 2, 3)
    pieces_out, up_weight, down_weight_first = lax.optimization_barrier(
        (pieces_out, up_weight, down_weight)
    )
    spread = lax.all_to_all(
        pieces_out,
        "group",
        split_axis=0,
        concat_axis=0,
        tiled=True,
    ).reshape(rows * piece, width_here)

    slot_ids = jnp.arange(slot_cap, dtype=jnp.int32)
    row_ids = jnp.arange(rows_here, dtype=jnp.int32)
    row_position = position.reshape(groups, rows_here)
    hit_row = assign.reshape(groups, rows_here) == own_group
    low_pick = jnp.max(jnp.where(own_dest[None, :] == group_ids[:, None], row_ids, -1), axis=1)
    projected_pick = jnp.max(jnp.where(hit_row, rows_here + row_position, -1), axis=1)
    slot_match = hit_row[:, :, None] & (row_position[:, :, None] == slot_ids)
    slot_source = jnp.max(jnp.where(slot_match, group_ids[:, None, None], -1), axis=(0, 1))
    owners = []
    for step in (0, chips - 1, 1, 2):
        pair = 2 * lax.rem(y + step, chips)
        owners += [pair + core, pair + 1 - core]
    pieces = [
        assign, position, jnp.stack([low_pick, projected_pick], axis=1).reshape(-1), slot_source,
        own_dest, jnp.stack(owners + [core]).astype(jnp.int32),
    ]
    at = [0]
    for part in pieces:
        at.append(at[-1] + part.shape[0])
    _, _, pick_at, source_at, dest_at, owner_at, end = at
    table = jnp.concatenate(pieces)

    up_all = lax.all_gather(up_weight, "tp", axis=0)
    low_part = dot_minor(up_weight, output_gradient_rows)
    projected_part = lax.dot_general(
        down_weight_first, attention_slot_outputs, (((0,), (1,)), ((), ())),
        preferred_element_type=jnp.float32,
    )
    parts = jnp.concatenate([low_part, projected_part], axis=1)
    parts = parts + swap(parts)
    share = lax.dynamic_slice_in_dim(parts, core * (rank // 2), rank // 2, axis=0)
    share = share + move(share, 1) + move(share, -1) + move(share, 2)

    send = rank_sums_to_send(table, pick_at, groups, share)
    crossed = lax.all_to_all(send, "group", split_axis=0, concat_axis=0, tiled=True)

    spread, _ = lax.optimization_barrier((spread, share))
    left, right = move(spread, 1), move(spread, -1)
    other = swap(spread)
    sums, done = block_products(
        table, [owner_at, owner_at + 1], [spread, other], output_weight, up_all, send,
        name="own_products",
    )
    crossed_other = swap(crossed)
    left_top, right_bottom, left, right = take_halves(left, right, crossed, done)
    far = [move(left_top, 1), move(right_bottom, -1)]
    partial_grads = gradient_products(
        table, end - 1, source_at, dest_at, crossed, crossed_other, left_top, attention_slot_outputs,
        output_gradient_rows,
    )
    share_rows = 2 * rank // groups
    grads = lax.all_to_all(
        partial_grads.reshape(groups, share_rows, width_here), "group", split_axis=0, concat_axis=0,
        tiled=True,
    )
    sums, _ = block_products(
        table, [owner_at + i for i in range(2, 6)], [left, swap(left), right, swap(right)],
        output_weight, up_all, partial_grads, sums, name="side_products",
    )
    placed = last_products(
        rows, scale_factor, table, [owner_at + 6, owner_at + 7], far, [swap(part) for part in far],
        grads, output_weight, up_all, sums, down_weight.T, groups, slot_cap,
    )

    arrived = lax.all_to_all(placed, "group", split_axis=0, concat_axis=0, tiled=True)
    attention_gradient, down_gradient, up_gradient = unfold(arrived, slot_cap)
    return attention_gradient, down_gradient.T, up_gradient


def solution(mesh):
    in_specs = (
        P("group", "tp"),
        P("group", "tp"),
        P("tp", None),
        P("tp", None),
        P(None, "tp"),
        P(),
        P(),
    )
    out_specs = (P("group", "tp"), P("tp", None), P(None, "tp"))
    return jax.shard_map(body, mesh=mesh, in_specs=in_specs, out_specs=out_specs, check_vma=False)
```

```python
import functools
import math

import jax
import jax.numpy as jnp
from jax import lax
from jax.experimental import pallas as pl
from jax.experimental.pallas import tpu as pltpu
from jax.sharding import PartitionSpec as P

ROW_TOKENS = 128
LANES = 128
VMEM_LIMIT = 44 * 2**20
BASE_ROOM = 16
SMALL_LIMIT = 18 * 2**20


adapter_scale = 2.0

ANY = pl.BlockSpec(memory_space=pl.ANY)
HBM = pl.BlockSpec(memory_space=pltpu.HBM)
VMEM = pl.BlockSpec(memory_space=pltpu.VMEM)
SMEM = pl.BlockSpec(memory_space=pltpu.SMEM)


def dot_minor(left, right):
    return lax.dot_general(
        left, right, (((1,), (1,)), ((), ())), preferred_element_type=jnp.float32
    )


def halves_kernel(left, right, token, token_too, top, bottom, left_out, right_out, buffer, sem):
    half = top.shape[0]
    parts = ((left.at[pl.ds(0, half)], top), (right.at[pl.ds(half, half)], bottom))
    loads = [
        pltpu.make_async_copy(part, buffer.at[i], sem.at[i]) for i, (part, _) in enumerate(parts)
    ]
    stores = [
        pltpu.make_async_copy(buffer.at[i], out, sem.at[2 + i]) for i, (_, out) in enumerate(parts)
    ]
    for load in loads:
        load.start()
    for load, store in zip(loads, stores):
        load.wait()
        store.start()
    for store in stores:
        store.wait()


def take_halves(left, right, *tokens):
    half = jax.ShapeDtypeStruct((left.shape[0] // 2, left.shape[1]), left.dtype)
    return pl.pallas_call(
        halves_kernel,
        in_specs=[ANY] * 4,
        out_specs=[HBM] * 2 + [ANY] * 2,
        out_shape=[half] * 2 + [jax.ShapeDtypeStruct(left.shape, left.dtype)] * 2,
        input_output_aliases={0: 2, 1: 3},
        scratch_shapes=[
            pltpu.VMEM((2,) + half.shape, half.dtype),
            pltpu.SemaphoreType.DMA((4,)),
        ],
        compiler_params=pltpu.CompilerParams(vmem_limit_bytes=SMALL_LIMIT),
        cost_estimate=pl.CostEstimate(
            flops=0, bytes_accessed=8 * left.shape[0] * left.shape[1], transcendentals=0
        ),
        name="take_halves",
    )(left, right, *tokens)


def block_kernel(table, first, index, *refs):
    refs = list(refs)
    count = len(table)
    blocks = [refs.pop(0) for _ in range(count)]
    weight, _ = refs.pop(0), refs.pop(0)
    if not first:
        sums_in = refs.pop(0)
    sums_out, done, x, w, sums, sums_was, x_sem, w_sem, sem = refs
    tokens, width = x.shape[1:]
    done[...] = jnp.zeros_like(done)
    copies = []
    for k, place in enumerate(table):
        owner = index[place]
        columns = pl.ds(pl.multiple_of(owner * width, width), width)
        copies.append([
            pltpu.make_async_copy(blocks[k], x.at[k], x_sem.at[k]),
            pltpu.make_async_copy(weight.at[:, columns], w.at[k % 4], w_sem.at[k]),
        ])
    if not first:
        copies.append([pltpu.make_async_copy(sums_in.at[pl.ds(0, tokens)], sums_was, sem.at[0])])
    for each in copies[:3]:
        for copy in each:
            copy.start()
    for k in range(count):
        for copy in copies[k]:
            copy.wait()
        if k + 3 < len(copies):
            for copy in copies[k + 3]:
                copy.start()
        value = dot_minor(x[k], w[k % 4])
        if k > 0:
            sums[...] += value
        else:
            sums[...] = value
    if not first:
        copies[count][0].wait()
        sums[...] += sums_was[...]
    store = pltpu.make_async_copy(sums, sums_out.at[pl.ds(0, tokens)], sem.at[1])
    store.start()
    store.wait()


def block_products(index, table, blocks, weight, token, sums=None, name=""):
    count = len(blocks)
    tokens, width = blocks[0].shape
    out_width = weight.shape[0]
    first = sums is None
    return pl.pallas_call(
        functools.partial(block_kernel, table, first),
        in_specs=[SMEM] + [ANY] * (count + (2 if first else 3)),
        out_specs=[HBM, VMEM],
        out_shape=[
            jax.ShapeDtypeStruct((BASE_ROOM * tokens, out_width), jnp.float32),
            jax.ShapeDtypeStruct((8, LANES), jnp.float32),
        ],
        scratch_shapes=[
            pltpu.VMEM((count, tokens, width), jnp.bfloat16),
            pltpu.VMEM((4, out_width, width), jnp.bfloat16),
            pltpu.VMEM((tokens, out_width), jnp.float32),
            pltpu.VMEM((tokens, out_width), jnp.float32),
            pltpu.SemaphoreType.DMA((count,)),
            pltpu.SemaphoreType.DMA((count,)),
            pltpu.SemaphoreType.DMA((2,)),
        ],
        compiler_params=pltpu.CompilerParams(vmem_limit_bytes=VMEM_LIMIT),
        cost_estimate=pl.CostEstimate(
            flops=2 * count * tokens * width * out_width,
            bytes_accessed=2 * width * count * (tokens + out_width),
            transcendentals=0,
        ),
        name=name,
    )(index, *blocks, weight, token, *([] if first else [sums]))


def last_kernel(
    rows, scale, table, core_at, index, far_a, far_b, other_a, other_b, grads_in, crossed,
    crossed_other, weight, sums_in, down, out, x, w, sums, grads, pieces, low, low_rounded, x_sem,
    w_sem, sem,
):
    half, width = far_a.shape
    groups, ranks = pieces.shape[1:3]
    tokens = 2 * half
    piece = tokens // rows
    tile = 2 * LANES
    tiles = w.shape[0] // tile
    core = index[core_at]

    def load_sums(columns, semaphore):
        return pltpu.make_async_copy(
            sums_in.at[pl.ds(0, tokens), columns], sums.at[:, columns], semaphore
        )

    copies = []
    for i, part in enumerate((far_a, far_b, other_a, other_b)):
        rows_of, lanes = pl.ds((i % 2) * half, half), pl.ds((i // 2) * width, width)
        copies.append(pltpu.make_async_copy(part, x.at[rows_of, lanes], x_sem.at[i]))
    low_copies = [
        pltpu.make_async_copy(crossed.at[:, 2], pieces.at[core], sem.at[tiles]),
        pltpu.make_async_copy(crossed_other.at[:, 2], pieces.at[1 - core], sem.at[tiles + 1]),
    ]
    tile_copies = []
    for n in range(tiles):
        span = pl.ds(n * tile, tile)
        each = []
        for k in range(2):
            columns = pl.ds(pl.multiple_of(index[table[k]] * width, width), width)
            lanes = pl.ds(k * width, width)
            each.append(
                pltpu.make_async_copy(weight.at[span, columns], w.at[span, lanes], w_sem.at[n, k])
            )
        each.append(load_sums(span, sem.at[n]))
        tile_copies.append(each)
    load_grads = pltpu.make_async_copy(grads_in, grads, sem.at[tiles + 2])
    for each in [low_copies, copies] + tile_copies + [[load_grads]]:
        for copy in each:
            copy.start()
    out[...] = jnp.zeros_like(out)
    for copy in low_copies:
        copy.wait()
    share = tokens // groups
    for group in range(groups):
        both = jnp.concatenate([pieces[0, group], pieces[1, group]], axis=0).astype(jnp.float32)
        low[group * share : (group + 1) * share] = both.T[:share]
    low_rounded[...] = low[...].astype(jnp.bfloat16)
    for copy in copies:
        copy.wait()
    for n in range(tiles):
        span = slice(n * tile, (n + 1) * tile)
        for copy in tile_copies[n]:
            copy.wait()
        total = sums[:, span] + dot_minor(x[...], w[span])
        total += adapter_scale * jnp.dot(
            low_rounded[...], down[:, span], preferred_element_type=jnp.float32
        )
        for row in range(rows):
            mine = total[row * piece : (row + 1) * piece]
            folded = jnp.concatenate([mine[:, :LANES], mine[:, LANES:]], axis=0)
            out[index[row], index[rows + row], :, n * LANES : (n + 1) * LANES] = folded.astype(
                jnp.bfloat16
            )
    load_grads.wait()
    total = scale * jnp.sum(grads[...], axis=0)
    folded = jnp.concatenate([total[:, : width // 2], total[:, width // 2 :]], axis=0)
    folded = folded.astype(jnp.bfloat16)
    for group in range(out.shape[0]):
        out[group, out.shape[1] - 1] = folded


def last_products(
    rows, scale, index, table, core_at, far, other, grads, crossed, weight, sums, down, slots
):
    half, width = far[0].shape
    tokens = 2 * half
    rank, out_width = down.shape
    groups = crossed[0].shape[0]
    piece = tokens // rows
    tiles = out_width // (2 * LANES)
    return pl.pallas_call(
        functools.partial(last_kernel, rows, scale, table, core_at),
        in_specs=[SMEM] + [ANY] * 9 + [VMEM],
        out_specs=VMEM,
        scratch_shapes=[
            pltpu.VMEM((tokens, 2 * width), jnp.bfloat16),
            pltpu.VMEM((out_width, 2 * width), jnp.bfloat16),
            pltpu.VMEM((tokens, out_width), jnp.float32),
            pltpu.VMEM(grads.shape, grads.dtype),
            pltpu.VMEM((2, groups, rank // 2, LANES), jnp.bfloat16),
            pltpu.VMEM((tokens, rank), jnp.float32),
            pltpu.VMEM((tokens, rank), jnp.bfloat16),
            pltpu.SemaphoreType.DMA((4,)),
            pltpu.SemaphoreType.DMA((tiles, 2)),
            pltpu.SemaphoreType.DMA((tiles + 3,)),
        ],
        out_shape=jax.ShapeDtypeStruct(
            (groups, slots + 1, 2 * piece, out_width // 2), jnp.bfloat16
        ),
        compiler_params=pltpu.CompilerParams(vmem_limit_bytes=VMEM_LIMIT),
        cost_estimate=pl.CostEstimate(
            flops=4 * tokens * width * out_width,
            bytes_accessed=4 * width * tokens + 8 * tokens * out_width,
            transcendentals=0,
        ),
        name="last_products",
    )(index, *far, *other, grads, *crossed, weight, sums, down)


def send_kernel(groups, rows_here, pick_at, index, share, out):
    piece = ROW_TOKENS // groups
    lane = lax.broadcasted_iota(jnp.int32, (share.shape[0], ROW_TOKENS), 1)
    for group in range(groups):
        for kind in range(2):
            pick = index[pick_at + 2 * group + kind]
            lanes = pl.ds(pl.multiple_of(jnp.maximum(pick, 0) * ROW_TOKENS, ROW_TOKENS), ROW_TOKENS)
            keep = (pick >= 0).astype(jnp.float32)
            out[group, kind] = (share[:, lanes] * keep).astype(jnp.bfloat16)
        value = jnp.zeros(lane.shape, jnp.float32)
        for r in range(rows_here):
            shift = (r - group) * piece % ROW_TOKENS
            row = share[:, r * ROW_TOKENS : (r + 1) * ROW_TOKENS]
            if shift:
                row = pltpu.roll(row, shift, 1)
            value = jnp.where(lane // piece == r, row, value)
        out[group, 2] = value.astype(jnp.bfloat16)


def rank_sums_to_send(index, pick_at, groups, rows_here, share):
    half = share.shape[0]
    return pl.pallas_call(
        functools.partial(send_kernel, groups, rows_here, pick_at),
        in_specs=[SMEM, VMEM],
        out_specs=VMEM,
        out_shape=jax.ShapeDtypeStruct((groups, 3, half, ROW_TOKENS), jnp.bfloat16),
        compiler_params=pltpu.CompilerParams(vmem_limit_bytes=SMALL_LIMIT),
        cost_estimate=pl.CostEstimate(
            flops=2 * groups * half * ROW_TOKENS, bytes_accessed=8 * groups * half * ROW_TOKENS,
            transcendentals=0,
        ),
        name="rank_sums_to_send",
    )(index, share)


def gradient_kernel(
    core_at, source_at, dest_at, index, crossed, crossed_other, token, attention, gradient, out,
    done, parts, low, projected, sums, tokens, more, sem,
):
    half = crossed.shape[2]
    rank = 2 * half
    core = index[core_at]
    part_copies = [
        pltpu.make_async_copy(part.at[:, pl.ds(0, 2)], parts.at[i], sem.at[3 + i])
        for i, part in enumerate((crossed, crossed_other))
    ]
    copies = [
        pltpu.make_async_copy(attention, tokens, sem.at[0]),
        pltpu.make_async_copy(gradient, more, sem.at[1]),
    ]
    for copy in part_copies + copies:
        copy.start()
    for copy in part_copies:
        copy.wait()
    halves = [
        (pl.ds(pl.multiple_of(owner * half, half), half), parts.at[i])
        for i, owner in enumerate((core, 1 - core))
    ]
    for s in range(tokens.shape[0] // ROW_TOKENS):
        source = index[source_at + s]
        keep = (source >= 0).astype(jnp.float32)
        for ranks, part in halves:
            value = part[jnp.maximum(source, 0), 0].astype(jnp.float32) * keep
            low[ranks, s * ROW_TOKENS : (s + 1) * ROW_TOKENS] = value.astype(jnp.bfloat16)
    for r in range(more.shape[0] // ROW_TOKENS):
        for ranks, part in halves:
            projected[ranks, r * ROW_TOKENS : (r + 1) * ROW_TOKENS] = part[index[dest_at + r], 1]
    copies[0].wait()
    sums[:rank] = jnp.dot(low[...], tokens[...], preferred_element_type=jnp.float32)
    copies[1].wait()
    sums[rank:] = jnp.dot(projected[...], more[...], preferred_element_type=jnp.float32)
    done[...] = jnp.zeros_like(done)
    store = pltpu.make_async_copy(sums, out, sem.at[2])
    store.start()
    store.wait()


def gradient_products(
    index, core_at, source_at, dest_at, crossed, other, token, attention, gradient
):
    rank = 2 * crossed.shape[2]
    slot_tokens, width = attention.shape
    row_tokens = gradient.shape[0]
    return pl.pallas_call(
        functools.partial(gradient_kernel, core_at, source_at, dest_at),
        in_specs=[SMEM] + [ANY] * 5,
        out_specs=[HBM, VMEM],
        out_shape=[
            jax.ShapeDtypeStruct((2 * rank, width), jnp.float32),
            jax.ShapeDtypeStruct((8, LANES), jnp.float32),
        ],
        scratch_shapes=[
            pltpu.VMEM((2, crossed.shape[0], 2) + crossed.shape[2:], jnp.bfloat16),
            pltpu.VMEM((rank, slot_tokens), jnp.bfloat16),
            pltpu.VMEM((rank, row_tokens), jnp.bfloat16),
            pltpu.VMEM((2 * rank, width), jnp.float32),
            pltpu.VMEM(attention.shape, jnp.bfloat16),
            pltpu.VMEM(gradient.shape, jnp.bfloat16),
            pltpu.SemaphoreType.DMA((5,)),
        ],
        compiler_params=pltpu.CompilerParams(vmem_limit_bytes=SMALL_LIMIT),
        cost_estimate=pl.CostEstimate(
            flops=2 * rank * width * (slot_tokens + row_tokens),
            bytes_accessed=2 * width * (slot_tokens + row_tokens),
            transcendentals=0,
        ),
        name="gradient_products",
    )(index, crossed, other, token, attention, gradient)


def unfold_kernel(arrived, gradients, out, down_gradient, up_gradient):
    groups, slots, folded, half_width = arrived.shape
    piece = folded // 2
    for slot in range(slots):
        for pair in range(groups // 2):
            halves = []
            for j in (2 * pair, 2 * pair + 1):
                value = arrived[j, slot].astype(jnp.float32)
                pieces = []
                for n in range(half_width // LANES):
                    lanes = slice(n * LANES, (n + 1) * LANES)
                    pieces += [value[:piece, lanes], value[piece:, lanes]]
                halves.append(jnp.concatenate(pieces, axis=1))
            rows = pl.ds(slot * groups * piece + pair * folded, folded)
            out[rows, :] = jnp.concatenate(halves, axis=0).astype(out.dtype)

    @pl.when(pl.program_id(0) == 0)
    def _():
        values = []
        for j in range(groups):
            value = gradients[j, 0].astype(jnp.float32)
            values.append(jnp.concatenate([value[:piece], value[piece:]], axis=1))
        down_gradient[...] = jnp.concatenate(values[: groups // 2], axis=0)
        up_gradient[...] = jnp.concatenate(values[groups // 2 :], axis=0)


def unfold(arrived, slots):
    groups, _, folded, half_width = arrived.shape
    piece, width = folded // 2, 2 * half_width
    rank = groups * piece // 2
    step = slots // 2
    return pl.pallas_call(
        unfold_kernel,
        grid=(slots // step,),
        in_specs=[
            pl.BlockSpec((groups, step, folded, half_width), lambda s: (0, s, 0, 0)),
            pl.BlockSpec((groups, 1, folded, half_width), lambda s: (0, slots, 0, 0)),
        ],
        out_specs=[
            pl.BlockSpec((step * groups * piece, width), lambda s: (s, 0)),
            pl.BlockSpec((rank, width), lambda s: (0, 0)),
            pl.BlockSpec((rank, width), lambda s: (0, 0)),
        ],
        out_shape=[
            jax.ShapeDtypeStruct((slots * groups * piece, width), jnp.bfloat16),
            jax.ShapeDtypeStruct((rank, width), jnp.float32),
            jax.ShapeDtypeStruct((rank, width), jnp.float32),
        ],
        compiler_params=pltpu.CompilerParams(vmem_limit_bytes=SMALL_LIMIT),
        name="unfold",
    )(arrived, arrived)


def body(
    attention_slot_outputs,
    output_gradient_rows,
    output_weight,
    down_weight,
    up_weight,
    assign,
    counts,
):
    groups = counts.shape[0]
    rows = assign.shape[0]
    rows_here = output_gradient_rows.shape[0] // ROW_TOKENS
    slot_cap = attention_slot_outputs.shape[0] // ROW_TOKENS
    width_here = output_gradient_rows.shape[1]
    rank = up_weight.shape[0]
    tp = lax.axis_size("tp")
    piece = ROW_TOKENS // groups
    own_group = lax.axis_index("group")
    group_ids = jnp.arange(groups, dtype=jnp.int32)
    onehot = (assign[:, None] == group_ids[None, :]).astype(jnp.int32)
    before = jnp.cumsum(onehot, axis=0) - onehot
    order_in = jnp.sum(before * onehot, axis=1)
    free_slots = jnp.sum(onehot * counts[None, :], axis=1)
    position = slot_cap - free_slots + order_in
    own_dest = lax.dynamic_slice_in_dim(assign, own_group * rows_here, rows_here)
    scale_factor = adapter_scale / math.sqrt(rows * ROW_TOKENS)

    index = lax.axis_index("tp")
    chips = tp // 2
    y, core = index // 2, index % 2

    def move(value, n):
        pairs = [(2 * a + b, 2 * ((a + n) % chips) + b) for a in range(chips) for b in range(2)]
        return lax.ppermute(value, "tp", pairs)

    def swap(value):
        return lax.ppermute(value, "tp", [(i, i ^ 1) for i in range(tp)])

    pieces_out = output_gradient_rows.reshape(rows_here, groups, piece, width_here)
    pieces_out = pieces_out.transpose(1, 0, 2, 3)
    pieces_out, up_weight, down_weight_first = lax.optimization_barrier(
        (pieces_out, up_weight, down_weight)
    )
    spread = lax.all_to_all(
        pieces_out,
        "group",
        split_axis=0,
        concat_axis=0,
        tiled=True,
    ).reshape(rows * piece, width_here)

    slot_ids = jnp.arange(slot_cap, dtype=jnp.int32)
    row_ids = jnp.arange(rows_here, dtype=jnp.int32)
    row_position = position.reshape(groups, rows_here)
    hit_row = assign.reshape(groups, rows_here) == own_group
    low_pick = jnp.max(jnp.where(own_dest[None, :] == group_ids[:, None], row_ids, -1), axis=1)
    projected_pick = jnp.max(jnp.where(hit_row, rows_here + row_position, -1), axis=1)
    slot_match = hit_row[:, :, None] & (row_position[:, :, None] == slot_ids)
    slot_source = jnp.max(jnp.where(slot_match, group_ids[:, None, None], -1), axis=(0, 1))
    owners = []
    for step in (0, chips - 1, 1, 2):
        pair = 2 * lax.rem(y + step, chips)
        owners += [pair + core, pair + 1 - core]
    pieces = [
        assign, position, jnp.stack([low_pick, projected_pick], axis=1).reshape(-1), slot_source,
        own_dest, jnp.stack(owners + [core]).astype(jnp.int32),
    ]
    at = [0]
    for part in pieces:
        at.append(at[-1] + part.shape[0])
    _, _, pick_at, source_at, dest_at, owner_at, end = at
    table = jnp.concatenate(pieces)

    low_part = dot_minor(up_weight, output_gradient_rows)
    projected_part = lax.dot_general(
        down_weight_first, attention_slot_outputs, (((0,), (1,)), ((), ())),
        preferred_element_type=jnp.float32,
    )
    parts = jnp.concatenate([low_part, projected_part], axis=1)
    parts = parts + swap(parts)
    share = lax.dynamic_slice_in_dim(parts, core * (rank // 2), rank // 2, axis=0)
    share = share + move(share, 1) + move(share, -1) + move(share, 2)

    send = rank_sums_to_send(table, pick_at, groups, rows_here, share)
    crossed = lax.all_to_all(send, "group", split_axis=0, concat_axis=0, tiled=True)

    spread, _ = lax.optimization_barrier((spread, share))
    left, right = move(spread, 1), move(spread, -1)
    other = swap(spread)
    sums, done = block_products(
        table, [owner_at, owner_at + 1], [spread, other], output_weight, send,
        name="own_products",
    )
    crossed_other = swap(crossed)
    left_top, right_bottom, left, right = take_halves(left, right, crossed, done)
    far = [move(left_top, 1), move(right_bottom, -1)]
    partial_grads, done = gradient_products(
        table, end - 1, source_at, dest_at, crossed, crossed_other, left_top, attention_slot_outputs,
        output_gradient_rows,
    )
    share_rows = 2 * rank // groups
    grads = lax.all_to_all(
        partial_grads.reshape(groups, share_rows, width_here), "group", split_axis=0, concat_axis=0,
        tiled=True,
    )
    sums, _ = block_products(
        table, [owner_at + i for i in range(2, 6)], [left, swap(left), right, swap(right)],
        output_weight, done, sums, name="side_products",
    )
    placed = last_products(
        rows, scale_factor, table, [owner_at + 6, owner_at + 7], end - 1, far,
        [swap(part) for part in far], grads, (crossed, crossed_other), output_weight, sums,
        down_weight.T, slot_cap,
    )

    arrived = lax.all_to_all(placed, "group", split_axis=0, concat_axis=0, tiled=True)
    attention_gradient, down_gradient, up_gradient = unfold(arrived, slot_cap)
    return attention_gradient, down_gradient.T, up_gradient


def solution(mesh):
    in_specs = (
        P("group", "tp"),
        P("group", "tp"),
        P("tp", None),
        P("tp", None),
        P(None, "tp"),
        P(),
        P(),
    )
    out_specs = (P("group", "tp"), P("tp", None), P(None, "tp"))
    return jax.shard_map(body, mesh=mesh, in_specs=in_specs, out_specs=out_specs, check_vma=False)
```

```python
import functools
import math

import jax
import jax.numpy as jnp
from jax import lax
from jax.experimental import pallas as pl
from jax.experimental.pallas import tpu as pltpu
from jax.sharding import PartitionSpec as P

ROW_TOKENS = 128
LANES = 128
VMEM_LIMIT = 44 * 2**20
BASE_ROOM = 16
SMALL_LIMIT = 18 * 2**20


adapter_scale = 2.0

ANY = pl.BlockSpec(memory_space=pl.ANY)
HBM = pl.BlockSpec(memory_space=pltpu.HBM)
VMEM = pl.BlockSpec(memory_space=pltpu.VMEM)
SMEM = pl.BlockSpec(memory_space=pltpu.SMEM)


def dot_minor(left, right):
    return lax.dot_general(
        left, right, (((1,), (1,)), ((), ())), preferred_element_type=jnp.float32
    )


def after_kernel(*refs):
    pass


def after(values, token):
    count = len(values)
    return pl.pallas_call(
        after_kernel,
        in_specs=[ANY] * (count + 1),
        out_specs=[ANY] * count,
        out_shape=[jax.ShapeDtypeStruct(value.shape, value.dtype) for value in values],
        input_output_aliases={i: i for i in range(count)},
        compiler_params=pltpu.CompilerParams(vmem_limit_bytes=2**20),
        name="after",
    )(*values, token)


def halves_kernel(left, right, grads, token, top, bottom, *refs):
    buffer, sem = refs[3:]
    half = top.shape[0]
    parts = ((left.at[pl.ds(0, half)], top), (right.at[pl.ds(half, half)], bottom))
    loads = [
        pltpu.make_async_copy(part, buffer.at[i], sem.at[i]) for i, (part, _) in enumerate(parts)
    ]
    stores = [
        pltpu.make_async_copy(buffer.at[i], out, sem.at[2 + i]) for i, (_, out) in enumerate(parts)
    ]
    for load in loads:
        load.start()
    for load, store in zip(loads, stores):
        load.wait()
        store.start()
    for store in stores:
        store.wait()


def take_halves(left, right, grads, token):
    half = jax.ShapeDtypeStruct((left.shape[0] // 2, left.shape[1]), left.dtype)
    return pl.pallas_call(
        halves_kernel,
        in_specs=[ANY] * 4,
        out_specs=[HBM] * 2 + [ANY] * 3,
        out_shape=[half] * 2
        + [jax.ShapeDtypeStruct(part.shape, part.dtype) for part in (left, right, grads)],
        input_output_aliases={0: 2, 1: 3, 2: 4},
        scratch_shapes=[
            pltpu.VMEM((2,) + half.shape, half.dtype),
            pltpu.SemaphoreType.DMA((4,)),
        ],
        compiler_params=pltpu.CompilerParams(vmem_limit_bytes=SMALL_LIMIT),
        cost_estimate=pl.CostEstimate(
            flops=0, bytes_accessed=8 * left.shape[0] * left.shape[1], transcendentals=0
        ),
        name="take_halves",
    )(left, right, grads, token)


def block_kernel(table, first, index, *refs):
    refs = list(refs)
    count = len(table)
    blocks = [refs.pop(0) for _ in range(count)]
    weight, _ = refs.pop(0), refs.pop(0)
    if not first:
        sums_in = refs.pop(0)
    sums_out, done, x, w, sums, sums_was, x_sem, w_sem, sem = refs
    tokens, width = x.shape[1:]
    done[...] = jnp.zeros_like(done)
    copies = []
    for k, place in enumerate(table):
        owner = index[place]
        columns = pl.ds(pl.multiple_of(owner * width, width), width)
        copies.append([
            pltpu.make_async_copy(blocks[k], x.at[k], x_sem.at[k]),
            pltpu.make_async_copy(weight.at[:, columns], w.at[k % 4], w_sem.at[k]),
        ])
    if not first:
        copies.append([pltpu.make_async_copy(sums_in.at[pl.ds(0, tokens)], sums_was, sem.at[0])])
    for each in copies[:3]:
        for copy in each:
            copy.start()
    for k in range(count):
        for copy in copies[k]:
            copy.wait()
        if k + 3 < len(copies):
            for copy in copies[k + 3]:
                copy.start()
        value = dot_minor(x[k], w[k % 4])
        if k > 0:
            sums[...] += value
        else:
            sums[...] = value
    if not first:
        copies[count][0].wait()
        sums[...] += sums_was[...]
    store = pltpu.make_async_copy(sums, sums_out.at[pl.ds(0, tokens)], sem.at[1])
    store.start()
    store.wait()


def block_products(index, table, blocks, weight, token, sums=None, name=""):
    count = len(blocks)
    tokens, width = blocks[0].shape
    out_width = weight.shape[0]
    first = sums is None
    return pl.pallas_call(
        functools.partial(block_kernel, table, first),
        in_specs=[SMEM] + [ANY] * (count + (2 if first else 3)),
        out_specs=[HBM, VMEM],
        out_shape=[
            jax.ShapeDtypeStruct((BASE_ROOM * tokens, out_width), jnp.float32),
            jax.ShapeDtypeStruct((8, LANES), jnp.float32),
        ],
        scratch_shapes=[
            pltpu.VMEM((count, tokens, width), jnp.bfloat16),
            pltpu.VMEM((4, out_width, width), jnp.bfloat16),
            pltpu.VMEM((tokens, out_width), jnp.float32),
            pltpu.VMEM((tokens, out_width), jnp.float32),
            pltpu.SemaphoreType.DMA((count,)),
            pltpu.SemaphoreType.DMA((count,)),
            pltpu.SemaphoreType.DMA((2,)),
        ],
        compiler_params=pltpu.CompilerParams(vmem_limit_bytes=VMEM_LIMIT),
        cost_estimate=pl.CostEstimate(
            flops=2 * count * tokens * width * out_width,
            bytes_accessed=2 * width * count * (tokens + out_width),
            transcendentals=0,
        ),
        name=name,
    )(index, *blocks, weight, token, *([] if first else [sums]))


def last_kernel(
    rows, scale, table, core_at, index, far_a, far_b, other_a, other_b, grads_in, crossed,
    crossed_other, weight, sums_in, down, out, x, w, sums, grads, pieces, low, low_rounded, x_sem,
    w_sem, sem,
):
    half, width = far_a.shape
    groups, ranks = pieces.shape[1:3]
    tokens = 2 * half
    piece = tokens // rows
    tile = 2 * LANES
    tiles = w.shape[0] // tile
    core = index[core_at]

    def load_sums(columns, semaphore):
        return pltpu.make_async_copy(
            sums_in.at[pl.ds(0, tokens), columns], sums.at[:, columns], semaphore
        )

    copies = []
    for i, part in enumerate((far_a, far_b, other_a, other_b)):
        rows_of, lanes = pl.ds((i % 2) * half, half), pl.ds((i // 2) * width, width)
        copies.append(pltpu.make_async_copy(part, x.at[rows_of, lanes], x_sem.at[i]))
    low_copies = [
        pltpu.make_async_copy(crossed.at[:, 2], pieces.at[core], sem.at[tiles]),
        pltpu.make_async_copy(crossed_other.at[:, 2], pieces.at[1 - core], sem.at[tiles + 1]),
    ]
    tile_copies = []
    for n in range(tiles):
        span = pl.ds(n * tile, tile)
        each = []
        for k in range(2):
            columns = pl.ds(pl.multiple_of(index[table[k]] * width, width), width)
            lanes = pl.ds(k * width, width)
            each.append(
                pltpu.make_async_copy(weight.at[span, columns], w.at[span, lanes], w_sem.at[n, k])
            )
        each.append(load_sums(span, sem.at[n]))
        tile_copies.append(each)
    load_grads = pltpu.make_async_copy(grads_in, grads, sem.at[tiles + 2])
    for each in [low_copies, copies] + tile_copies + [[load_grads]]:
        for copy in each:
            copy.start()
    out[...] = jnp.zeros_like(out)
    for copy in low_copies:
        copy.wait()
    share = tokens // groups
    for group in range(groups):
        both = jnp.concatenate([pieces[0, group], pieces[1, group]], axis=0).astype(jnp.float32)
        low[group * share : (group + 1) * share] = both.T[:share]
    low_rounded[...] = low[...].astype(jnp.bfloat16)
    for copy in copies:
        copy.wait()
    for n in range(tiles):
        span = slice(n * tile, (n + 1) * tile)
        for copy in tile_copies[n]:
            copy.wait()
        total = sums[:, span] + dot_minor(x[...], w[span])
        total += adapter_scale * jnp.dot(
            low_rounded[...], down[:, span], preferred_element_type=jnp.float32
        )
        for row in range(rows):
            mine = total[row * piece : (row + 1) * piece]
            folded = jnp.concatenate([mine[:, :LANES], mine[:, LANES:]], axis=0)
            out[index[row], index[rows + row], :, n * LANES : (n + 1) * LANES] = folded.astype(
                jnp.bfloat16
            )
    load_grads.wait()
    total = scale * jnp.sum(grads[...], axis=0)
    folded = jnp.concatenate([total[:, : width // 2], total[:, width // 2 :]], axis=0)
    folded = folded.astype(jnp.bfloat16)
    for group in range(out.shape[0]):
        out[group, out.shape[1] - 1] = folded


def last_products(
    rows, scale, index, table, core_at, far, other, grads, crossed, weight, sums, down, slots
):
    half, width = far[0].shape
    tokens = 2 * half
    rank, out_width = down.shape
    groups = crossed[0].shape[0]
    piece = tokens // rows
    tiles = out_width // (2 * LANES)
    return pl.pallas_call(
        functools.partial(last_kernel, rows, scale, table, core_at),
        in_specs=[SMEM] + [ANY] * 9 + [VMEM],
        out_specs=VMEM,
        scratch_shapes=[
            pltpu.VMEM((tokens, 2 * width), jnp.bfloat16),
            pltpu.VMEM((out_width, 2 * width), jnp.bfloat16),
            pltpu.VMEM((tokens, out_width), jnp.float32),
            pltpu.VMEM(grads.shape, grads.dtype),
            pltpu.VMEM((2, groups, rank // 2, LANES), jnp.bfloat16),
            pltpu.VMEM((tokens, rank), jnp.float32),
            pltpu.VMEM((tokens, rank), jnp.bfloat16),
            pltpu.SemaphoreType.DMA((4,)),
            pltpu.SemaphoreType.DMA((tiles, 2)),
            pltpu.SemaphoreType.DMA((tiles + 3,)),
        ],
        out_shape=jax.ShapeDtypeStruct(
            (groups, slots + 1, 2 * piece, out_width // 2), jnp.bfloat16
        ),
        compiler_params=pltpu.CompilerParams(vmem_limit_bytes=VMEM_LIMIT),
        cost_estimate=pl.CostEstimate(
            flops=4 * tokens * width * out_width,
            bytes_accessed=4 * width * tokens + 8 * tokens * out_width,
            transcendentals=0,
        ),
        name="last_products",
    )(index, *far, *other, grads, *crossed, weight, sums, down)


def send_kernel(groups, rows_here, pick_at, index, share, out):
    piece = ROW_TOKENS // groups
    lane = lax.broadcasted_iota(jnp.int32, (share.shape[0], ROW_TOKENS), 1)
    for group in range(groups):
        for kind in range(2):
            pick = index[pick_at + 2 * group + kind]
            lanes = pl.ds(pl.multiple_of(jnp.maximum(pick, 0) * ROW_TOKENS, ROW_TOKENS), ROW_TOKENS)
            keep = (pick >= 0).astype(jnp.float32)
            out[group, kind] = (share[:, lanes] * keep).astype(jnp.bfloat16)
        value = jnp.zeros(lane.shape, jnp.float32)
        for r in range(rows_here):
            shift = (r - group) * piece % ROW_TOKENS
            row = share[:, r * ROW_TOKENS : (r + 1) * ROW_TOKENS]
            if shift:
                row = pltpu.roll(row, shift, 1)
            value = jnp.where(lane // piece == r, row, value)
        out[group, 2] = value.astype(jnp.bfloat16)


def rank_sums_to_send(index, pick_at, groups, rows_here, share):
    half = share.shape[0]
    return pl.pallas_call(
        functools.partial(send_kernel, groups, rows_here, pick_at),
        in_specs=[SMEM, VMEM],
        out_specs=VMEM,
        out_shape=jax.ShapeDtypeStruct((groups, 3, half, ROW_TOKENS), jnp.bfloat16),
        compiler_params=pltpu.CompilerParams(vmem_limit_bytes=SMALL_LIMIT),
        cost_estimate=pl.CostEstimate(
            flops=2 * groups * half * ROW_TOKENS, bytes_accessed=8 * groups * half * ROW_TOKENS,
            transcendentals=0,
        ),
        name="rank_sums_to_send",
    )(index, share)


def gradient_kernel(
    core_at, source_at, dest_at, index, crossed, crossed_other, token, attention, gradient, out,
    done, parts, low, projected, sums, tokens, more, sem,
):
    half = crossed.shape[2]
    rank = 2 * half
    core = index[core_at]
    part_copies = [
        pltpu.make_async_copy(part.at[:, pl.ds(0, 2)], parts.at[i], sem.at[3 + i])
        for i, part in enumerate((crossed, crossed_other))
    ]
    copies = [
        pltpu.make_async_copy(attention, tokens, sem.at[0]),
        pltpu.make_async_copy(gradient, more, sem.at[1]),
    ]
    for copy in part_copies + copies:
        copy.start()
    for copy in part_copies:
        copy.wait()
    halves = [
        (pl.ds(pl.multiple_of(owner * half, half), half), parts.at[i])
        for i, owner in enumerate((core, 1 - core))
    ]
    for s in range(tokens.shape[0] // ROW_TOKENS):
        source = index[source_at + s]
        keep = (source >= 0).astype(jnp.float32)
        for ranks, part in halves:
            value = part[jnp.maximum(source, 0), 0].astype(jnp.float32) * keep
            low[ranks, s * ROW_TOKENS : (s + 1) * ROW_TOKENS] = value.astype(jnp.bfloat16)
    for r in range(more.shape[0] // ROW_TOKENS):
        for ranks, part in halves:
            projected[ranks, r * ROW_TOKENS : (r + 1) * ROW_TOKENS] = part[index[dest_at + r], 1]
    copies[0].wait()
    sums[:rank] = jnp.dot(low[...], tokens[...], preferred_element_type=jnp.float32)
    copies[1].wait()
    sums[rank:] = jnp.dot(projected[...], more[...], preferred_element_type=jnp.float32)
    done[...] = jnp.zeros_like(done)
    store = pltpu.make_async_copy(sums, out, sem.at[2])
    store.start()
    store.wait()


def gradient_products(
    index, core_at, source_at, dest_at, crossed, other, token, attention, gradient
):
    rank = 2 * crossed.shape[2]
    slot_tokens, width = attention.shape
    row_tokens = gradient.shape[0]
    return pl.pallas_call(
        functools.partial(gradient_kernel, core_at, source_at, dest_at),
        in_specs=[SMEM] + [ANY] * 5,
        out_specs=[HBM, VMEM],
        out_shape=[
            jax.ShapeDtypeStruct((2 * rank, width), jnp.float32),
            jax.ShapeDtypeStruct((8, LANES), jnp.float32),
        ],
        scratch_shapes=[
            pltpu.VMEM((2, crossed.shape[0], 2) + crossed.shape[2:], jnp.bfloat16),
            pltpu.VMEM((rank, slot_tokens), jnp.bfloat16),
            pltpu.VMEM((rank, row_tokens), jnp.bfloat16),
            pltpu.VMEM((2 * rank, width), jnp.float32),
            pltpu.VMEM(attention.shape, jnp.bfloat16),
            pltpu.VMEM(gradient.shape, jnp.bfloat16),
            pltpu.SemaphoreType.DMA((5,)),
        ],
        compiler_params=pltpu.CompilerParams(vmem_limit_bytes=SMALL_LIMIT),
        cost_estimate=pl.CostEstimate(
            flops=2 * rank * width * (slot_tokens + row_tokens),
            bytes_accessed=2 * width * (slot_tokens + row_tokens),
            transcendentals=0,
        ),
        name="gradient_products",
    )(index, crossed, other, token, attention, gradient)


def unfold_kernel(arrived, gradients, out, down_gradient, up_gradient):
    groups, slots, folded, half_width = arrived.shape
    piece = folded // 2
    for slot in range(slots):
        for pair in range(groups // 2):
            halves = []
            for j in (2 * pair, 2 * pair + 1):
                value = arrived[j, slot].astype(jnp.float32)
                pieces = []
                for n in range(half_width // LANES):
                    lanes = slice(n * LANES, (n + 1) * LANES)
                    pieces += [value[:piece, lanes], value[piece:, lanes]]
                halves.append(jnp.concatenate(pieces, axis=1))
            rows = pl.ds(slot * groups * piece + pair * folded, folded)
            out[rows, :] = jnp.concatenate(halves, axis=0).astype(out.dtype)

    @pl.when(pl.program_id(0) == 0)
    def _():
        values = []
        for j in range(groups):
            value = gradients[j, 0].astype(jnp.float32)
            values.append(jnp.concatenate([value[:piece], value[piece:]], axis=1))
        down_gradient[...] = jnp.concatenate(values[: groups // 2], axis=0)
        up_gradient[...] = jnp.concatenate(values[groups // 2 :], axis=0)


def unfold(arrived, slots):
    groups, _, folded, half_width = arrived.shape
    piece, width = folded // 2, 2 * half_width
    rank = groups * piece // 2
    step = slots // 2
    return pl.pallas_call(
        unfold_kernel,
        grid=(slots // step,),
        in_specs=[
            pl.BlockSpec((groups, step, folded, half_width), lambda s: (0, s, 0, 0)),
            pl.BlockSpec((groups, 1, folded, half_width), lambda s: (0, slots, 0, 0)),
        ],
        out_specs=[
            pl.BlockSpec((step * groups * piece, width), lambda s: (s, 0)),
            pl.BlockSpec((rank, width), lambda s: (0, 0)),
            pl.BlockSpec((rank, width), lambda s: (0, 0)),
        ],
        out_shape=[
            jax.ShapeDtypeStruct((slots * groups * piece, width), jnp.bfloat16),
            jax.ShapeDtypeStruct((rank, width), jnp.float32),
            jax.ShapeDtypeStruct((rank, width), jnp.float32),
        ],
        compiler_params=pltpu.CompilerParams(vmem_limit_bytes=SMALL_LIMIT),
        name="unfold",
    )(arrived, arrived)


def body(
    attention_slot_outputs,
    output_gradient_rows,
    output_weight,
    down_weight,
    up_weight,
    assign,
    counts,
):
    groups = counts.shape[0]
    rows = assign.shape[0]
    rows_here = output_gradient_rows.shape[0] // ROW_TOKENS
    slot_cap = attention_slot_outputs.shape[0] // ROW_TOKENS
    width_here = output_gradient_rows.shape[1]
    rank = up_weight.shape[0]
    tp = lax.axis_size("tp")
    piece = ROW_TOKENS // groups
    own_group = lax.axis_index("group")
    group_ids = jnp.arange(groups, dtype=jnp.int32)
    onehot = (assign[:, None] == group_ids[None, :]).astype(jnp.int32)
    before = jnp.cumsum(onehot, axis=0) - onehot
    order_in = jnp.sum(before * onehot, axis=1)
    free_slots = jnp.sum(onehot * counts[None, :], axis=1)
    position = slot_cap - free_slots + order_in
    own_dest = lax.dynamic_slice_in_dim(assign, own_group * rows_here, rows_here)
    scale_factor = adapter_scale / math.sqrt(rows * ROW_TOKENS)

    index = lax.axis_index("tp")
    chips = tp // 2
    y, core = index // 2, index % 2

    def move(value, n):
        pairs = [(2 * a + b, 2 * ((a + n) % chips) + b) for a in range(chips) for b in range(2)]
        return lax.ppermute(value, "tp", pairs)

    def swap(value):
        return lax.ppermute(value, "tp", [(i, i ^ 1) for i in range(tp)])

    pieces_out = output_gradient_rows.reshape(rows_here, groups, piece, width_here)
    pieces_out = pieces_out.transpose(1, 0, 2, 3)
    pieces_out, up_weight, down_weight_first = lax.optimization_barrier(
        (pieces_out, up_weight, down_weight)
    )
    spread = lax.all_to_all(
        pieces_out,
        "group",
        split_axis=0,
        concat_axis=0,
        tiled=True,
    ).reshape(rows * piece, width_here)

    slot_ids = jnp.arange(slot_cap, dtype=jnp.int32)
    row_ids = jnp.arange(rows_here, dtype=jnp.int32)
    row_position = position.reshape(groups, rows_here)
    hit_row = assign.reshape(groups, rows_here) == own_group
    low_pick = jnp.max(jnp.where(own_dest[None, :] == group_ids[:, None], row_ids, -1), axis=1)
    projected_pick = jnp.max(jnp.where(hit_row, rows_here + row_position, -1), axis=1)
    slot_match = hit_row[:, :, None] & (row_position[:, :, None] == slot_ids)
    slot_source = jnp.max(jnp.where(slot_match, group_ids[:, None, None], -1), axis=(0, 1))
    owners = []
    for step in (0, chips - 1, 1, 2):
        pair = 2 * lax.rem(y + step, chips)
        owners += [pair + core, pair + 1 - core]
    pieces = [
        assign, position, jnp.stack([low_pick, projected_pick], axis=1).reshape(-1), slot_source,
        own_dest, jnp.stack(owners + [core]).astype(jnp.int32),
    ]
    at = [0]
    for part in pieces:
        at.append(at[-1] + part.shape[0])
    _, _, pick_at, source_at, dest_at, owner_at, end = at
    table = jnp.concatenate(pieces)

    low_part = dot_minor(up_weight, output_gradient_rows)
    projected_part = lax.dot_general(
        down_weight_first, attention_slot_outputs, (((0,), (1,)), ((), ())),
        preferred_element_type=jnp.float32,
    )
    parts = jnp.concatenate([low_part, projected_part], axis=1)
    parts = parts + swap(parts)
    share = lax.dynamic_slice_in_dim(parts, core * (rank // 2), rank // 2, axis=0)
    share = share + move(share, 1) + move(share, -1) + move(share, 2)

    send = rank_sums_to_send(table, pick_at, groups, rows_here, share)
    crossed = lax.all_to_all(send, "group", split_axis=0, concat_axis=0, tiled=True)

    spread, _ = lax.optimization_barrier((spread, share))
    left, right = move(spread, 1), move(spread, -1)
    other = swap(spread)
    sums, done = block_products(
        table, [owner_at, owner_at + 1], [spread, other], output_weight, send,
        name="own_products",
    )
    (crossed,) = after([crossed], done)
    crossed_other = swap(crossed)
    partial_grads, done = gradient_products(
        table, end - 1, source_at, dest_at, crossed, crossed_other, done, attention_slot_outputs,
        output_gradient_rows,
    )
    left_top, right_bottom, left, right, partial_grads = take_halves(
        left, right, partial_grads, done
    )
    far = [move(left_top, 1), move(right_bottom, -1)]
    share_rows = 2 * rank // groups
    grads = lax.all_to_all(
        partial_grads.reshape(groups, share_rows, width_here), "group", split_axis=0, concat_axis=0,
        tiled=True,
    )
    sums, done = block_products(
        table, [owner_at + i for i in range(2, 6)], [left, swap(left), right, swap(right)],
        output_weight, done, sums, name="side_products",
    )
    far = after(far, done)
    placed = last_products(
        rows, scale_factor, table, [owner_at + 6, owner_at + 7], end - 1, far,
        [swap(part) for part in far], grads, (crossed, crossed_other), output_weight, sums,
        down_weight.T, slot_cap,
    )

    arrived = lax.all_to_all(placed, "group", split_axis=0, concat_axis=0, tiled=True)
    attention_gradient, down_gradient, up_gradient = unfold(arrived, slot_cap)
    return attention_gradient, down_gradient.T, up_gradient


def solution(mesh):
    in_specs = (
        P("group", "tp"),
        P("group", "tp"),
        P("tp", None),
        P("tp", None),
        P(None, "tp"),
        P(),
        P(),
    )
    out_specs = (P("group", "tp"), P("tp", None), P(None, "tp"))
    return jax.shard_map(body, mesh=mesh, in_specs=in_specs, out_specs=out_specs, check_vma=False)
```

```python
import functools
import math

import jax
import jax.numpy as jnp
from jax import lax
from jax.experimental import pallas as pl
from jax.experimental.pallas import tpu as pltpu
from jax.sharding import PartitionSpec as P

ROW_TOKENS = 128
LANES = 128
VMEM_LIMIT = 44 * 2**20
BASE_ROOM = 16
SMALL_LIMIT = 18 * 2**20


adapter_scale = 2.0

ANY = pl.BlockSpec(memory_space=pl.ANY)
HBM = pl.BlockSpec(memory_space=pltpu.HBM)
VMEM = pl.BlockSpec(memory_space=pltpu.VMEM)
SMEM = pl.BlockSpec(memory_space=pltpu.SMEM)


def dot_minor(left, right):
    return lax.dot_general(
        left, right, (((1,), (1,)), ((), ())), preferred_element_type=jnp.float32
    )


def prepare_kernel(
    groups, gradient, attention, up, down, pieces, parts, rows_in, slots_in, sem
):
    loads = [
        pltpu.make_async_copy(gradient, rows_in, sem.at[0]),
        pltpu.make_async_copy(attention, slots_in, sem.at[1]),
    ]
    for load in loads:
        load.start()
    tokens = rows_in.shape[0]
    rows_here, piece = tokens // ROW_TOKENS, ROW_TOKENS // groups
    loads[0].wait()
    starts = [r * ROW_TOKENS + j * piece for j in range(groups) for r in range(rows_here)]
    for pair in range(len(starts) // 2):
        both = []
        for start in starts[2 * pair : 2 * pair + 2]:
            tile = start // (2 * piece) * 2 * piece
            value = rows_in[tile : tile + 2 * piece, :].astype(jnp.float32)
            both.append(value[start - tile : start - tile + piece])
        pieces[2 * pair * piece : 2 * (pair + 1) * piece, :] = jnp.concatenate(
            both, axis=0
        ).astype(pieces.dtype)
    parts[:, :tokens] = dot_minor(up[...], rows_in[...])
    loads[1].wait()
    parts[:, tokens:] = dot_minor(down[...], slots_in[...])


def prepare(groups, gradient, attention, up, down):
    rank = up.shape[0]
    return pl.pallas_call(
        functools.partial(prepare_kernel, groups),
        in_specs=[ANY] * 2 + [VMEM] * 2,
        out_specs=[VMEM] * 2,
        out_shape=[
            jax.ShapeDtypeStruct(gradient.shape, gradient.dtype),
            jax.ShapeDtypeStruct((rank, gradient.shape[0] + attention.shape[0]), jnp.float32),
        ],
        scratch_shapes=[
            pltpu.VMEM(gradient.shape, gradient.dtype),
            pltpu.VMEM(attention.shape, attention.dtype),
            pltpu.SemaphoreType.DMA((2,)),
        ],
        compiler_params=pltpu.CompilerParams(vmem_limit_bytes=56 * 2**20),
        name="prepare",
    )(gradient, attention, up, down)


def after_kernel(*refs):
    pass


def after(values, token):
    count = len(values)
    return pl.pallas_call(
        after_kernel,
        in_specs=[ANY] * (count + 1),
        out_specs=[ANY] * count,
        out_shape=[jax.ShapeDtypeStruct(value.shape, value.dtype) for value in values],
        input_output_aliases={i: i for i in range(count)},
        compiler_params=pltpu.CompilerParams(vmem_limit_bytes=2**20),
        name="after",
    )(*values, token)


def halves_kernel(left, right, grads, token, top, bottom, *refs):
    buffer, sem = refs[3:]
    half = top.shape[0]
    parts = ((left.at[pl.ds(0, half)], top), (right.at[pl.ds(half, half)], bottom))
    loads = [
        pltpu.make_async_copy(part, buffer.at[i], sem.at[i]) for i, (part, _) in enumerate(parts)
    ]
    stores = [
        pltpu.make_async_copy(buffer.at[i], out, sem.at[2 + i]) for i, (_, out) in enumerate(parts)
    ]
    for load in loads:
        load.start()
    for load, store in zip(loads, stores):
        load.wait()
        store.start()
    for store in stores:
        store.wait()


def take_halves(left, right, grads, token):
    half = jax.ShapeDtypeStruct((left.shape[0] // 2, left.shape[1]), left.dtype)
    return pl.pallas_call(
        halves_kernel,
        in_specs=[ANY] * 4,
        out_specs=[HBM] * 2 + [ANY] * 3,
        out_shape=[half] * 2
        + [jax.ShapeDtypeStruct(part.shape, part.dtype) for part in (left, right, grads)],
        input_output_aliases={0: 2, 1: 3, 2: 4},
        scratch_shapes=[
            pltpu.VMEM((2,) + half.shape, half.dtype),
            pltpu.SemaphoreType.DMA((4,)),
        ],
        compiler_params=pltpu.CompilerParams(vmem_limit_bytes=SMALL_LIMIT),
        cost_estimate=pl.CostEstimate(
            flops=0, bytes_accessed=8 * left.shape[0] * left.shape[1], transcendentals=0
        ),
        name="take_halves",
    )(left, right, grads, token)


def block_kernel(table, first, index, *refs):
    refs = list(refs)
    count = len(table)
    blocks = [refs.pop(0) for _ in range(count)]
    weight, _ = refs.pop(0), refs.pop(0)
    if not first:
        sums_in = refs.pop(0)
    sums_out, done, x, w, sums, sums_was, x_sem, w_sem, sem = refs
    tokens, width = x.shape[1:]
    done[...] = jnp.zeros_like(done)
    copies = []
    for k, place in enumerate(table):
        owner = index[place]
        columns = pl.ds(pl.multiple_of(owner * width, width), width)
        copies.append([
            pltpu.make_async_copy(blocks[k], x.at[k], x_sem.at[k]),
            pltpu.make_async_copy(weight.at[:, columns], w.at[k % 4], w_sem.at[k]),
        ])
    if not first:
        copies.append([pltpu.make_async_copy(sums_in.at[pl.ds(0, tokens)], sums_was, sem.at[0])])
    for each in copies[:3]:
        for copy in each:
            copy.start()
    for k in range(count):
        for copy in copies[k]:
            copy.wait()
        if k + 3 < len(copies):
            for copy in copies[k + 3]:
                copy.start()
        value = dot_minor(x[k], w[k % 4])
        if k > 0:
            sums[...] += value
        else:
            sums[...] = value
    if not first:
        copies[count][0].wait()
        sums[...] += sums_was[...]
    store = pltpu.make_async_copy(sums, sums_out.at[pl.ds(0, tokens)], sem.at[1])
    store.start()
    store.wait()


def block_products(index, table, blocks, weight, token, sums=None, name=""):
    count = len(blocks)
    tokens, width = blocks[0].shape
    out_width = weight.shape[0]
    first = sums is None
    return pl.pallas_call(
        functools.partial(block_kernel, table, first),
        in_specs=[SMEM] + [ANY] * (count + (2 if first else 3)),
        out_specs=[HBM, VMEM],
        out_shape=[
            jax.ShapeDtypeStruct((BASE_ROOM * tokens, out_width), jnp.float32),
            jax.ShapeDtypeStruct((8, LANES), jnp.float32),
        ],
        scratch_shapes=[
            pltpu.VMEM((count, tokens, width), jnp.bfloat16),
            pltpu.VMEM((4, out_width, width), jnp.bfloat16),
            pltpu.VMEM((tokens, out_width), jnp.float32),
            pltpu.VMEM((tokens, out_width), jnp.float32),
            pltpu.SemaphoreType.DMA((count,)),
            pltpu.SemaphoreType.DMA((count,)),
            pltpu.SemaphoreType.DMA((2,)),
        ],
        compiler_params=pltpu.CompilerParams(vmem_limit_bytes=VMEM_LIMIT),
        cost_estimate=pl.CostEstimate(
            flops=2 * count * tokens * width * out_width,
            bytes_accessed=2 * width * count * (tokens + out_width),
            transcendentals=0,
        ),
        name=name,
    )(index, *blocks, weight, token, *([] if first else [sums]))


def last_kernel(
    rows, scale, table, core_at, index, far_a, far_b, other_a, other_b, grads_in, crossed,
    crossed_other, weight, sums_in, down, out, x, w, sums, grads, pieces, low, low_rounded, x_sem,
    w_sem, sem,
):
    half, width = far_a.shape
    groups, ranks = pieces.shape[1:3]
    tokens = 2 * half
    piece = tokens // rows
    tile = 2 * LANES
    tiles = w.shape[0] // tile
    core = index[core_at]

    def load_sums(columns, semaphore):
        return pltpu.make_async_copy(
            sums_in.at[pl.ds(0, tokens), columns], sums.at[:, columns], semaphore
        )

    copies = []
    for i, part in enumerate((far_a, far_b, other_a, other_b)):
        rows_of, lanes = pl.ds((i % 2) * half, half), pl.ds((i // 2) * width, width)
        copies.append(pltpu.make_async_copy(part, x.at[rows_of, lanes], x_sem.at[i]))
    low_copies = [
        pltpu.make_async_copy(crossed.at[:, 2], pieces.at[core], sem.at[tiles]),
        pltpu.make_async_copy(crossed_other.at[:, 2], pieces.at[1 - core], sem.at[tiles + 1]),
    ]
    tile_copies = []
    for n in range(tiles):
        span = pl.ds(n * tile, tile)
        each = []
        for k in range(2):
            columns = pl.ds(pl.multiple_of(index[table[k]] * width, width), width)
            lanes = pl.ds(k * width, width)
            each.append(
                pltpu.make_async_copy(weight.at[span, columns], w.at[span, lanes], w_sem.at[n, k])
            )
        each.append(load_sums(span, sem.at[n]))
        tile_copies.append(each)
    load_grads = pltpu.make_async_copy(grads_in, grads, sem.at[tiles + 2])
    for each in [low_copies, copies, tile_copies[0]]:
        for copy in each:
            copy.start()
    out[...] = jnp.zeros_like(out)
    for copy in low_copies:
        copy.wait()
    share = tokens // groups
    for group in range(groups):
        both = jnp.concatenate([pieces[0, group], pieces[1, group]], axis=0).astype(jnp.float32)
        low[group * share : (group + 1) * share] = both.T[:share]
    low_rounded[...] = low[...].astype(jnp.bfloat16)
    for each in tile_copies[1:] + [[load_grads]]:
        for copy in each:
            copy.start()
    for copy in copies:
        copy.wait()
    for n in range(tiles):
        span = slice(n * tile, (n + 1) * tile)
        for copy in tile_copies[n]:
            copy.wait()
        total = sums[:, span] + dot_minor(x[...], w[span])
        total += adapter_scale * jnp.dot(
            low_rounded[...], down[:, span], preferred_element_type=jnp.float32
        )
        for row in range(rows):
            mine = total[row * piece : (row + 1) * piece]
            folded = jnp.concatenate([mine[:, :LANES], mine[:, LANES:]], axis=0)
            out[index[row], index[rows + row], :, n * LANES : (n + 1) * LANES] = folded.astype(
                jnp.bfloat16
            )
    load_grads.wait()
    total = scale * jnp.sum(grads[...], axis=0)
    folded = jnp.concatenate([total[:, : width // 2], total[:, width // 2 :]], axis=0)
    folded = folded.astype(jnp.bfloat16)
    for group in range(out.shape[0]):
        out[group, out.shape[1] - 1] = folded


def last_products(
    rows, scale, index, table, core_at, far, other, grads, crossed, weight, sums, down, slots
):
    half, width = far[0].shape
    tokens = 2 * half
    rank, out_width = down.shape
    groups = crossed[0].shape[0]
    piece = tokens // rows
    tiles = out_width // (2 * LANES)
    return pl.pallas_call(
        functools.partial(last_kernel, rows, scale, table, core_at),
        in_specs=[SMEM] + [ANY] * 9 + [VMEM],
        out_specs=VMEM,
        scratch_shapes=[
            pltpu.VMEM((tokens, 2 * width), jnp.bfloat16),
            pltpu.VMEM((out_width, 2 * width), jnp.bfloat16),
            pltpu.VMEM((tokens, out_width), jnp.float32),
            pltpu.VMEM(grads.shape, grads.dtype),
            pltpu.VMEM((2, groups, rank // 2, LANES), jnp.bfloat16),
            pltpu.VMEM((tokens, rank), jnp.float32),
            pltpu.VMEM((tokens, rank), jnp.bfloat16),
            pltpu.SemaphoreType.DMA((4,)),
            pltpu.SemaphoreType.DMA((tiles, 2)),
            pltpu.SemaphoreType.DMA((tiles + 3,)),
        ],
        out_shape=jax.ShapeDtypeStruct(
            (groups, slots + 1, 2 * piece, out_width // 2), jnp.bfloat16
        ),
        compiler_params=pltpu.CompilerParams(vmem_limit_bytes=VMEM_LIMIT),
        cost_estimate=pl.CostEstimate(
            flops=4 * tokens * width * out_width,
            bytes_accessed=4 * width * tokens + 8 * tokens * out_width,
            transcendentals=0,
        ),
        name="last_products",
    )(index, *far, *other, grads, *crossed, weight, sums, down)


def send_kernel(groups, rows_here, pick_at, index, share, out):
    piece = ROW_TOKENS // groups
    lane = lax.broadcasted_iota(jnp.int32, (share.shape[0], ROW_TOKENS), 1)
    for group in range(groups):
        for kind in range(2):
            pick = index[pick_at + 2 * group + kind]
            lanes = pl.ds(pl.multiple_of(jnp.maximum(pick, 0) * ROW_TOKENS, ROW_TOKENS), ROW_TOKENS)
            keep = (pick >= 0).astype(jnp.float32)
            out[group, kind] = (share[:, lanes] * keep).astype(jnp.bfloat16)
        value = jnp.zeros(lane.shape, jnp.float32)
        for r in range(rows_here):
            shift = (r - group) * piece % ROW_TOKENS
            row = share[:, r * ROW_TOKENS : (r + 1) * ROW_TOKENS]
            if shift:
                row = pltpu.roll(row, shift, 1)
            value = jnp.where(lane // piece == r, row, value)
        out[group, 2] = value.astype(jnp.bfloat16)


def rank_sums_to_send(index, pick_at, groups, rows_here, share):
    half = share.shape[0]
    return pl.pallas_call(
        functools.partial(send_kernel, groups, rows_here, pick_at),
        in_specs=[SMEM, VMEM],
        out_specs=VMEM,
        out_shape=jax.ShapeDtypeStruct((groups, 3, half, ROW_TOKENS), jnp.bfloat16),
        compiler_params=pltpu.CompilerParams(vmem_limit_bytes=SMALL_LIMIT),
        cost_estimate=pl.CostEstimate(
            flops=2 * groups * half * ROW_TOKENS, bytes_accessed=8 * groups * half * ROW_TOKENS,
            transcendentals=0,
        ),
        name="rank_sums_to_send",
    )(index, share)


def gradient_kernel(
    core_at, source_at, dest_at, index, crossed, crossed_other, token, attention, gradient, out,
    done, parts, low, projected, sums, tokens, more, sem,
):
    half = crossed.shape[2]
    rank = 2 * half
    core = index[core_at]
    part_copies = [
        pltpu.make_async_copy(part.at[:, pl.ds(0, 2)], parts.at[i], sem.at[3 + i])
        for i, part in enumerate((crossed, crossed_other))
    ]
    copies = [
        pltpu.make_async_copy(attention, tokens, sem.at[0]),
        pltpu.make_async_copy(gradient, more, sem.at[1]),
    ]
    for copy in part_copies + copies:
        copy.start()
    for copy in part_copies:
        copy.wait()
    halves = [
        (pl.ds(pl.multiple_of(owner * half, half), half), parts.at[i])
        for i, owner in enumerate((core, 1 - core))
    ]
    for s in range(tokens.shape[0] // ROW_TOKENS):
        source = index[source_at + s]
        keep = (source >= 0).astype(jnp.float32)
        for ranks, part in halves:
            value = part[jnp.maximum(source, 0), 0].astype(jnp.float32) * keep
            low[ranks, s * ROW_TOKENS : (s + 1) * ROW_TOKENS] = value.astype(jnp.bfloat16)
    for r in range(more.shape[0] // ROW_TOKENS):
        for ranks, part in halves:
            projected[ranks, r * ROW_TOKENS : (r + 1) * ROW_TOKENS] = part[index[dest_at + r], 1]
    copies[0].wait()
    sums[:rank] = jnp.dot(low[...], tokens[...], preferred_element_type=jnp.float32)
    copies[1].wait()
    sums[rank:] = jnp.dot(projected[...], more[...], preferred_element_type=jnp.float32)
    done[...] = jnp.zeros_like(done)
    store = pltpu.make_async_copy(sums, out, sem.at[2])
    store.start()
    store.wait()


def gradient_products(
    index, core_at, source_at, dest_at, crossed, other, token, attention, gradient
):
    rank = 2 * crossed.shape[2]
    slot_tokens, width = attention.shape
    row_tokens = gradient.shape[0]
    return pl.pallas_call(
        functools.partial(gradient_kernel, core_at, source_at, dest_at),
        in_specs=[SMEM] + [ANY] * 5,
        out_specs=[HBM, VMEM],
        out_shape=[
            jax.ShapeDtypeStruct((2 * rank, width), jnp.float32),
            jax.ShapeDtypeStruct((8, LANES), jnp.float32),
        ],
        scratch_shapes=[
            pltpu.VMEM((2, crossed.shape[0], 2) + crossed.shape[2:], jnp.bfloat16),
            pltpu.VMEM((rank, slot_tokens), jnp.bfloat16),
            pltpu.VMEM((rank, row_tokens), jnp.bfloat16),
            pltpu.VMEM((2 * rank, width), jnp.float32),
            pltpu.VMEM(attention.shape, jnp.bfloat16),
            pltpu.VMEM(gradient.shape, jnp.bfloat16),
            pltpu.SemaphoreType.DMA((5,)),
        ],
        compiler_params=pltpu.CompilerParams(vmem_limit_bytes=SMALL_LIMIT),
        cost_estimate=pl.CostEstimate(
            flops=2 * rank * width * (slot_tokens + row_tokens),
            bytes_accessed=2 * width * (slot_tokens + row_tokens),
            transcendentals=0,
        ),
        name="gradient_products",
    )(index, crossed, other, token, attention, gradient)


def unfold_kernel(arrived, gradients, out, down_gradient, up_gradient):
    groups, slots, folded, half_width = arrived.shape
    piece = folded // 2
    for slot in range(slots):
        for pair in range(groups // 2):
            halves = []
            for j in (2 * pair, 2 * pair + 1):
                value = arrived[j, slot].astype(jnp.float32)
                pieces = []
                for n in range(half_width // LANES):
                    lanes = slice(n * LANES, (n + 1) * LANES)
                    pieces += [value[:piece, lanes], value[piece:, lanes]]
                halves.append(jnp.concatenate(pieces, axis=1))
            rows = pl.ds(slot * groups * piece + pair * folded, folded)
            out[rows, :] = jnp.concatenate(halves, axis=0).astype(out.dtype)

    @pl.when(pl.program_id(0) == 0)
    def _():
        values = []
        for j in range(groups):
            value = gradients[j, 0].astype(jnp.float32)
            values.append(jnp.concatenate([value[:piece], value[piece:]], axis=1))
        down_gradient[...] = jnp.concatenate(values[: groups // 2], axis=0)
        up_gradient[...] = jnp.concatenate(values[groups // 2 :], axis=0)


def unfold(arrived, slots):
    groups, _, folded, half_width = arrived.shape
    piece, width = folded // 2, 2 * half_width
    rank = groups * piece // 2
    step = slots // 2
    return pl.pallas_call(
        unfold_kernel,
        grid=(slots // step,),
        in_specs=[
            pl.BlockSpec((groups, step, folded, half_width), lambda s: (0, s, 0, 0)),
            pl.BlockSpec((groups, 1, folded, half_width), lambda s: (0, slots, 0, 0)),
        ],
        out_specs=[
            pl.BlockSpec((step * groups * piece, width), lambda s: (s, 0)),
            pl.BlockSpec((rank, width), lambda s: (0, 0)),
            pl.BlockSpec((rank, width), lambda s: (0, 0)),
        ],
        out_shape=[
            jax.ShapeDtypeStruct((slots * groups * piece, width), jnp.bfloat16),
            jax.ShapeDtypeStruct((rank, width), jnp.float32),
            jax.ShapeDtypeStruct((rank, width), jnp.float32),
        ],
        compiler_params=pltpu.CompilerParams(vmem_limit_bytes=SMALL_LIMIT),
        name="unfold",
    )(arrived, arrived)


def body(
    attention_slot_outputs,
    output_gradient_rows,
    output_weight,
    down_weight,
    up_weight,
    assign,
    counts,
):
    groups = counts.shape[0]
    rows = assign.shape[0]
    rows_here = output_gradient_rows.shape[0] // ROW_TOKENS
    slot_cap = attention_slot_outputs.shape[0] // ROW_TOKENS
    width_here = output_gradient_rows.shape[1]
    rank = up_weight.shape[0]
    tp = lax.axis_size("tp")
    piece = ROW_TOKENS // groups
    own_group = lax.axis_index("group")
    group_ids = jnp.arange(groups, dtype=jnp.int32)
    onehot = (assign[:, None] == group_ids[None, :]).astype(jnp.int32)
    before = jnp.cumsum(onehot, axis=0) - onehot
    order_in = jnp.sum(before * onehot, axis=1)
    free_slots = jnp.sum(onehot * counts[None, :], axis=1)
    position = slot_cap - free_slots + order_in
    own_dest = lax.dynamic_slice_in_dim(assign, own_group * rows_here, rows_here)
    scale_factor = adapter_scale / math.sqrt(rows * ROW_TOKENS)

    index = lax.axis_index("tp")
    chips = tp // 2
    y, core = index // 2, index % 2

    def move(value, n):
        pairs = [(2 * a + b, 2 * ((a + n) % chips) + b) for a in range(chips) for b in range(2)]
        return lax.ppermute(value, "tp", pairs)

    def swap(value):
        return lax.ppermute(value, "tp", [(i, i ^ 1) for i in range(tp)])

    pieces_out, parts = prepare(
        groups, output_gradient_rows, attention_slot_outputs, up_weight, down_weight.T
    )
    spread = lax.all_to_all(
        pieces_out.reshape(groups, rows_here, piece, width_here),
        "group",
        split_axis=0,
        concat_axis=0,
        tiled=True,
    ).reshape(rows * piece, width_here)

    slot_ids = jnp.arange(slot_cap, dtype=jnp.int32)
    row_ids = jnp.arange(rows_here, dtype=jnp.int32)
    row_position = position.reshape(groups, rows_here)
    hit_row = assign.reshape(groups, rows_here) == own_group
    low_pick = jnp.max(jnp.where(own_dest[None, :] == group_ids[:, None], row_ids, -1), axis=1)
    projected_pick = jnp.max(jnp.where(hit_row, rows_here + row_position, -1), axis=1)
    slot_match = hit_row[:, :, None] & (row_position[:, :, None] == slot_ids)
    slot_source = jnp.max(jnp.where(slot_match, group_ids[:, None, None], -1), axis=(0, 1))
    owners = []
    for step in (0, chips - 1, 1, 2):
        pair = 2 * lax.rem(y + step, chips)
        owners += [pair + core, pair + 1 - core]
    pieces = [
        assign, position, jnp.stack([low_pick, projected_pick], axis=1).reshape(-1), slot_source,
        own_dest, jnp.stack(owners + [core]).astype(jnp.int32),
    ]
    at = [0]
    for part in pieces:
        at.append(at[-1] + part.shape[0])
    _, _, pick_at, source_at, dest_at, owner_at, end = at
    table = jnp.concatenate(pieces)

    parts = parts + swap(parts)
    share = lax.dynamic_slice_in_dim(parts, core * (rank // 2), rank // 2, axis=0)
    share = share + move(share, 1) + move(share, -1) + move(share, 2)

    send = rank_sums_to_send(table, pick_at, groups, rows_here, share)
    crossed = lax.all_to_all(send, "group", split_axis=0, concat_axis=0, tiled=True)

    left, right = move(spread, 1), move(spread, -1)
    other = swap(spread)
    sums, done = block_products(
        table, [owner_at, owner_at + 1], [spread, other], output_weight, send,
        name="own_products",
    )
    (crossed,) = after([crossed], done)
    crossed_other = swap(crossed)
    partial_grads, done = gradient_products(
        table, end - 1, source_at, dest_at, crossed, crossed_other, done, attention_slot_outputs,
        output_gradient_rows,
    )
    left_top, right_bottom, left, right, partial_grads = take_halves(
        left, right, partial_grads, done
    )
    far = [move(left_top, 1), move(right_bottom, -1)]
    share_rows = 2 * rank // groups
    grads = lax.all_to_all(
        partial_grads.reshape(groups, share_rows, width_here), "group", split_axis=0, concat_axis=0,
        tiled=True,
    )
    sums, done = block_products(
        table, [owner_at + i for i in range(2, 6)], [left, swap(left), right, swap(right)],
        output_weight, done, sums, name="side_products",
    )
    far = after(far, done)
    placed = last_products(
        rows, scale_factor, table, [owner_at + 6, owner_at + 7], end - 1, far,
        [swap(part) for part in far], grads, (crossed, crossed_other), output_weight, sums,
        down_weight.T, slot_cap,
    )

    arrived = lax.all_to_all(placed, "group", split_axis=0, concat_axis=0, tiled=True)
    attention_gradient, down_gradient, up_gradient = unfold(arrived, slot_cap)
    return attention_gradient, down_gradient.T, up_gradient


def solution(mesh):
    in_specs = (
        P("group", "tp"),
        P("group", "tp"),
        P("tp", None),
        P("tp", None),
        P(None, "tp"),
        P(),
        P(),
    )
    out_specs = (P("group", "tp"), P("tp", None), P(None, "tp"))
    return jax.shard_map(body, mesh=mesh, in_specs=in_specs, out_specs=out_specs, check_vma=False)
```

```python
import functools
import math

import jax
import jax.numpy as jnp
from jax import lax
from jax.experimental import pallas as pl
from jax.experimental.pallas import tpu as pltpu
from jax.sharding import PartitionSpec as P

ROW_TOKENS = 128
LANES = 128
VMEM_LIMIT = 44 * 2**20
BASE_ROOM = 16
SMALL_LIMIT = 18 * 2**20


adapter_scale = 2.0

ANY = pl.BlockSpec(memory_space=pl.ANY)
HBM = pl.BlockSpec(memory_space=pltpu.HBM)
VMEM = pl.BlockSpec(memory_space=pltpu.VMEM)
SMEM = pl.BlockSpec(memory_space=pltpu.SMEM)


def dot_minor(left, right):
    return lax.dot_general(
        left, right, (((1,), (1,)), ((), ())), preferred_element_type=jnp.float32
    )


def prepare_kernel(
    groups, gradient, attention, up, down, pieces, parts, rows_in, slots_in, sem
):
    loads = [
        pltpu.make_async_copy(gradient, rows_in, sem.at[0]),
        pltpu.make_async_copy(attention, slots_in, sem.at[1]),
    ]
    for load in loads:
        load.start()
    tokens = rows_in.shape[0]
    rows_here, piece = tokens // ROW_TOKENS, ROW_TOKENS // groups
    loads[0].wait()
    starts = [r * ROW_TOKENS + j * piece for j in range(groups) for r in range(rows_here)]
    for pair in range(len(starts) // 2):
        both = []
        for start in starts[2 * pair : 2 * pair + 2]:
            tile = start // (2 * piece) * 2 * piece
            value = rows_in[tile : tile + 2 * piece, :].astype(jnp.float32)
            both.append(value[start - tile : start - tile + piece])
        pieces[2 * pair * piece : 2 * (pair + 1) * piece, :] = jnp.concatenate(
            both, axis=0
        ).astype(pieces.dtype)
    parts[:, :tokens] = dot_minor(up[...], rows_in[...])
    loads[1].wait()
    parts[:, tokens:] = dot_minor(down[...], slots_in[...])


def prepare(groups, gradient, attention, up, down):
    rank = up.shape[0]
    return pl.pallas_call(
        functools.partial(prepare_kernel, groups),
        in_specs=[ANY] * 2 + [VMEM] * 2,
        out_specs=[VMEM] * 2,
        out_shape=[
            jax.ShapeDtypeStruct(gradient.shape, gradient.dtype),
            jax.ShapeDtypeStruct((rank, gradient.shape[0] + attention.shape[0]), jnp.float32),
        ],
        scratch_shapes=[
            pltpu.VMEM(gradient.shape, gradient.dtype),
            pltpu.VMEM(attention.shape, attention.dtype),
            pltpu.SemaphoreType.DMA((2,)),
        ],
        compiler_params=pltpu.CompilerParams(vmem_limit_bytes=56 * 2**20),
        name="prepare",
    )(gradient, attention, up, down)


def after_kernel(*refs):
    pass


def after(values, token):
    count = len(values)
    return pl.pallas_call(
        after_kernel,
        in_specs=[ANY] * (count + 1),
        out_specs=[ANY] * count,
        out_shape=[jax.ShapeDtypeStruct(value.shape, value.dtype) for value in values],
        input_output_aliases={i: i for i in range(count)},
        compiler_params=pltpu.CompilerParams(vmem_limit_bytes=2**20),
        name="after",
    )(*values, token)


def halves_kernel(left, right, grads, token, top, bottom, *refs):
    buffer, sem = refs[3:]
    half = top.shape[0]
    chunk = half // (buffer.shape[0] // 2)
    loads, stores = [], []
    for i in range(buffer.shape[0]):
        part, start, out = (left, 0, top) if i % 2 == 0 else (right, half, bottom)
        offset = i // 2 * chunk
        loads.append(
            pltpu.make_async_copy(part.at[pl.ds(start + offset, chunk)], buffer.at[i], sem.at[0, i])
        )
        stores.append(
            pltpu.make_async_copy(buffer.at[i], out.at[pl.ds(offset, chunk)], sem.at[1, i])
        )
    for load in loads:
        load.start()
    for load, store in zip(loads, stores):
        load.wait()
        store.start()
    for store in stores:
        store.wait()


def take_halves(left, right, grads, token):
    half = jax.ShapeDtypeStruct((left.shape[0] // 2, left.shape[1]), left.dtype)
    return pl.pallas_call(
        halves_kernel,
        in_specs=[ANY] * 4,
        out_specs=[HBM] * 2 + [ANY] * 3,
        out_shape=[half] * 2
        + [jax.ShapeDtypeStruct(part.shape, part.dtype) for part in (left, right, grads)],
        input_output_aliases={0: 2, 1: 3, 2: 4},
        scratch_shapes=[
            pltpu.VMEM((8, half.shape[0] // 4, half.shape[1]), half.dtype),
            pltpu.SemaphoreType.DMA((2, 8)),
        ],
        compiler_params=pltpu.CompilerParams(vmem_limit_bytes=SMALL_LIMIT),
        cost_estimate=pl.CostEstimate(
            flops=0, bytes_accessed=8 * left.shape[0] * left.shape[1], transcendentals=0
        ),
        name="take_halves",
    )(left, right, grads, token)


def block_kernel(table, first, index, *refs):
    refs = list(refs)
    count = len(table)
    blocks = [refs.pop(0) for _ in range(count)]
    weight, _ = refs.pop(0), refs.pop(0)
    if not first:
        sums_in = refs.pop(0)
    sums_out, done, x, w, sums, sums_was, x_sem, w_sem, sem = refs
    tokens, width = x.shape[1:]
    done[...] = jnp.zeros_like(done)
    copies = []
    for k, place in enumerate(table):
        owner = index[place]
        columns = pl.ds(pl.multiple_of(owner * width, width), width)
        copies.append([
            pltpu.make_async_copy(blocks[k], x.at[k], x_sem.at[k]),
            pltpu.make_async_copy(weight.at[:, columns], w.at[k % 4], w_sem.at[k]),
        ])
    if not first:
        copies.append([pltpu.make_async_copy(sums_in.at[pl.ds(0, tokens)], sums_was, sem.at[0])])
    for each in copies[:3]:
        for copy in each:
            copy.start()
    for k in range(count):
        for copy in copies[k]:
            copy.wait()
        if k + 3 < len(copies):
            for copy in copies[k + 3]:
                copy.start()
        if k == count - 1:
            break
        value = dot_minor(x[k], w[k % 4])
        if k > 0:
            sums[...] += value
        else:
            sums[...] = value
    if not first:
        copies[count][0].wait()
    tile = sums.shape[1] // 4
    stores = []
    for n in range(4):
        span = slice(n * tile, (n + 1) * tile)
        value = sums[:, span] + dot_minor(x[count - 1], w[(count - 1) % 4, span])
        if not first:
            value += sums_was[:, span]
        sums[:, span] = value
        stores.append(
            pltpu.make_async_copy(
                sums.at[:, pl.ds(n * tile, tile)],
                sums_out.at[pl.ds(0, tokens), pl.ds(n * tile, tile)],
                sem.at[1 + n],
            )
        )
        stores[-1].start()
    for store in stores:
        store.wait()


def block_products(index, table, blocks, weight, token, sums=None, name=""):
    count = len(blocks)
    tokens, width = blocks[0].shape
    out_width = weight.shape[0]
    first = sums is None
    return pl.pallas_call(
        functools.partial(block_kernel, table, first),
        in_specs=[SMEM] + [ANY] * (count + (2 if first else 3)),
        out_specs=[HBM, VMEM],
        out_shape=[
            jax.ShapeDtypeStruct((BASE_ROOM * tokens, out_width), jnp.float32),
            jax.ShapeDtypeStruct((8, LANES), jnp.float32),
        ],
        scratch_shapes=[
            pltpu.VMEM((count, tokens, width), jnp.bfloat16),
            pltpu.VMEM((4, out_width, width), jnp.bfloat16),
            pltpu.VMEM((tokens, out_width), jnp.float32),
            pltpu.VMEM((tokens, out_width), jnp.float32),
            pltpu.SemaphoreType.DMA((count,)),
            pltpu.SemaphoreType.DMA((count,)),
            pltpu.SemaphoreType.DMA((5,)),
        ],
        compiler_params=pltpu.CompilerParams(vmem_limit_bytes=VMEM_LIMIT),
        cost_estimate=pl.CostEstimate(
            flops=2 * count * tokens * width * out_width,
            bytes_accessed=2 * width * count * (tokens + out_width),
            transcendentals=0,
        ),
        name=name,
    )(index, *blocks, weight, token, *([] if first else [sums]))


def last_kernel(
    rows, scale, table, core_at, index, far_a, far_b, other_a, other_b, grads_in, crossed,
    crossed_other, weight, sums_in, down, out, x, w, sums, grads, pieces, low, low_rounded, x_sem,
    w_sem, sem,
):
    half, width = far_a.shape
    groups, ranks = pieces.shape[1:3]
    tokens = 2 * half
    piece = tokens // rows
    tile = 2 * LANES
    tiles = w.shape[0] // tile
    core = index[core_at]

    def load_sums(columns, semaphore):
        return pltpu.make_async_copy(
            sums_in.at[pl.ds(0, tokens), columns], sums.at[:, columns], semaphore
        )

    copies = []
    for i, part in enumerate((far_a, far_b, other_a, other_b)):
        rows_of, lanes = pl.ds((i % 2) * half, half), pl.ds((i // 2) * width, width)
        copies.append(pltpu.make_async_copy(part, x.at[rows_of, lanes], x_sem.at[i]))
    low_copies = [
        pltpu.make_async_copy(crossed.at[:, 2], pieces.at[core], sem.at[tiles]),
        pltpu.make_async_copy(crossed_other.at[:, 2], pieces.at[1 - core], sem.at[tiles + 1]),
    ]
    tile_copies = []
    for n in range(tiles):
        span = pl.ds(n * tile, tile)
        each = []
        for k in range(2):
            columns = pl.ds(pl.multiple_of(index[table[k]] * width, width), width)
            lanes = pl.ds(k * width, width)
            each.append(
                pltpu.make_async_copy(weight.at[span, columns], w.at[span, lanes], w_sem.at[n, k])
            )
        each.append(load_sums(span, sem.at[n]))
        tile_copies.append(each)
    load_grads = pltpu.make_async_copy(grads_in, grads, sem.at[tiles + 2])
    for each in [low_copies, copies, tile_copies[0]]:
        for copy in each:
            copy.start()
    out[...] = jnp.zeros_like(out)
    for copy in low_copies:
        copy.wait()
    share = tokens // groups
    for group in range(groups):
        both = jnp.concatenate([pieces[0, group], pieces[1, group]], axis=0).astype(jnp.float32)
        low[group * share : (group + 1) * share] = both.T[:share]
    low_rounded[...] = low[...].astype(jnp.bfloat16)
    for each in tile_copies[1:] + [[load_grads]]:
        for copy in each:
            copy.start()
    for copy in copies:
        copy.wait()
    for n in range(tiles):
        span = slice(n * tile, (n + 1) * tile)
        for copy in tile_copies[n]:
            copy.wait()
        total = sums[:, span] + dot_minor(x[...], w[span])
        total += adapter_scale * jnp.dot(
            low_rounded[...], down[:, span], preferred_element_type=jnp.float32
        )
        for row in range(rows):
            mine = total[row * piece : (row + 1) * piece]
            folded = jnp.concatenate([mine[:, :LANES], mine[:, LANES:]], axis=0)
            out[index[row], index[rows + row], :, n * LANES : (n + 1) * LANES] = folded.astype(
                jnp.bfloat16
            )
    load_grads.wait()
    total = scale * jnp.sum(grads[...], axis=0)
    folded = jnp.concatenate([total[:, : width // 2], total[:, width // 2 :]], axis=0)
    folded = folded.astype(jnp.bfloat16)
    for group in range(out.shape[0]):
        out[group, out.shape[1] - 1] = folded


def last_products(
    rows, scale, index, table, core_at, far, other, grads, crossed, weight, sums, down, slots
):
    half, width = far[0].shape
    tokens = 2 * half
    rank, out_width = down.shape
    groups = crossed[0].shape[0]
    piece = tokens // rows
    tiles = out_width // (2 * LANES)
    return pl.pallas_call(
        functools.partial(last_kernel, rows, scale, table, core_at),
        in_specs=[SMEM] + [ANY] * 9 + [VMEM],
        out_specs=VMEM,
        scratch_shapes=[
            pltpu.VMEM((tokens, 2 * width), jnp.bfloat16),
            pltpu.VMEM((out_width, 2 * width), jnp.bfloat16),
            pltpu.VMEM((tokens, out_width), jnp.float32),
            pltpu.VMEM(grads.shape, grads.dtype),
            pltpu.VMEM((2, groups, rank // 2, LANES), jnp.bfloat16),
            pltpu.VMEM((tokens, rank), jnp.float32),
            pltpu.VMEM((tokens, rank), jnp.bfloat16),
            pltpu.SemaphoreType.DMA((4,)),
            pltpu.SemaphoreType.DMA((tiles, 2)),
            pltpu.SemaphoreType.DMA((tiles + 3,)),
        ],
        out_shape=jax.ShapeDtypeStruct(
            (groups, slots + 1, 2 * piece, out_width // 2), jnp.bfloat16
        ),
        compiler_params=pltpu.CompilerParams(vmem_limit_bytes=VMEM_LIMIT),
        cost_estimate=pl.CostEstimate(
            flops=4 * tokens * width * out_width,
            bytes_accessed=4 * width * tokens + 8 * tokens * out_width,
            transcendentals=0,
        ),
        name="last_products",
    )(index, *far, *other, grads, *crossed, weight, sums, down)


def send_kernel(groups, rows_here, pick_at, index, share, out):
    piece = ROW_TOKENS // groups
    lane = lax.broadcasted_iota(jnp.int32, (share.shape[0], ROW_TOKENS), 1)
    for group in range(groups):
        for kind in range(2):
            pick = index[pick_at + 2 * group + kind]
            lanes = pl.ds(pl.multiple_of(jnp.maximum(pick, 0) * ROW_TOKENS, ROW_TOKENS), ROW_TOKENS)
            keep = (pick >= 0).astype(jnp.float32)
            out[group, kind] = (share[:, lanes] * keep).astype(jnp.bfloat16)
        value = jnp.zeros(lane.shape, jnp.float32)
        for r in range(rows_here):
            shift = (r - group) * piece % ROW_TOKENS
            row = share[:, r * ROW_TOKENS : (r + 1) * ROW_TOKENS]
            if shift:
                row = pltpu.roll(row, shift, 1)
            value = jnp.where(lane // piece == r, row, value)
        out[group, 2] = value.astype(jnp.bfloat16)


def rank_sums_to_send(index, pick_at, groups, rows_here, share):
    half = share.shape[0]
    return pl.pallas_call(
        functools.partial(send_kernel, groups, rows_here, pick_at),
        in_specs=[SMEM, VMEM],
        out_specs=VMEM,
        out_shape=jax.ShapeDtypeStruct((groups, 3, half, ROW_TOKENS), jnp.bfloat16),
        compiler_params=pltpu.CompilerParams(vmem_limit_bytes=SMALL_LIMIT),
        cost_estimate=pl.CostEstimate(
            flops=2 * groups * half * ROW_TOKENS, bytes_accessed=8 * groups * half * ROW_TOKENS,
            transcendentals=0,
        ),
        name="rank_sums_to_send",
    )(index, share)


def gradient_kernel(
    core_at, source_at, dest_at, index, crossed, crossed_other, token, attention, gradient, out,
    done, parts, low, projected, sums, tokens, more, sem,
):
    half = crossed.shape[2]
    rank = 2 * half
    core = index[core_at]
    part_copies = [
        pltpu.make_async_copy(part.at[:, pl.ds(0, 2)], parts.at[i], sem.at[3 + i])
        for i, part in enumerate((crossed, crossed_other))
    ]
    copies = [
        pltpu.make_async_copy(attention, tokens, sem.at[0]),
        pltpu.make_async_copy(gradient, more, sem.at[1]),
    ]
    for copy in part_copies + copies:
        copy.start()
    for copy in part_copies:
        copy.wait()
    halves = [
        (pl.ds(pl.multiple_of(owner * half, half), half), parts.at[i])
        for i, owner in enumerate((core, 1 - core))
    ]
    for s in range(tokens.shape[0] // ROW_TOKENS):
        source = index[source_at + s]
        keep = (source >= 0).astype(jnp.float32)
        for ranks, part in halves:
            value = part[jnp.maximum(source, 0), 0].astype(jnp.float32) * keep
            low[ranks, s * ROW_TOKENS : (s + 1) * ROW_TOKENS] = value.astype(jnp.bfloat16)
    for r in range(more.shape[0] // ROW_TOKENS):
        for ranks, part in halves:
            projected[ranks, r * ROW_TOKENS : (r + 1) * ROW_TOKENS] = part[index[dest_at + r], 1]
    copies[0].wait()
    sums[:rank] = jnp.dot(low[...], tokens[...], preferred_element_type=jnp.float32)
    copies[1].wait()
    sums[rank:] = jnp.dot(projected[...], more[...], preferred_element_type=jnp.float32)
    done[...] = jnp.zeros_like(done)
    store = pltpu.make_async_copy(sums, out, sem.at[2])
    store.start()
    store.wait()


def gradient_products(
    index, core_at, source_at, dest_at, crossed, other, token, attention, gradient
):
    rank = 2 * crossed.shape[2]
    slot_tokens, width = attention.shape
    row_tokens = gradient.shape[0]
    return pl.pallas_call(
        functools.partial(gradient_kernel, core_at, source_at, dest_at),
        in_specs=[SMEM] + [ANY] * 5,
        out_specs=[HBM, VMEM],
        out_shape=[
            jax.ShapeDtypeStruct((2 * rank, width), jnp.float32),
            jax.ShapeDtypeStruct((8, LANES), jnp.float32),
        ],
        scratch_shapes=[
            pltpu.VMEM((2, crossed.shape[0], 2) + crossed.shape[2:], jnp.bfloat16),
            pltpu.VMEM((rank, slot_tokens), jnp.bfloat16),
            pltpu.VMEM((rank, row_tokens), jnp.bfloat16),
            pltpu.VMEM((2 * rank, width), jnp.float32),
            pltpu.VMEM(attention.shape, jnp.bfloat16),
            pltpu.VMEM(gradient.shape, jnp.bfloat16),
            pltpu.SemaphoreType.DMA((5,)),
        ],
        compiler_params=pltpu.CompilerParams(vmem_limit_bytes=SMALL_LIMIT),
        cost_estimate=pl.CostEstimate(
            flops=2 * rank * width * (slot_tokens + row_tokens),
            bytes_accessed=2 * width * (slot_tokens + row_tokens),
            transcendentals=0,
        ),
        name="gradient_products",
    )(index, crossed, other, token, attention, gradient)


def unfold_kernel(arrived, gradients, out, down_gradient, up_gradient):
    groups, slots, folded, half_width = arrived.shape
    piece = folded // 2
    for slot in range(slots):
        for pair in range(groups // 2):
            halves = []
            for j in (2 * pair, 2 * pair + 1):
                value = arrived[j, slot].astype(jnp.float32)
                pieces = []
                for n in range(half_width // LANES):
                    lanes = slice(n * LANES, (n + 1) * LANES)
                    pieces += [value[:piece, lanes], value[piece:, lanes]]
                halves.append(jnp.concatenate(pieces, axis=1))
            rows = pl.ds(slot * groups * piece + pair * folded, folded)
            out[rows, :] = jnp.concatenate(halves, axis=0).astype(out.dtype)

    @pl.when(pl.program_id(0) == 0)
    def _():
        values = []
        for j in range(groups):
            value = gradients[j, 0].astype(jnp.float32)
            values.append(jnp.concatenate([value[:piece], value[piece:]], axis=1))
        down_gradient[...] = jnp.concatenate(values[: groups // 2], axis=0)
        up_gradient[...] = jnp.concatenate(values[groups // 2 :], axis=0)


def unfold(arrived, slots):
    groups, _, folded, half_width = arrived.shape
    piece, width = folded // 2, 2 * half_width
    rank = groups * piece // 2
    step = slots // 2
    return pl.pallas_call(
        unfold_kernel,
        grid=(slots // step,),
        in_specs=[
            pl.BlockSpec((groups, step, folded, half_width), lambda s: (0, s, 0, 0)),
            pl.BlockSpec((groups, 1, folded, half_width), lambda s: (0, slots, 0, 0)),
        ],
        out_specs=[
            pl.BlockSpec((step * groups * piece, width), lambda s: (s, 0)),
            pl.BlockSpec((rank, width), lambda s: (0, 0)),
            pl.BlockSpec((rank, width), lambda s: (0, 0)),
        ],
        out_shape=[
            jax.ShapeDtypeStruct((slots * groups * piece, width), jnp.bfloat16),
            jax.ShapeDtypeStruct((rank, width), jnp.float32),
            jax.ShapeDtypeStruct((rank, width), jnp.float32),
        ],
        compiler_params=pltpu.CompilerParams(vmem_limit_bytes=SMALL_LIMIT),
        name="unfold",
    )(arrived, arrived)


def body(
    attention_slot_outputs,
    output_gradient_rows,
    output_weight,
    down_weight,
    up_weight,
    assign,
    counts,
):
    groups = counts.shape[0]
    rows = assign.shape[0]
    rows_here = output_gradient_rows.shape[0] // ROW_TOKENS
    slot_cap = attention_slot_outputs.shape[0] // ROW_TOKENS
    width_here = output_gradient_rows.shape[1]
    rank = up_weight.shape[0]
    tp = lax.axis_size("tp")
    piece = ROW_TOKENS // groups
    own_group = lax.axis_index("group")
    group_ids = jnp.arange(groups, dtype=jnp.int32)
    onehot = (assign[:, None] == group_ids[None, :]).astype(jnp.int32)
    before = jnp.cumsum(onehot, axis=0) - onehot
    order_in = jnp.sum(before * onehot, axis=1)
    free_slots = jnp.sum(onehot * counts[None, :], axis=1)
    position = slot_cap - free_slots + order_in
    own_dest = lax.dynamic_slice_in_dim(assign, own_group * rows_here, rows_here)
    scale_factor = adapter_scale / math.sqrt(rows * ROW_TOKENS)

    index = lax.axis_index("tp")
    chips = tp // 2
    y, core = index // 2, index % 2

    def move(value, n):
        pairs = [(2 * a + b, 2 * ((a + n) % chips) + b) for a in range(chips) for b in range(2)]
        return lax.ppermute(value, "tp", pairs)

    def swap(value):
        return lax.ppermute(value, "tp", [(i, i ^ 1) for i in range(tp)])

    pieces_out, parts = prepare(
        groups, output_gradient_rows, attention_slot_outputs, up_weight, down_weight.T
    )
    spread = lax.all_to_all(
        pieces_out.reshape(groups, rows_here, piece, width_here),
        "group",
        split_axis=0,
        concat_axis=0,
        tiled=True,
    ).reshape(rows * piece, width_here)

    slot_ids = jnp.arange(slot_cap, dtype=jnp.int32)
    row_ids = jnp.arange(rows_here, dtype=jnp.int32)
    row_position = position.reshape(groups, rows_here)
    hit_row = assign.reshape(groups, rows_here) == own_group
    low_pick = jnp.max(jnp.where(own_dest[None, :] == group_ids[:, None], row_ids, -1), axis=1)
    projected_pick = jnp.max(jnp.where(hit_row, rows_here + row_position, -1), axis=1)
    slot_match = hit_row[:, :, None] & (row_position[:, :, None] == slot_ids)
    slot_source = jnp.max(jnp.where(slot_match, group_ids[:, None, None], -1), axis=(0, 1))
    owners = []
    for step in (0, chips - 1, 1, 2):
        pair = 2 * lax.rem(y + step, chips)
        owners += [pair + core, pair + 1 - core]
    pieces = [
        assign, position, jnp.stack([low_pick, projected_pick], axis=1).reshape(-1), slot_source,
        own_dest, jnp.stack(owners + [core]).astype(jnp.int32),
    ]
    at = [0]
    for part in pieces:
        at.append(at[-1] + part.shape[0])
    _, _, pick_at, source_at, dest_at, owner_at, end = at
    table = jnp.concatenate(pieces)

    parts = parts + swap(parts)
    share = lax.dynamic_slice_in_dim(parts, core * (rank // 2), rank // 2, axis=0)
    share = share + move(share, 1) + move(share, -1) + move(share, 2)

    send = rank_sums_to_send(table, pick_at, groups, rows_here, share)
    crossed = lax.all_to_all(send, "group", split_axis=0, concat_axis=0, tiled=True)

    left, right = move(spread, 1), move(spread, -1)
    other = swap(spread)
    sums, done = block_products(
        table, [owner_at, owner_at + 1], [spread, other], output_weight, send,
        name="own_products",
    )
    (crossed,) = after([crossed], done)
    crossed_other = swap(crossed)
    partial_grads, done = gradient_products(
        table, end - 1, source_at, dest_at, crossed, crossed_other, done, attention_slot_outputs,
        output_gradient_rows,
    )
    left_top, right_bottom, left, right, partial_grads = take_halves(
        left, right, partial_grads, done
    )
    far = [move(left_top, 1), move(right_bottom, -1)]
    share_rows = 2 * rank // groups
    grads = lax.all_to_all(
        partial_grads.reshape(groups, share_rows, width_here), "group", split_axis=0, concat_axis=0,
        tiled=True,
    )
    sums, done = block_products(
        table, [owner_at + i for i in range(2, 6)], [left, swap(left), right, swap(right)],
        output_weight, done, sums, name="side_products",
    )
    far = after(far, done)
    placed = last_products(
        rows, scale_factor, table, [owner_at + 6, owner_at + 7], end - 1, far,
        [swap(part) for part in far], grads, (crossed, crossed_other), output_weight, sums,
        down_weight.T, slot_cap,
    )

    arrived = lax.all_to_all(placed, "group", split_axis=0, concat_axis=0, tiled=True)
    attention_gradient, down_gradient, up_gradient = unfold(arrived, slot_cap)
    return attention_gradient, down_gradient.T, up_gradient


def solution(mesh):
    in_specs = (
        P("group", "tp"),
        P("group", "tp"),
        P("tp", None),
        P("tp", None),
        P(None, "tp"),
        P(),
        P(),
    )
    out_specs = (P("group", "tp"), P("tp", None), P(None, "tp"))
    return jax.shard_map(body, mesh=mesh, in_specs=in_specs, out_specs=out_specs, check_vma=False)
```

```python
import functools
import math

import jax
import jax.numpy as jnp
from jax import lax
from jax.experimental import pallas as pl
from jax.experimental.pallas import tpu as pltpu
from jax.sharding import PartitionSpec as P

ROW_TOKENS = 128
LANES = 128
VMEM_LIMIT = 44 * 2**20
BASE_ROOM = 16
SMALL_LIMIT = 18 * 2**20


adapter_scale = 2.0

ANY = pl.BlockSpec(memory_space=pl.ANY)
HBM = pl.BlockSpec(memory_space=pltpu.HBM)
VMEM = pl.BlockSpec(memory_space=pltpu.VMEM)
SMEM = pl.BlockSpec(memory_space=pltpu.SMEM)


def dot_minor(left, right):
    return lax.dot_general(
        left, right, (((1,), (1,)), ((), ())), preferred_element_type=jnp.float32
    )


def prepare_kernel(
    groups, gradient, attention, up, down, pieces, parts, rows_in, slots_in, sem
):
    loads = [
        pltpu.make_async_copy(gradient, rows_in, sem.at[0]),
        pltpu.make_async_copy(attention, slots_in, sem.at[1]),
    ]
    for load in loads:
        load.start()
    tokens = rows_in.shape[0]
    rows_here, piece = tokens // ROW_TOKENS, ROW_TOKENS // groups
    loads[0].wait()
    starts = [r * ROW_TOKENS + j * piece for j in range(groups) for r in range(rows_here)]
    for pair in range(len(starts) // 2):
        both = []
        for start in starts[2 * pair : 2 * pair + 2]:
            tile = start // (2 * piece) * 2 * piece
            value = rows_in[tile : tile + 2 * piece, :].astype(jnp.float32)
            both.append(value[start - tile : start - tile + piece])
        pieces[2 * pair * piece : 2 * (pair + 1) * piece, :] = jnp.concatenate(
            both, axis=0
        ).astype(pieces.dtype)
    parts[:, :tokens] = dot_minor(rows_in[...], up[...]).T
    loads[1].wait()
    parts[:, tokens:] = dot_minor(slots_in[...], down[...]).T


def prepare(groups, gradient, attention, up, down):
    rank = up.shape[0]
    return pl.pallas_call(
        functools.partial(prepare_kernel, groups),
        in_specs=[ANY] * 2 + [VMEM] * 2,
        out_specs=[VMEM] * 2,
        out_shape=[
            jax.ShapeDtypeStruct(gradient.shape, gradient.dtype),
            jax.ShapeDtypeStruct((rank, gradient.shape[0] + attention.shape[0]), jnp.float32),
        ],
        scratch_shapes=[
            pltpu.VMEM(gradient.shape, gradient.dtype),
            pltpu.VMEM(attention.shape, attention.dtype),
            pltpu.SemaphoreType.DMA((2,)),
        ],
        compiler_params=pltpu.CompilerParams(vmem_limit_bytes=56 * 2**20),
        name="prepare",
    )(gradient, attention, up, down)


def after_kernel(*refs):
    pass


def after(values, token):
    count = len(values)
    return pl.pallas_call(
        after_kernel,
        in_specs=[ANY] * (count + 1),
        out_specs=[ANY] * count,
        out_shape=[jax.ShapeDtypeStruct(value.shape, value.dtype) for value in values],
        input_output_aliases={i: i for i in range(count)},
        compiler_params=pltpu.CompilerParams(vmem_limit_bytes=2**20),
        name="after",
    )(*values, token)


def halves_kernel(left, right, grads, token, top, bottom, *refs):
    buffer, sem = refs[3:]
    half = top.shape[0]
    chunk = half // (buffer.shape[0] // 2)
    loads, stores = [], []
    for i in range(buffer.shape[0]):
        part, start, out = (left, 0, top) if i % 2 == 0 else (right, half, bottom)
        offset = i // 2 * chunk
        loads.append(
            pltpu.make_async_copy(part.at[pl.ds(start + offset, chunk)], buffer.at[i], sem.at[0, i])
        )
        stores.append(
            pltpu.make_async_copy(buffer.at[i], out.at[pl.ds(offset, chunk)], sem.at[1, i])
        )
    for load in loads:
        load.start()
    for load, store in zip(loads, stores):
        load.wait()
        store.start()
    for store in stores:
        store.wait()


def take_halves(left, right, grads, token):
    half = jax.ShapeDtypeStruct((left.shape[0] // 2, left.shape[1]), left.dtype)
    return pl.pallas_call(
        halves_kernel,
        in_specs=[ANY] * 4,
        out_specs=[HBM] * 2 + [ANY] * 3,
        out_shape=[half] * 2
        + [jax.ShapeDtypeStruct(part.shape, part.dtype) for part in (left, right, grads)],
        input_output_aliases={0: 2, 1: 3, 2: 4},
        scratch_shapes=[
            pltpu.VMEM((8, half.shape[0] // 4, half.shape[1]), half.dtype),
            pltpu.SemaphoreType.DMA((2, 8)),
        ],
        compiler_params=pltpu.CompilerParams(vmem_limit_bytes=SMALL_LIMIT),
        cost_estimate=pl.CostEstimate(
            flops=0, bytes_accessed=8 * left.shape[0] * left.shape[1], transcendentals=0
        ),
        name="take_halves",
    )(left, right, grads, token)


def block_kernel(table, first, index, *refs):
    refs = list(refs)
    count = len(table)
    blocks = [refs.pop(0) for _ in range(count)]
    weight, _ = refs.pop(0), refs.pop(0)
    if not first:
        sums_in = refs.pop(0)
    sums_out, done, x, w, sums, sums_was, x_sem, w_sem, sem = refs
    tokens, width = x.shape[1:]
    done[...] = jnp.zeros_like(done)
    copies = []
    for k, place in enumerate(table):
        owner = index[place]
        columns = pl.ds(pl.multiple_of(owner * width, width), width)
        copies.append([
            pltpu.make_async_copy(blocks[k], x.at[k], x_sem.at[k]),
            pltpu.make_async_copy(weight.at[:, columns], w.at[k % 4], w_sem.at[k]),
        ])
    if not first:
        copies.append([pltpu.make_async_copy(sums_in.at[pl.ds(0, tokens)], sums_was, sem.at[0])])
    for each in copies[:3]:
        for copy in each:
            copy.start()
    for k in range(count):
        for copy in copies[k]:
            copy.wait()
        if k + 3 < len(copies):
            for copy in copies[k + 3]:
                copy.start()
        if k == count - 1:
            break
        value = dot_minor(x[k], w[k % 4])
        if k > 0:
            sums[...] += value
        else:
            sums[...] = value
    if not first:
        copies[count][0].wait()
    tile = sums.shape[1] // 4
    stores = []
    for n in range(4):
        span = slice(n * tile, (n + 1) * tile)
        value = sums[:, span] + dot_minor(x[count - 1], w[(count - 1) % 4, span])
        if not first:
            value += sums_was[:, span]
        sums[:, span] = value
        stores.append(
            pltpu.make_async_copy(
                sums.at[:, pl.ds(n * tile, tile)],
                sums_out.at[pl.ds(0, tokens), pl.ds(n * tile, tile)],
                sem.at[1 + n],
            )
        )
        stores[-1].start()
    for store in stores:
        store.wait()


def block_products(index, table, blocks, weight, token, sums=None, name=""):
    count = len(blocks)
    tokens, width = blocks[0].shape
    out_width = weight.shape[0]
    first = sums is None
    return pl.pallas_call(
        functools.partial(block_kernel, table, first),
        in_specs=[SMEM] + [ANY] * (count + (2 if first else 3)),
        out_specs=[HBM, VMEM],
        out_shape=[
            jax.ShapeDtypeStruct((BASE_ROOM * tokens, out_width), jnp.float32),
            jax.ShapeDtypeStruct((8, LANES), jnp.float32),
        ],
        scratch_shapes=[
            pltpu.VMEM((count, tokens, width), jnp.bfloat16),
            pltpu.VMEM((4, out_width, width), jnp.bfloat16),
            pltpu.VMEM((tokens, out_width), jnp.float32),
            pltpu.VMEM((tokens, out_width), jnp.float32),
            pltpu.SemaphoreType.DMA((count,)),
            pltpu.SemaphoreType.DMA((count,)),
            pltpu.SemaphoreType.DMA((5,)),
        ],
        compiler_params=pltpu.CompilerParams(vmem_limit_bytes=VMEM_LIMIT),
        cost_estimate=pl.CostEstimate(
            flops=2 * count * tokens * width * out_width,
            bytes_accessed=2 * width * count * (tokens + out_width),
            transcendentals=0,
        ),
        name=name,
    )(index, *blocks, weight, token, *([] if first else [sums]))


def last_kernel(
    rows, scale, table, core_at, index, far_a, far_b, other_a, other_b, grads_in, crossed,
    crossed_other, weight, sums_in, down, out, x, w, sums, grads, pieces, low, low_rounded, x_sem,
    w_sem, sem,
):
    half, width = far_a.shape
    groups, ranks = pieces.shape[1:3]
    tokens = 2 * half
    piece = tokens // rows
    tile = 2 * LANES
    tiles = w.shape[0] // tile
    core = index[core_at]

    def load_sums(columns, semaphore):
        return pltpu.make_async_copy(
            sums_in.at[pl.ds(0, tokens), columns], sums.at[:, columns], semaphore
        )

    copies = []
    for i, part in enumerate((far_a, far_b, other_a, other_b)):
        rows_of, lanes = pl.ds((i % 2) * half, half), pl.ds((i // 2) * width, width)
        copies.append(pltpu.make_async_copy(part, x.at[rows_of, lanes], x_sem.at[i]))
    low_copies = [
        pltpu.make_async_copy(crossed.at[:, 2], pieces.at[core], sem.at[tiles]),
        pltpu.make_async_copy(crossed_other.at[:, 2], pieces.at[1 - core], sem.at[tiles + 1]),
    ]
    tile_copies = []
    for n in range(tiles):
        span = pl.ds(n * tile, tile)
        each = []
        for k in range(2):
            columns = pl.ds(pl.multiple_of(index[table[k]] * width, width), width)
            lanes = pl.ds(k * width, width)
            each.append(
                pltpu.make_async_copy(weight.at[span, columns], w.at[span, lanes], w_sem.at[n, k])
            )
        each.append(load_sums(span, sem.at[n]))
        tile_copies.append(each)
    load_grads = pltpu.make_async_copy(grads_in, grads, sem.at[tiles + 2])
    for each in [low_copies, copies, tile_copies[0]]:
        for copy in each:
            copy.start()
    out[...] = jnp.zeros_like(out)
    for copy in low_copies:
        copy.wait()
    share = tokens // groups
    for group in range(groups):
        both = jnp.concatenate([pieces[0, group], pieces[1, group]], axis=0).astype(jnp.float32)
        low[group * share : (group + 1) * share] = both.T[:share]
    low_rounded[...] = low[...].astype(jnp.bfloat16)
    for each in tile_copies[1:] + [[load_grads]]:
        for copy in each:
            copy.start()
    for copy in copies:
        copy.wait()
    for n in range(tiles):
        span = slice(n * tile, (n + 1) * tile)
        for copy in tile_copies[n]:
            copy.wait()
        total = sums[:, span] + dot_minor(x[...], w[span])
        total += adapter_scale * jnp.dot(
            low_rounded[...], down[:, span], preferred_element_type=jnp.float32
        )
        for row in range(rows):
            mine = total[row * piece : (row + 1) * piece]
            folded = jnp.concatenate([mine[:, :LANES], mine[:, LANES:]], axis=0)
            out[index[row], index[rows + row], :, n * LANES : (n + 1) * LANES] = folded.astype(
                jnp.bfloat16
            )
    load_grads.wait()
    total = scale * jnp.sum(grads[...], axis=0)
    folded = jnp.concatenate([total[:, : width // 2], total[:, width // 2 :]], axis=0)
    folded = folded.astype(jnp.bfloat16)
    for group in range(out.shape[0]):
        out[group, out.shape[1] - 1] = folded


def last_products(
    rows, scale, index, table, core_at, far, other, grads, crossed, weight, sums, down, slots
):
    half, width = far[0].shape
    tokens = 2 * half
    rank, out_width = down.shape
    groups = crossed[0].shape[0]
    piece = tokens // rows
    tiles = out_width // (2 * LANES)
    return pl.pallas_call(
        functools.partial(last_kernel, rows, scale, table, core_at),
        in_specs=[SMEM] + [ANY] * 9 + [VMEM],
        out_specs=VMEM,
        scratch_shapes=[
            pltpu.VMEM((tokens, 2 * width), jnp.bfloat16),
            pltpu.VMEM((out_width, 2 * width), jnp.bfloat16),
            pltpu.VMEM((tokens, out_width), jnp.float32),
            pltpu.VMEM(grads.shape, grads.dtype),
            pltpu.VMEM((2, groups, rank // 2, LANES), jnp.bfloat16),
            pltpu.VMEM((tokens, rank), jnp.float32),
            pltpu.VMEM((tokens, rank), jnp.bfloat16),
            pltpu.SemaphoreType.DMA((4,)),
            pltpu.SemaphoreType.DMA((tiles, 2)),
            pltpu.SemaphoreType.DMA((tiles + 3,)),
        ],
        out_shape=jax.ShapeDtypeStruct(
            (groups, slots + 1, 2 * piece, out_width // 2), jnp.bfloat16
        ),
        compiler_params=pltpu.CompilerParams(vmem_limit_bytes=VMEM_LIMIT),
        cost_estimate=pl.CostEstimate(
            flops=4 * tokens * width * out_width,
            bytes_accessed=4 * width * tokens + 8 * tokens * out_width,
            transcendentals=0,
        ),
        name="last_products",
    )(index, *far, *other, grads, *crossed, weight, sums, down)


def send_kernel(groups, rows_here, pick_at, index, share, out):
    piece = ROW_TOKENS // groups
    lane = lax.broadcasted_iota(jnp.int32, (share.shape[0], ROW_TOKENS), 1)
    for group in range(groups):
        for kind in range(2):
            pick = index[pick_at + 2 * group + kind]
            lanes = pl.ds(pl.multiple_of(jnp.maximum(pick, 0) * ROW_TOKENS, ROW_TOKENS), ROW_TOKENS)
            keep = (pick >= 0).astype(jnp.float32)
            out[group, kind] = (share[:, lanes] * keep).astype(jnp.bfloat16)
        value = jnp.zeros(lane.shape, jnp.float32)
        for r in range(rows_here):
            shift = (r - group) * piece % ROW_TOKENS
            row = share[:, r * ROW_TOKENS : (r + 1) * ROW_TOKENS]
            if shift:
                row = pltpu.roll(row, shift, 1)
            value = jnp.where(lane // piece == r, row, value)
        out[group, 2] = value.astype(jnp.bfloat16)


def rank_sums_to_send(index, pick_at, groups, rows_here, share):
    half = share.shape[0]
    return pl.pallas_call(
        functools.partial(send_kernel, groups, rows_here, pick_at),
        in_specs=[SMEM, VMEM],
        out_specs=VMEM,
        out_shape=jax.ShapeDtypeStruct((groups, 3, half, ROW_TOKENS), jnp.bfloat16),
        compiler_params=pltpu.CompilerParams(vmem_limit_bytes=SMALL_LIMIT),
        cost_estimate=pl.CostEstimate(
            flops=2 * groups * half * ROW_TOKENS, bytes_accessed=8 * groups * half * ROW_TOKENS,
            transcendentals=0,
        ),
        name="rank_sums_to_send",
    )(index, share)


def gradient_kernel(
    core_at, source_at, dest_at, index, crossed, crossed_other, token, attention, gradient, out,
    done, parts, low, projected, sums, tokens, more, sem,
):
    half = crossed.shape[2]
    rank = 2 * half
    core = index[core_at]
    part_copies = [
        pltpu.make_async_copy(part.at[:, pl.ds(0, 2)], parts.at[i], sem.at[3 + i])
        for i, part in enumerate((crossed, crossed_other))
    ]
    copies = [
        pltpu.make_async_copy(attention, tokens, sem.at[0]),
        pltpu.make_async_copy(gradient, more, sem.at[1]),
    ]
    for copy in part_copies + copies:
        copy.start()
    for copy in part_copies:
        copy.wait()
    halves = [
        (pl.ds(pl.multiple_of(owner * half, half), half), parts.at[i])
        for i, owner in enumerate((core, 1 - core))
    ]
    for s in range(tokens.shape[0] // ROW_TOKENS):
        source = index[source_at + s]
        keep = (source >= 0).astype(jnp.float32)
        for ranks, part in halves:
            value = part[jnp.maximum(source, 0), 0].astype(jnp.float32) * keep
            low[ranks, s * ROW_TOKENS : (s + 1) * ROW_TOKENS] = value.astype(jnp.bfloat16)
    for r in range(more.shape[0] // ROW_TOKENS):
        for ranks, part in halves:
            projected[ranks, r * ROW_TOKENS : (r + 1) * ROW_TOKENS] = part[index[dest_at + r], 1]
    copies[0].wait()
    sums[:rank] = jnp.dot(low[...], tokens[...], preferred_element_type=jnp.float32)
    copies[1].wait()
    sums[rank:] = jnp.dot(projected[...], more[...], preferred_element_type=jnp.float32)
    done[...] = jnp.zeros_like(done)
    store = pltpu.make_async_copy(sums, out, sem.at[2])
    store.start()
    store.wait()


def gradient_products(
    index, core_at, source_at, dest_at, crossed, other, token, attention, gradient
):
    rank = 2 * crossed.shape[2]
    slot_tokens, width = attention.shape
    row_tokens = gradient.shape[0]
    return pl.pallas_call(
        functools.partial(gradient_kernel, core_at, source_at, dest_at),
        in_specs=[SMEM] + [ANY] * 5,
        out_specs=[HBM, VMEM],
        out_shape=[
            jax.ShapeDtypeStruct((2 * rank, width), jnp.float32),
            jax.ShapeDtypeStruct((8, LANES), jnp.float32),
        ],
        scratch_shapes=[
            pltpu.VMEM((2, crossed.shape[0], 2) + crossed.shape[2:], jnp.bfloat16),
            pltpu.VMEM((rank, slot_tokens), jnp.bfloat16),
            pltpu.VMEM((rank, row_tokens), jnp.bfloat16),
            pltpu.VMEM((2 * rank, width), jnp.float32),
            pltpu.VMEM(attention.shape, jnp.bfloat16),
            pltpu.VMEM(gradient.shape, jnp.bfloat16),
            pltpu.SemaphoreType.DMA((5,)),
        ],
        compiler_params=pltpu.CompilerParams(vmem_limit_bytes=SMALL_LIMIT),
        cost_estimate=pl.CostEstimate(
            flops=2 * rank * width * (slot_tokens + row_tokens),
            bytes_accessed=2 * width * (slot_tokens + row_tokens),
            transcendentals=0,
        ),
        name="gradient_products",
    )(index, crossed, other, token, attention, gradient)


def unfold_kernel(arrived, gradients, out, down_gradient, up_gradient):
    groups, slots, folded, half_width = arrived.shape
    piece = folded // 2
    for slot in range(slots):
        for pair in range(groups // 2):
            halves = []
            for j in (2 * pair, 2 * pair + 1):
                value = arrived[j, slot].astype(jnp.float32)
                pieces = []
                for n in range(half_width // LANES):
                    lanes = slice(n * LANES, (n + 1) * LANES)
                    pieces += [value[:piece, lanes], value[piece:, lanes]]
                halves.append(jnp.concatenate(pieces, axis=1))
            rows = pl.ds(slot * groups * piece + pair * folded, folded)
            out[rows, :] = jnp.concatenate(halves, axis=0).astype(out.dtype)

    @pl.when(pl.program_id(0) == 0)
    def _():
        values = []
        for j in range(groups):
            value = gradients[j, 0].astype(jnp.float32)
            values.append(jnp.concatenate([value[:piece], value[piece:]], axis=1))
        down_gradient[...] = jnp.concatenate(values[: groups // 2], axis=0)
        up_gradient[...] = jnp.concatenate(values[groups // 2 :], axis=0)


def unfold(arrived, slots):
    groups, _, folded, half_width = arrived.shape
    piece, width = folded // 2, 2 * half_width
    rank = groups * piece // 2
    step = slots // 2
    return pl.pallas_call(
        unfold_kernel,
        grid=(slots // step,),
        in_specs=[
            pl.BlockSpec((groups, step, folded, half_width), lambda s: (0, s, 0, 0)),
            pl.BlockSpec((groups, 1, folded, half_width), lambda s: (0, slots, 0, 0)),
        ],
        out_specs=[
            pl.BlockSpec((step * groups * piece, width), lambda s: (s, 0)),
            pl.BlockSpec((rank, width), lambda s: (0, 0)),
            pl.BlockSpec((rank, width), lambda s: (0, 0)),
        ],
        out_shape=[
            jax.ShapeDtypeStruct((slots * groups * piece, width), jnp.bfloat16),
            jax.ShapeDtypeStruct((rank, width), jnp.float32),
            jax.ShapeDtypeStruct((rank, width), jnp.float32),
        ],
        compiler_params=pltpu.CompilerParams(vmem_limit_bytes=SMALL_LIMIT),
        name="unfold",
    )(arrived, arrived)


def body(
    attention_slot_outputs,
    output_gradient_rows,
    output_weight,
    down_weight,
    up_weight,
    assign,
    counts,
):
    groups = counts.shape[0]
    rows = assign.shape[0]
    rows_here = output_gradient_rows.shape[0] // ROW_TOKENS
    slot_cap = attention_slot_outputs.shape[0] // ROW_TOKENS
    width_here = output_gradient_rows.shape[1]
    rank = up_weight.shape[0]
    tp = lax.axis_size("tp")
    piece = ROW_TOKENS // groups
    own_group = lax.axis_index("group")
    group_ids = jnp.arange(groups, dtype=jnp.int32)
    onehot = (assign[:, None] == group_ids[None, :]).astype(jnp.int32)
    before = jnp.cumsum(onehot, axis=0) - onehot
    order_in = jnp.sum(before * onehot, axis=1)
    free_slots = jnp.sum(onehot * counts[None, :], axis=1)
    position = slot_cap - free_slots + order_in
    own_dest = lax.dynamic_slice_in_dim(assign, own_group * rows_here, rows_here)
    scale_factor = adapter_scale / math.sqrt(rows * ROW_TOKENS)

    index = lax.axis_index("tp")
    chips = tp // 2
    y, core = index // 2, index % 2

    def move(value, n):
        pairs = [(2 * a + b, 2 * ((a + n) % chips) + b) for a in range(chips) for b in range(2)]
        return lax.ppermute(value, "tp", pairs)

    def swap(value):
        return lax.ppermute(value, "tp", [(i, i ^ 1) for i in range(tp)])

    pieces_out, parts = prepare(
        groups, output_gradient_rows, attention_slot_outputs, up_weight, down_weight.T
    )
    spread = lax.all_to_all(
        pieces_out.reshape(groups, rows_here, piece, width_here),
        "group",
        split_axis=0,
        concat_axis=0,
        tiled=True,
    ).reshape(rows * piece, width_here)

    slot_ids = jnp.arange(slot_cap, dtype=jnp.int32)
    row_ids = jnp.arange(rows_here, dtype=jnp.int32)
    row_position = position.reshape(groups, rows_here)
    hit_row = assign.reshape(groups, rows_here) == own_group
    low_pick = jnp.max(jnp.where(own_dest[None, :] == group_ids[:, None], row_ids, -1), axis=1)
    projected_pick = jnp.max(jnp.where(hit_row, rows_here + row_position, -1), axis=1)
    slot_match = hit_row[:, :, None] & (row_position[:, :, None] == slot_ids)
    slot_source = jnp.max(jnp.where(slot_match, group_ids[:, None, None], -1), axis=(0, 1))
    owners = []
    for step in (0, chips - 1, 1, 2):
        pair = 2 * lax.rem(y + step, chips)
        owners += [pair + core, pair + 1 - core]
    pieces = [
        assign, position, jnp.stack([low_pick, projected_pick], axis=1).reshape(-1), slot_source,
        own_dest, jnp.stack(owners + [core]).astype(jnp.int32),
    ]
    at = [0]
    for part in pieces:
        at.append(at[-1] + part.shape[0])
    _, _, pick_at, source_at, dest_at, owner_at, end = at
    table = jnp.concatenate(pieces)

    parts = parts + swap(parts)
    share = lax.dynamic_slice_in_dim(parts, core * (rank // 2), rank // 2, axis=0)
    share = share + move(share, 1) + move(share, -1) + move(share, 2)

    send = rank_sums_to_send(table, pick_at, groups, rows_here, share)
    crossed = lax.all_to_all(send, "group", split_axis=0, concat_axis=0, tiled=True)

    left, right = move(spread, 1), move(spread, -1)
    other = swap(spread)
    sums, done = block_products(
        table, [owner_at, owner_at + 1], [spread, other], output_weight, send,
        name="own_products",
    )
    (crossed,) = after([crossed], done)
    crossed_other = swap(crossed)
    partial_grads, done = gradient_products(
        table, end - 1, source_at, dest_at, crossed, crossed_other, done, attention_slot_outputs,
        output_gradient_rows,
    )
    left_top, right_bottom, left, right, partial_grads = take_halves(
        left, right, partial_grads, done
    )
    far = [move(left_top, 1), move(right_bottom, -1)]
    share_rows = 2 * rank // groups
    grads = lax.all_to_all(
        partial_grads.reshape(groups, share_rows, width_here), "group", split_axis=0, concat_axis=0,
        tiled=True,
    )
    sums, done = block_products(
        table, [owner_at + i for i in range(2, 6)], [left, swap(left), right, swap(right)],
        output_weight, done, sums, name="side_products",
    )
    far = after(far, done)
    placed = last_products(
        rows, scale_factor, table, [owner_at + 6, owner_at + 7], end - 1, far,
        [swap(part) for part in far], grads, (crossed, crossed_other), output_weight, sums,
        down_weight.T, slot_cap,
    )

    arrived = lax.all_to_all(placed, "group", split_axis=0, concat_axis=0, tiled=True)
    attention_gradient, down_gradient, up_gradient = unfold(arrived, slot_cap)
    return attention_gradient, down_gradient.T, up_gradient


def solution(mesh):
    in_specs = (
        P("group", "tp"),
        P("group", "tp"),
        P("tp", None),
        P("tp", None),
        P(None, "tp"),
        P(),
        P(),
    )
    out_specs = (P("group", "tp"), P("tp", None), P(None, "tp"))
    return jax.shard_map(body, mesh=mesh, in_specs=in_specs, out_specs=out_specs, check_vma=False)
```
